128 devices in a mesh: layout: 4 (over z), gx: 4 (over y_hi, core), gy: 8 (over y_lo, x).
Axes of the slice: x: 4, y: 4 (y_hi: 2, y_lo: 2; y = y_hi * 2 + y_lo), z: 4, core: 2. Of those that a mesh axis runs over, the one named last changes fastest.
Arguments:
- state: float32 [4, 4, 64, 32, 1024], P('layout', None, 'gx', None, 'gy'), may hold values from -2 to 2
- planes: float32 [8, 4, 32, 1024], P('layout', None, None, 'gy'), may hold values from -2 to 2
- turbine_cell: int32 [4, 64, 32, 1024], P('layout', 'gx', None, 'gy'), may hold values from -1 to 63, as said below
- active: int32 [4, 64], P('layout'), may hold values 0 or 1
- yaw_sector: int32 [4, 64], P('layout'), may hold values from 0 to 7
- slot: int32 [4], replicated, may hold values from 0 to 7
Outputs:
- fields: float32 [4, 4, 64, 32, 1024], P('layout', None, 'gx', None, 'gy')
The draws below stay inside these ranges and needn't reach their ends.
Inputs may be any that keep to these rules, and one draw needn't show every extreme that they name: `turbine_cell`: cells of value t form turbine t's actuator disk: one streamwise cell, 11 levels around level 16 and 11 spanwise cells (periodic). Every turbine has its disk and disks don't intersect; -1 elsewhere.
All inputs are finite; a program needn't handle non-finite values. No bound on the sum of `active` on one device may be relied on, other than what follows from the above.
Results may differ from the reference program's by a relative error of at most 0.00015.
Values sent between devices are 32-bit elements; how exact they have to be, the bound alone decides.
No kernel may reach another device: no remote copies, remote signals or barrier semaphores. Data moves between devices by JAX's collectives and lax.ppermute only.
A program may use at most 64 MiB of HBM per device.

```python
import math
import jax
import jax.numpy as jnp
from jax import lax

NZ = 32
STEPS = 4
SWEEPS = 4
RADIUS = 5
TSPACE = 32
NLAY = 4
NX = 64
NY = 1024
TURB = 64
PLANES = 8


def ripple(index, phase):
    return jnp.sin((index + phase).astype(jnp.float32) * (0.5 * math.pi))


def jitter_field(key, extent):
    return jnp.clip(0.3 * jax.random.normal(key, extent, jnp.float32), -0.55, 0.55)


def draw_state(key, part):
    jitter = jitter_field(jax.random.fold_in(key, 101), (NLAY, 4, NX, NZ, NY))
    phases = jax.random.randint(jax.random.fold_in(key, 103), (3, NLAY), 0, 4)
    stream = jnp.arange(NX, dtype=jnp.int32)[None, :, None, None]
    levels = jnp.arange(NZ, dtype=jnp.int32)[None, None, :, None]
    spanwise = jnp.arange(NY, dtype=jnp.int32)[None, None, None, :]
    phase_x = phases[0][:, None, None, None]
    phase_z = phases[1][:, None, None, None]
    phase_y = phases[2][:, None, None, None]
    stream_wind = jitter[:, 0] + 1.4 * ripple(stream, phase_x)
    span_wind = jitter[:, 1] + 1.4 * ripple(spanwise, phase_y)
    vertical_wind = jitter[:, 2] + 0.5 * ripple(levels, phase_z)
    warmth = jitter[:, 3] + 0.6 * ripple(stream + 1, phase_x)
    fields = jnp.stack([stream_wind, span_wind, vertical_wind, warmth], axis=1)
    return jnp.clip(fields, -1.98, 1.98)


def draw_planes(key, part):
    jitter = jitter_field(jax.random.fold_in(key, 201), (PLANES, 4, NZ, NY))
    phases = jax.random.randint(jax.random.fold_in(key, 203), (2, PLANES), 0, 4)
    spanwise = jnp.arange(NY, dtype=jnp.int32)[None, None, :]
    phase_u = phases[0][:, None, None]
    phase_v = phases[1][:, None, None]
    stream_wind = jitter[:, 0] + 0.8 * ripple(spanwise, phase_u)
    span_wind = jitter[:, 1] + 1.4 * ripple(spanwise, phase_v)
    vertical_wind = jitter[:, 2]
    warmth = jitter[:, 3]
    fields = jnp.stack([stream_wind, span_wind, vertical_wind, warmth], axis=1)
    return jnp.clip(fields, -1.98, 1.98)


def draw_turbine_cell(key, part):
    blocks_x = NX // TSPACE
    blocks_y = NY // TSPACE
    key_x = jax.random.fold_in(key, 11)
    key_y = jax.random.fold_in(key, 23)
    offset_x = jax.random.randint(key_x, (NLAY, blocks_x * blocks_y), 0, TSPACE)
    offset_y = jax.random.randint(key_y, (NLAY, blocks_x * blocks_y), RADIUS - TSPACE // 2, TSPACE // 2 - RADIUS)
    stream = jnp.arange(NX)
    span = jnp.arange(NY)
    levels = jnp.arange(NZ)
    block_x = stream // TSPACE
    block_y = (span + TSPACE // 2) // TSPACE % blocks_y
    inside_y = (span + TSPACE // 2) % TSPACE - TSPACE // 2
    turbine = block_x[:, None] * blocks_y + block_y[None, :]
    chosen_x = jnp.take(offset_x, turbine, axis=1)
    chosen_y = jnp.take(offset_y, turbine, axis=1)
    hit = (stream[None, :, None] % TSPACE == chosen_x) & (jnp.abs(inside_y[None, None, :] - chosen_y) <= RADIUS)
    level_hit = jnp.abs(levels - NZ // 2) <= RADIUS
    both = hit[:, :, None, :] & level_hit[None, None, :, None]
    return jnp.where(both, turbine[None, :, None, :], -1).astype(jnp.int32)


def place_ends(values, stream_key, low, largest):
    shape = values.shape
    place = [jax.random.randint(jax.random.fold_in(stream_key, axis), (), 0, shape[axis]) for axis in range(len(shape))]
    values = values.at[tuple(place)].set(low)
    longest = shape.index(max(shape))
    place[longest] = (place[longest] + 1) % shape[longest]
    return values.at[tuple(place)].set(largest)


def setup_inputs(seed: int = 0) -> dict:
    arg_keys = jax.random.split(jax.random.key(seed), 7)
    state = draw_state(jax.random.fold_in(arg_keys[6], 71), 0)
    planes = draw_planes(jax.random.fold_in(arg_keys[6], 71), 0)
    turbine_cell = draw_turbine_cell(jax.random.fold_in(arg_keys[6], 71), 0)
    active = place_ends((jax.random.randint(arg_keys[3], (NLAY, TURB), 0, 4) < 3).astype(jnp.int32), jax.random.fold_in(arg_keys[3], 1), 0, 1)
    yaw_sector = place_ends(jax.random.randint(arg_keys[4], (NLAY, TURB), 0, 8), jax.random.fold_in(arg_keys[4], 1), 0, 7).astype(jnp.int32)
    slot = place_ends(jax.random.randint(arg_keys[5], (STEPS,), 0, PLANES), jax.random.fold_in(arg_keys[5], 1), 0, PLANES - 1).astype(jnp.int32)
    return dict(state=state, planes=planes, turbine_cell=turbine_cell, active=active, yaw_sector=yaw_sector, slot=slot)


TIME_STEP = 0.25
VISCOSITY = 0.02
SMAGORINSKY = 0.0289
DIFFUSIVITY_RATIO = 1.0 / 0.7
BUOYANCY = 0.5
THRUST_COEFF = 1.33
YAW_INCREMENT = 0.1

def profiles(levels):
    height = (jnp.arange(levels).astype(jnp.float32) + 0.5) / levels
    wind_speed = height ** (1.0 / 7.0)
    warmth = 0.5 * height
    zeros = jnp.zeros((levels,), jnp.float32)
    return jnp.stack([wind_speed, zeros, zeros, warmth])

def pad_levels(values):
    keeping = jnp.array([1.0, 1.0, 0.0, 1.0], jnp.float32).reshape(4, 1, 1, 1)
    return jnp.concatenate([values[:, :, :1] * keeping, values, values[:, :, -1:] * keeping], axis=2)

def stencil(padded):
    centre = padded[:, 1:-1, 1:-1, 1:-1]
    along_x = (padded[:, 2:, 1:-1, 1:-1] - padded[:, :-2, 1:-1, 1:-1]) * 0.5
    along_z = (padded[:, 1:-1, 2:, 1:-1] - padded[:, 1:-1, :-2, 1:-1]) * 0.5
    along_y = (padded[:, 1:-1, 1:-1, 2:] - padded[:, 1:-1, 1:-1, :-2]) * 0.5
    laplacian = padded[:, 2:, 1:-1, 1:-1] + padded[:, :-2, 1:-1, 1:-1] + padded[:, 1:-1, 2:, 1:-1] + padded[:, 1:-1, :-2, 1:-1] + padded[:, 1:-1, 1:-1, 2:] + padded[:, 1:-1, 1:-1, :-2] - 6.0 * centre
    return (centre, along_x, along_y, along_z, laplacian)

def tendency(padded, mean_theta, force_u, force_v):
    centre, along_x, along_y, along_z, laplacian = stencil(padded)
    advect = centre[0] * along_x + centre[1] * along_y + centre[2] * along_z
    shear_xy = 0.5 * (along_y[0] + along_x[1])
    shear_xz = 0.5 * (along_z[0] + along_x[2])
    shear_yz = 0.5 * (along_z[1] + along_y[2])
    strain = jnp.sqrt(2.0 * (along_x[0] ** 2 + along_y[1] ** 2 + along_z[2] ** 2) + 4.0 * (shear_xy ** 2 + shear_xz ** 2 + shear_yz ** 2))
    viscous = VISCOSITY + SMAGORINSKY * strain
    scaling = jnp.array([1.0, 1.0, 1.0, DIFFUSIVITY_RATIO], jnp.float32).reshape(4, 1, 1, 1)
    extra = jnp.stack([force_u, force_v, BUOYANCY * (centre[3] - mean_theta[None, :, None]), jnp.zeros_like(force_u)])
    return (centre, laplacian * viscous * scaling - advect + extra)

def disk_terms(values, disk_ids, yaw_angle):
    turbines = yaw_angle.shape[0]
    slot_ids = disk_ids + 1
    cos_cell = jnp.take(jnp.concatenate([jnp.zeros((1,), jnp.float32), jnp.cos(yaw_angle)]), slot_ids)
    sin_cell = jnp.take(jnp.concatenate([jnp.zeros((1,), jnp.float32), jnp.sin(yaw_angle)]), slot_ids)
    normal = values[0] * cos_cell + values[1] * sin_cell
    disk_sums = jax.ops.segment_sum(normal.reshape(-1), slot_ids.reshape(-1), num_segments=turbines + 1)[1:]
    return (cos_cell, sin_cell, disk_sums)

def disk_force(disk_sums, running, disk_ids, cos_cell, sin_cell):
    disk_speed = disk_sums / float((2 * RADIUS + 1) ** 2)
    thrust = -0.5 * THRUST_COEFF * disk_speed * jnp.abs(disk_speed) * running
    per_cell = jnp.take(jnp.concatenate([jnp.zeros((1,), jnp.float32), thrust]), disk_ids + 1)
    return (per_cell * cos_cell, per_cell * sin_cell)

def divergence(extended):
    vertical = extended[2][1:-1, :, 1:-1]
    zeros = jnp.zeros_like(vertical[:, :1])
    padded_w = jnp.concatenate([zeros, vertical, zeros], axis=1)
    return (extended[0][2:, :, 1:-1] - extended[0][:-2, :, 1:-1]) * 0.5 + (extended[1][1:-1, :, 2:] - extended[1][1:-1, :, :-2]) * 0.5 + (padded_w[:, 2:] - padded_w[:, :-2]) * 0.5

def vertical_pair(padded):
    centre = padded[1:-1, :, 1:-1]
    upward = jnp.concatenate([centre[:, 1:], centre[:, -1:]], axis=1)
    downward = jnp.concatenate([centre[:, :1], centre[:, :-1]], axis=1)
    return (upward, downward)

def jacobi(padded, source):
    upward, downward = vertical_pair(padded)
    beside_all = padded[2:, :, 1:-1] + padded[:-2, :, 1:-1] + padded[1:-1, :, 2:] + padded[1:-1, :, :-2] + upward + downward
    return (beside_all - source) / 6.0

def gradient(padded):
    upward, downward = vertical_pair(padded)
    return jnp.stack([(padded[2:, :, 1:-1] - padded[:-2, :, 1:-1]) * 0.5, (padded[1:-1, :, 2:] - padded[1:-1, :, :-2]) * 0.5, (upward - downward) * 0.5])

def wrap_span(values):
    return jnp.concatenate([values[..., -1:], values, values[..., :1]], axis=-1)

def pad_pressure(pressure):
    zeros = jnp.zeros_like(pressure[:1])
    return wrap_span(jnp.concatenate([zeros, pressure, zeros], axis=0))

def advance(fields, inflow, disk_ids, yaw_angle, running):
    theta_sum = lax.optimization_barrier(jnp.sum(fields[3], axis=(0, 2)))
    cos_cell, sin_cell, disk_sums = disk_terms(fields, disk_ids, yaw_angle)
    cell_count = fields.shape[1] * fields.shape[3]
    extended = wrap_span(jnp.concatenate([inflow[:, None], fields, fields[:, -1:]], axis=1))
    force_u, force_v = disk_force(disk_sums, running, disk_ids, cos_cell, sin_cell)
    current, tendencies = tendency(pad_levels(extended), theta_sum / cell_count, force_u, force_v)
    stepped = current + TIME_STEP * tendencies
    provisional = stepped[:3]
    star_ext = wrap_span(jnp.concatenate([inflow[:3, None], provisional, provisional[:, -1:]], axis=1))
    source = divergence(star_ext)
    pressure = -source / 6.0
    for sweep_index in range(SWEEPS):
        pressure = jacobi(pad_pressure(pressure), source)
    gradients = gradient(pad_pressure(pressure))
    return jnp.concatenate([provisional - gradients, stepped[3:]], axis=0)

def reference(state, planes, turbine_cell, active, yaw_sector, slot):
    mean_wind = profiles(state.shape[3])

    def evolve_layout(items):
        start_fields, disk_ids, running, sectors = items
        fields = start_fields + mean_wind[:, None, :, None]
        yaw_angle = (sectors.astype(jnp.float32) - 3.5) * YAW_INCREMENT
        running_f = running.astype(jnp.float32)
        for step_index in range(STEPS):
            inflow = lax.dynamic_index_in_dim(planes, slot[step_index], 0, keepdims=False) + mean_wind[:, :, None]
            fields = advance(fields, inflow, disk_ids, yaw_angle, running_f)
        return fields
    return lax.map(evolve_layout, (state, turbine_cell, active, yaw_sector))
```

```python
import functools
import math

import jax
import jax.numpy as jnp
from jax import lax
from jax.experimental import pallas as pl
from jax.experimental.pallas import tpu as pltpu
from jax.sharding import PartitionSpec as P

STEPS = 4
SWEEPS = 4
RADIUS = 5
NZ = 32
XI = 16
GX = 4
OWN = 32
HALO = 8
EXT = OWN + 2 * HALO
PAD = EXT + 16
LANES = 128
WIDTH = 2 * RADIUS + 1
LOWEST = NZ // 2 - RADIUS
TILES = 4 * XI

TIME_STEP = 0.25
VISCOSITY = 0.02
SMAGORINSKY = 0.0289
DIFFUSIVITY_RATIO = 1.0 / 0.7
BUOYANCY = 0.5
THRUST_COEFF = 1.33
YAW_INCREMENT = 0.1
SIXTH = 1.0 / 6.0
F32 = jnp.float32
VLIMIT = 40 * 1024 * 1024

VMEM = pl.BlockSpec(memory_space=pltpu.VMEM)
SMEM = pl.BlockSpec(memory_space=pltpu.SMEM)


def shape(*dims):
    return jax.ShapeDtypeStruct(dims, F32)


def lanes(rows=8):
    return lax.broadcasted_iota(jnp.int32, (rows, LANES), 1)


def level_masks(rows=8):
    level = lanes(rows) & (NZ - 1)
    return level == 0, level == NZ - 1


def below(f, first):
    return jnp.where(first, f, pltpu.roll(f, 1, axis=1))


def above(f, last):
    return jnp.where(last, f, pltpu.roll(f, LANES - 1, axis=1))


def call(kernel, out_shape, in_specs, scratch=(), flops=10_000_000, **kwargs):
    return pl.pallas_call(
        kernel,
        out_shape=out_shape,
        in_specs=in_specs,
        out_specs=jax.tree.map(lambda _: VMEM, out_shape),
        scratch_shapes=list(scratch),
        compiler_params=pltpu.CompilerParams(vmem_limit_bytes=VLIMIT),
        cost_estimate=pl.CostEstimate(flops=flops, bytes_accessed=4_000_000, transcendentals=0),
        **kwargs,
    )


def block_transposed(sources, group, masks):
    out = None
    for c, value in enumerate(sources):
        moved = pltpu.roll(value, ((c - group) & 3) * 32, axis=1)
        out = moved if out is None else jnp.where(masks[c], moved, out)
    return out


def pack_kernel(scal, state, planes, s0, s1, s2, s3, pl_out):
    slab = scal[1]
    group = lanes() >> 5
    masks = [group == c for c in range(4)]

    def per_row(x, carry):
        for kt in range(4):
            sources = [state[c, x, kt * 8 : kt * 8 + 8, :] for c in range(4)]
            for s, out in enumerate((s0, s1, s2, s3)):
                out[x * 4 + kt] = block_transposed(sources, slab ^ s, masks)
        return carry

    lax.fori_loop(0, XI, per_row, 0)
    for plane in range(planes.shape[0]):
        for kt in range(4):
            sources = [planes[plane, c, kt * 8 : kt * 8 + 8, :] for c in range(4)]
            pl_out[plane * 4 + kt] = block_transposed(sources, slab, masks)


def maps_kernel(scal, active, yaw, ids, maps, counts, stage):
    own, slab = scal[0], scal[1]
    lane = lanes(XI)
    for g in range(GX):
        source = own ^ g
        left, mid, right = ids[source, 1], ids[source, 0], ids[source, 2]
        shift = (HALO - 32 * slab) & (LANES - 1)
        moved_mid = pltpu.roll(mid, shift, axis=1)
        moved_left = pltpu.roll(left, HALO, axis=1)
        moved_right = pltpu.roll(right, OWN + HALO, axis=1)
        here = jnp.where((lane < HALO) & (slab == 0), moved_left, moved_mid)
        here = jnp.where((lane >= OWN + HALO) & (slab == 3), moved_right, here)
        stage[0, g * XI : (g + 1) * XI, :] = here
    here = stage[0]

    def per_turbine(t, carry):
        sector, running = carry
        match = here == t.astype(F32)
        return (
            jnp.where(match, yaw[t].astype(F32), sector),
            jnp.where(match, active[t].astype(F32), running),
        )

    none = jnp.full((GX * XI, LANES), -1.0, F32)
    sector, running = lax.fori_loop(
        0, active.shape[0], per_turbine, (none, jnp.zeros((GX * XI, LANES), F32))
    )
    cosine = jnp.zeros((GX * XI, LANES), F32)
    sine = jnp.zeros((GX * XI, LANES), F32)
    for value in range(8):
        angle = (value - 3.5) * YAW_INCREMENT
        cosine = jnp.where(sector == value, F32(math.cos(angle)), cosine)
        sine = jnp.where(sector == value, F32(math.sin(angle)), sine)
    thrust = running * F32(-0.5 * THRUST_COEFF * TIME_STEP / float(WIDTH**2) ** 2)
    low = lanes(GX * XI) < 64
    stage[0] = jnp.where(low, here, pltpu.roll(thrust, 64, axis=1))
    stage[1] = jnp.where(low, cosine, pltpu.roll(sine, 64, axis=1))
    level = lanes(EXT) & (NZ - 1)
    band = (level >= LOWEST) & (level < LOWEST + WIDTH)
    row = lax.broadcasted_iota(jnp.int32, (EXT, LANES), 0)
    outside = jnp.full((8, LANES), -2.0, F32)
    for xi in range(XI):
        pair = []
        for which in range(2):
            rows = [
                jnp.broadcast_to(stage[which, g * XI + xi : g * XI + xi + 1, :], (NZ, LANES))
                for g in range(GX)
            ]
            pair.append(jnp.concatenate(rows, axis=0).T)
        ident = pair[0][:EXT]
        cos_u = jnp.where(band, pair[1][:EXT], 0.0)
        sin_v = jnp.where(band, pair[1][64 : 64 + EXT], 0.0)
        maps[0, xi, 0:8, :] = outside
        maps[0, xi, 8 : 8 + EXT, :] = ident
        maps[0, xi, 8 + EXT : PAD, :] = outside
        maps[1, xi, 8 : 8 + EXT, :] = cos_u
        maps[2, xi, 8 : 8 + EXT, :] = sin_v
        maps[3, xi, 8 : 8 + EXT, :] = pair[0][64 : 64 + EXT]
        for which in (1, 2, 3):
            maps[which, xi, 0:8, :] = jnp.zeros((8, LANES), F32)
            maps[which, xi, 8 + EXT : PAD, :] = jnp.zeros((8, LANES), F32)
        first, final = ident[:1], ident[EXT - 1 :]
        beyond = (ident == first) & (row > 0)
        before = (ident == final) & (row < EXT - 1)
        left_count = WIDTH - jnp.sum(jnp.where(beyond, 1.0, 0.0), axis=0, keepdims=True)
        right_count = WIDTH - jnp.sum(jnp.where(before, 1.0, 0.0), axis=0, keepdims=True)
        counts[0, xi : xi + 1, :] = jnp.where(first >= 0.0, left_count * cos_u[:1], 0.0)
        counts[1, xi : xi + 1, :] = jnp.where(final >= 0.0, right_count * cos_u[EXT - 1 :], 0.0)


def disk_edges(fields, maps, su, sd):
    row24 = lax.broadcasted_iota(jnp.int32, (24, LANES), 0)
    for xi in range(XI):
        base = 8 + HALO
        ident = maps[0, xi, base + 8 : base + 32, :]
        normal = (
            maps[1, xi, base + 8 : base + 32, :] * fields[0, xi, 8:32, :]
            + maps[2, xi, base + 8 : base + 32, :] * fields[1, xi, 8:32, :]
        )
        take = (ident == ident[16:17]) & (row24 <= 16)
        su[TILES + xi // 8, xi % 8 : xi % 8 + 1, :] = jnp.sum(
            jnp.where(take, normal, 0.0), axis=0, keepdims=True
        )
        ident = maps[0, xi, base : base + 24, :]
        normal = (
            maps[1, xi, base : base + 24, :] * fields[0, xi, 0:24, :]
            + maps[2, xi, base : base + 24, :] * fields[1, xi, 0:24, :]
        )
        take = (ident == ident[7:8]) & (row24 >= 7)
        sd[TILES + xi // 8, xi % 8 : xi % 8 + 1, :] = jnp.sum(
            jnp.where(take, normal, 0.0), axis=0, keepdims=True
        )


def over_groups(row):
    row = row + pltpu.roll(row, 64, axis=1)
    return row + pltpu.roll(row, 32, axis=1)


def unpack_kernel(
    scal, slot, profile, maps, s0, r1, r2, r3, p0, *rest, layouts, per_layout
):
    plane_refs = (p0,) + rest[: layouts - 1]
    fields, inflow, su, sd, sums, held, planes = rest[layouts - 1 :]
    own, here = scal[0], scal[2]
    for s, source in enumerate((s0, r1, r2, r3)):
        held[own ^ s] = source[...]
    for s, source in enumerate(plane_refs):
        planes[here ^ s] = source[...]

    def per_row(xi, total):
        rows = [held[g, pl.ds(xi * 4, 4)].reshape(NZ, LANES) for g in range(GX)]
        turned = jnp.concatenate(rows, axis=0).T
        for c in range(4):
            value = turned[c * 32 : c * 32 + 32] + profile[c : c + 1, :]
            fields[c, xi] = value
            sd[c * XI + xi] = value[:HALO]
            su[c * XI + xi] = value[OWN - HALO :]
            if c == 3:
                total = total + jnp.sum(value, axis=0, keepdims=True)
        return total

    total = lax.fori_loop(0, XI, per_row, jnp.zeros((1, LANES), F32))
    sums[...] = jnp.broadcast_to(over_groups(total), (8, LANES))
    rows = []
    for step in range(STEPS):
        plane = slot[step]
        rows.append(
            planes[plane // per_layout, pl.ds((plane % per_layout) * 4, 4)].reshape(NZ, LANES)
        )
    turned = jnp.concatenate(rows, axis=0).T
    for c in range(4):
        value = turned[c * 32 : c * 32 + 32] + profile[c : c + 1, :]
        inflow[c] = value
        sd[TILES + 2 + c] = value[:HALO]
        su[TILES + 2 + c] = value[OWN - HALO :]
    disk_edges(fields, maps, su, sd)


def mean_response(mean):
    lane = lanes(XI)
    row = lax.broadcasted_iota(jnp.int32, (XI, LANES), 0)
    level = lane & (NZ - 1)
    first, last = level == 0, level == NZ - 1

    def x_pair(p):
        lower = pltpu.roll(p, 1, axis=0)
        edge = jnp.where(lane < 32, 0.0, pltpu.roll(lower, 32, axis=1))
        lower = jnp.where(row == 0, edge, lower)
        upper = pltpu.roll(p, XI - 1, axis=0)
        edge = jnp.where(lane >= 96, 0.0, pltpu.roll(upper, 96, axis=1))
        upper = jnp.where(row == XI - 1, edge, upper)
        return lower, upper

    vertical = jnp.broadcast_to(mean, (XI, LANES)) * F32(-TIME_STEP * BUOYANCY)
    up = jnp.where(last, 0.0, pltpu.roll(vertical, LANES - 1, axis=1))
    down = jnp.where(first, 0.0, pltpu.roll(vertical, 1, axis=1))
    source = (up - down) * 0.5
    p = source * F32(-SIXTH)
    for sweep in range(SWEEPS):
        lower, upper = x_pair(p)
        p = (lower + upper + 2.0 * p + above(p, last) + below(p, first) - source) * F32(SIXTH)
    lower, upper = x_pair(p)
    return (upper - lower) * -0.5, vertical - (above(p, last) - below(p, first)) * 0.5


def step_kernel(*refs, step, cells):
    refs = list(refs)
    fields_in, lo, hi, maps, counts, inflow_in = refs[:6]
    del refs[:6]
    mean = None
    if step > 0:
        mean = refs.pop(0)
    out = refs.pop(0)
    su = sd = sums = inflow_out = None
    if step < STEPS - 1:
        su, sd, sums = refs[:3]
        del refs[:3]
    if step == 0:
        inflow_out = refs.pop(0)
    f, v, r, pa, pb, ns, change, inflow = refs
    first, last = level_masks()
    lane_ext = lanes(EXT)
    body = slice(8, 8 + EXT)

    if step > 0:
        du, dw = mean_response(mean[0:1, :] * F32(1.0 / cells))
        change[0] = du
        change[1] = dw
        inflow[...] = inflow_in[...]
    else:
        for c in range(4):
            inflow[c, 0:8] = lo[TILES + 2 + c]
            inflow[c, 8 : 8 + OWN] = inflow_in[c]
            inflow[c, 8 + OWN : EXT] = hi[TILES + 2 + c]
        inflow_out[...] = inflow[...]

    def fill(xi, carry):
        for c in range(4):
            low, mid, high = lo[c * XI + xi], fields_in[c, xi], hi[c * XI + xi]
            if step > 0 and c in (0, 2):
                d = change[c // 2, pl.ds(xi, 1), :]
                low, mid, high = low + d, mid + d, high + d
            f[c, xi + 1, 8:16] = low
            f[c, xi + 1, 16 : 16 + OWN] = mid
            f[c, xi + 1, 16 + OWN : 8 + EXT] = high
        return carry

    lax.fori_loop(0, XI, fill, 0)
    shift = (LANES - 32 * step) % LANES

    def entry(c):
        value = inflow[c]
        return pltpu.roll(value, shift, axis=1) if shift else value

    for c in range(4):
        f[c, 0, body] = jnp.where(
            lane_ext < 32, entry(c), pltpu.roll(f[c, XI, body], 32, axis=1)
        )
        f[c, XI + 1, body] = jnp.where(
            lane_ext >= 96, f[c, XI, body], pltpu.roll(f[c, 1, body], 96, axis=1)
        )

    def normal_speed(xi, carry):
        ns[xi] = maps[1, xi] * f[0, xi + 1] + maps[2, xi] * f[1, xi + 1]
        return carry

    for c in range(2):
        for xi in range(XI):
            f[c, xi + 1, 0:8] = jnp.zeros((8, LANES), F32)
            f[c, xi + 1, 8 + EXT : PAD] = jnp.zeros((8, LANES), F32)
    lax.fori_loop(0, XI, normal_speed, 0)
    for xi in range(XI):
        left = lo[TILES + xi // 8, xi % 8 : xi % 8 + 1, :]
        right = hi[TILES + xi // 8, xi % 8 : xi % 8 + 1, :]
        if step > 0:
            left = left + counts[0, xi : xi + 1, :] * change[0, xi : xi + 1, :]
            right = right + counts[1, xi : xi + 1, :] * change[0, xi : xi + 1, :]
        ns[xi, 8:9, :] = left
        ns[xi, 7 + EXT : 8 + EXT, :] = right
    row_group = lax.broadcasted_iota(jnp.int32, (LANES, LANES), 0)
    col_group = lax.broadcasted_iota(jnp.int32, (LANES, LANES), 1)
    gather = jnp.where((row_group >> 5) == (col_group >> 5), 1.0, 0.0).astype(F32)

    def thrusts(xi, carry):
        speed = jnp.dot(ns[xi], gather, precision=lax.Precision.HIGHEST, preferred_element_type=F32)
        ident = maps[0, xi]
        forward = speed
        backward = speed
        for d in (1, 2, 4, 8):
            same = ident == pltpu.roll(ident, d, axis=0)
            forward = forward + jnp.where(same, pltpu.roll(forward, d, axis=0), 0.0)
            same = ident == pltpu.roll(ident, PAD - d, axis=0)
            backward = backward + jnp.where(same, pltpu.roll(backward, PAD - d, axis=0), 0.0)
        total = forward + backward - speed
        ns[xi] = maps[3, xi] * total * jnp.abs(total)
        return carry

    lax.fori_loop(0, XI, thrusts, 0)

    def tendencies(xi, total):
        for tile in range(EXT // 8):
            base = 8 + tile * 8
            centre, gx, gy, gz, lap = [], [], [], [], []
            for c in range(4):
                mid = f[c, xi + 1, base : base + 8, :]
                xm = f[c, xi, base : base + 8, :]
                xp = f[c, xi + 2, base : base + 8, :]
                ym = f[c, xi + 1, base - 1 : base + 7, :]
                yp = f[c, xi + 1, base + 1 : base + 9, :]
                if c == 2:
                    zm = jnp.where(first, 0.0, pltpu.roll(mid, 1, axis=1))
                    zp = jnp.where(last, 0.0, pltpu.roll(mid, LANES - 1, axis=1))
                else:
                    zm, zp = below(mid, first), above(mid, last)
                centre.append(mid)
                gx.append(xp - xm)
                gy.append(yp - ym)
                gz.append(zp - zm)
                lap.append((xp + xm) + (yp + ym) + (zp + zm) - 6.0 * mid)
            s_xy = gy[0] + gx[1]
            s_xz = gz[0] + gx[2]
            s_yz = gz[1] + gy[2]
            strain = jnp.sqrt(
                2.0 * (gx[0] * gx[0] + gy[1] * gy[1] + gz[2] * gz[2])
                + (s_xy * s_xy + s_xz * s_xz + s_yz * s_yz)
            )
            nu = F32(TIME_STEP * VISCOSITY) + F32(0.5 * TIME_STEP * SMAGORINSKY) * strain
            half = F32(0.5 * TIME_STEP)
            au, av, aw = half * centre[0], half * centre[1], half * centre[2]
            h = ns[xi, base : base + 8, :]
            for c in range(4):
                scale = nu * F32(DIFFUSIVITY_RATIO) if c == 3 else nu
                new = centre[c] + (scale * lap[c] - (au * gx[c] + av * gy[c] + aw * gz[c]))
                if c < 2:
                    new = new + maps[1 + c, xi, base : base + 8, :] * h
                elif c == 2:
                    new = new + F32(TIME_STEP * BUOYANCY) * centre[3]
                if c < 3:
                    v[c, xi + 1, base : base + 8, :] = new
                elif 1 <= tile <= 4:
                    out[3, xi, tile * 8 - 8 : tile * 8, :] = new
                    if sums is not None:
                        total = total + new
                        if tile == 1:
                            sd[3 * XI + xi] = new
                        if tile == 4:
                            su[3 * XI + xi] = new
        return total

    total = lax.fori_loop(0, XI, tendencies, jnp.zeros((8, LANES), F32))
    if sums is not None:
        total = over_groups(jnp.sum(total, axis=0, keepdims=True))
        sums[...] = jnp.broadcast_to(total, (8, LANES))

    v[0, 0, body] = jnp.where(lane_ext < 32, entry(0), pltpu.roll(v[0, XI, body], 32, axis=1))
    v[0, XI + 1, body] = jnp.where(
        lane_ext >= 96, v[0, XI, body], pltpu.roll(v[0, 1, body], 96, axis=1)
    )

    def divergence(xi, carry):
        for tile in range(EXT // 8):
            base = 8 + tile * 8
            here = slice(base, base + 8)
            w = v[2, xi + 1, here, :]
            up = jnp.where(last, 0.0, pltpu.roll(w, LANES - 1, axis=1))
            down = jnp.where(first, 0.0, pltpu.roll(w, 1, axis=1))
            total = (v[0, xi + 2, here, :] - v[0, xi, here, :]) + (up - down)
            total = total + (
                v[1, xi + 1, base + 1 : base + 9, :] - v[1, xi + 1, base - 1 : base + 7, :]
            )
            source = total * F32(0.5 * SIXTH)
            r[xi, tile * 8 : tile * 8 + 8, :] = source
            pa[xi + 1, here, :] = -source
        return carry

    lax.fori_loop(0, XI, divergence, 0)

    def ends(p):
        p[0, body] = jnp.where(lane_ext < 32, 0.0, pltpu.roll(p[XI, body], 32, axis=1))
        p[XI + 1, body] = jnp.where(lane_ext >= 96, 0.0, pltpu.roll(p[1, body], 96, axis=1))

    for sweep in range(SWEEPS):
        p, q = (pa, pb) if sweep % 2 == 0 else (pb, pa)
        ends(p)

        def relax(xi, carry, p=p, q=q):
            for tile in range(EXT // 8):
                base = 8 + tile * 8
                here = slice(base, base + 8)
                mid = p[xi + 1, here, :]
                beside = (p[xi, here, :] + p[xi + 2, here, :]) + (
                    p[xi + 1, base - 1 : base + 7, :] + p[xi + 1, base + 1 : base + 9, :]
                )
                beside = beside + (below(mid, first) + above(mid, last))
                q[xi + 1, here, :] = beside * F32(SIXTH) - r[xi, tile * 8 : tile * 8 + 8, :]
            return carry

        lax.fori_loop(0, XI, relax, 0)
    p = pa if SWEEPS % 2 == 0 else pb
    ends(p)

    def correct(xi, carry):
        for tile in range(1, 5):
            base = 8 + tile * 8
            here = slice(base, base + 8)
            mid = p[xi + 1, here, :]
            slopes = (
                p[xi + 2, here, :] - p[xi, here, :],
                p[xi + 1, base + 1 : base + 9, :] - p[xi + 1, base - 1 : base + 7, :],
                above(mid, last) - below(mid, first),
            )
            for c in range(3):
                new = v[c, xi + 1, here, :] - 0.5 * slopes[c]
                out[c, xi, tile * 8 - 8 : tile * 8, :] = new
                if sums is not None:
                    if tile == 1:
                        sd[c * XI + xi] = new
                    if tile == 4:
                        su[c * XI + xi] = new
        return carry

    lax.fori_loop(0, XI, correct, 0)
    if sums is not None:
        disk_edges(out, maps, su, sd)


def send_kernel(scal, fields, s0, s1, s2, s3, turned):
    own = scal[0]

    def per_row(xi, carry):
        rows = jnp.concatenate([fields[c, xi] for c in range(4)], axis=0)
        turned[...] = rows.T.reshape(GX, 4, 8, LANES)
        for s, out in enumerate((s0, s1, s2, s3)):
            out[pl.ds(xi * 4, 4)] = turned[own ^ s]
        return carry

    lax.fori_loop(0, XI, per_row, 0)


def final_kernel(scal, mean, s0, r1, r2, r3, out, columns, *, cells):
    own, slab = scal[0], scal[1]
    du, dw = mean_response(mean[0:1, :] * F32(1.0 / cells))
    pad = jnp.zeros((LANES - 2 * XI, LANES), F32)
    columns[...] = jnp.concatenate([du, dw, pad], axis=0).T
    own_columns = columns[pl.ds(pl.multiple_of(own * NZ, NZ), NZ), :]
    group = lanes() >> 5
    masks = [group == (slab ^ s) for s in range(4)]
    for x in range(XI):
        for kt in range(4):
            sources = [ref[x * 4 + kt] for ref in (s0, r1, r2, r3)]
            for c in range(4):
                value = None
                for s, source in enumerate(sources):
                    moved = pltpu.roll(source, (((slab ^ s) - c) & 3) * 32, axis=1)
                    value = moved if value is None else jnp.where(masks[s], moved, value)
                if c in (0, 2):
                    column = (0 if c == 0 else XI) + x
                    value = value + own_columns[kt * 8 : kt * 8 + 8, column : column + 1]
                out[c, x, kt * 8 : kt * 8 + 8, :] = value


def ring(groups):
    place = []
    for j in range(groups):
        for b in range(GX):
            i = b ^ (3 * (j & 1))
            place.append(i * groups + j)
    size = len(place)
    up = [(place[s], place[(s + 1) % size]) for s in range(size)]
    return up, [(b, a) for a, b in up]


def swapped(value, axis, size, distance):
    return lax.ppermute(value, axis, [(i, i ^ distance) for i in range(size)])


def reduced(sums, groups):
    distance = 1
    while distance < GX:
        sums = sums + swapped(sums, "gx", GX, distance)
        distance *= 2
    distance = 1
    while distance < groups:
        sums = sums + swapped(sums, "gy", groups, distance)
        distance *= 2
    return sums


def local(state, planes, turbine_cell, active, yaw_sector, slot, *, layouts, groups):
    gx_index, gy_index = lax.axis_index("gx"), lax.axis_index("gy")
    slab = gx_index ^ (3 * (gy_index & 1))
    scal = jnp.stack([gx_index, slab, lax.axis_index("layout")]).astype(jnp.int32)
    cells = float(GX * XI * GX * OWN * groups)
    per_layout = planes.shape[0]
    height = (jnp.arange(NZ).astype(F32) + 0.5) / NZ
    zeros = jnp.zeros((NZ,), F32)
    profile = jnp.tile(jnp.stack([height ** (1.0 / 7.0), zeros, zeros, 0.5 * height]), (1, GX))
    profile = jnp.pad(profile, ((0, 4), (0, 0)))
    up, down = ring(groups)
    gy_up = [(j, (j + 1) % groups) for j in range(groups)]
    gy_down = [(b, a) for a, b in gy_up]

    ids = turbine_cell[0, :, NZ // 2, :].astype(F32)
    ids = jnp.stack([ids, lax.ppermute(ids, "gy", gy_up), lax.ppermute(ids, "gy", gy_down)])

    chunk = shape(TILES, 8, LANES)
    s0, s1, s2, s3, plane = call(
        pack_kernel,
        (chunk, chunk, chunk, chunk, shape(per_layout * 4, 8, LANES)),
        [SMEM, VMEM, VMEM],
        name="pack",
    )(scal, state[0], planes)
    ids = jnp.stack([ids] + [swapped(ids, "gx", GX, s) for s in (1, 2, 3)])
    received = [swapped(value, "gx", GX, s) for s, value in ((1, s1), (2, s2), (3, s3))]
    plane_received = [swapped(plane, "layout", layouts, s) for s in range(1, layouts)]
    maps, counts = call(
        maps_kernel,
        (shape(4, XI, PAD, LANES), shape(2, XI, LANES)),
        [SMEM, SMEM, SMEM, VMEM],
        [pltpu.VMEM((2, GX * XI, LANES), F32)],
        name="maps",
    )(scal, active[0], yaw_sector[0], ids)

    first_payload = shape(TILES + 6, 8, LANES)
    fields, inflow, su, sd, sums = call(
        functools.partial(unpack_kernel, layouts=layouts, per_layout=per_layout),
        (
            shape(4, XI, OWN, LANES),
            shape(4, OWN, LANES),
            first_payload,
            first_payload,
            shape(8, LANES),
        ),
        [SMEM, SMEM, VMEM, VMEM] + [VMEM] * (4 + layouts),
        [
            pltpu.VMEM((GX, TILES, 8, LANES), F32),
            pltpu.VMEM((layouts, per_layout * 4, 8, LANES), F32),
        ],
        name="unpack",
    )(scal, slot, profile, maps, s0, *received, plane, *plane_received)

    mean = None
    for step in range(STEPS):
        lo = lax.ppermute(su, ("gx", "gy"), up)
        hi = lax.ppermute(sd, ("gx", "gy"), down)
        next_mean = reduced(sums, groups)
        outs = [shape(4, XI, OWN, LANES)]
        if step < STEPS - 1:
            outs += [shape(TILES + 2, 8, LANES), shape(TILES + 2, 8, LANES), shape(8, LANES)]
        if step == 0:
            outs += [shape(4, EXT, LANES)]
        operands = [fields, lo, hi, maps, counts, inflow] + ([mean] if step > 0 else [])
        results = call(
            functools.partial(step_kernel, step=step, cells=cells),
            tuple(outs),
            [VMEM] * len(operands),
            [
                pltpu.VMEM((4, XI + 2, PAD, LANES), F32),
                pltpu.VMEM((3, XI + 2, PAD, LANES), F32),
                pltpu.VMEM((XI, EXT, LANES), F32),
                pltpu.VMEM((XI + 2, PAD, LANES), F32),
                pltpu.VMEM((XI + 2, PAD, LANES), F32),
                pltpu.VMEM((XI, PAD, LANES), F32),
                pltpu.VMEM((2, XI, LANES), F32),
                pltpu.VMEM((4, EXT, LANES), F32),
            ],
            flops=30_000_000,
            name="step%d" % step,
        )(*operands)
        results = list(results)
        fields = results.pop(0)
        if step < STEPS - 1:
            su, sd, sums = results[:3]
            del results[:3]
        if step == 0:
            inflow = results.pop(0)
        mean = next_mean

    s0, s1, s2, s3 = call(
        send_kernel,
        (chunk, chunk, chunk, chunk),
        [SMEM, VMEM],
        [pltpu.VMEM((GX, 4, 8, LANES), F32)],
        name="send",
    )(scal, fields)
    received = [swapped(value, "gx", GX, s) for s, value in ((1, s1), (2, s2), (3, s3))]
    fields = call(
        functools.partial(final_kernel, cells=cells),
        shape(4, XI, NZ, LANES),
        [SMEM, VMEM] + [VMEM] * 4,
        [pltpu.VMEM((LANES, LANES), F32)],
        name="final",
    )(scal, mean, s0, *received)
    return fields[None]


def solution(mesh):
    body = functools.partial(local, layouts=mesh.shape["layout"], groups=mesh.shape["gy"])
    return jax.shard_map(
        body,
        mesh=mesh,
        in_specs=(
            P("layout", None, "gx", None, "gy"),
            P("layout", None, None, "gy"),
            P("layout", "gx", None, "gy"),
            P("layout", None),
            P("layout", None),
            P(),
        ),
        out_specs=P("layout", None, "gx", None, "gy"),
        check_vma=False,
    )
```

```python
import functools
import math

import jax
import jax.numpy as jnp
from jax import lax
from jax.experimental import pallas as pl
from jax.experimental.pallas import tpu as pltpu
from jax.sharding import PartitionSpec as P

STEPS = 4
SWEEPS = 4
RADIUS = 5
NZ = 32
XI = 16
GX = 4
OWN = 32
HALO = 8
EXT = OWN + 2 * HALO
PAD = EXT + 16
LANES = 128
WIDTH = 2 * RADIUS + 1
LOWEST = NZ // 2 - RADIUS
TILES = 4 * XI
MORE = 4
UNROLL = {"fill": 4, "tend": 4, "div": 16, "relax": 16, "correct": 16}

TIME_STEP = 0.25
VISCOSITY = 0.02
SMAGORINSKY = 0.0289
DIFFUSIVITY_RATIO = 1.0 / 0.7
BUOYANCY = 0.5
THRUST_COEFF = 1.33
YAW_INCREMENT = 0.1
SIXTH = 1.0 / 6.0
F32 = jnp.float32
INTS = 7
VLIMIT = 40 * 1024 * 1024

VMEM = pl.BlockSpec(memory_space=pltpu.VMEM)
SMEM = pl.BlockSpec(memory_space=pltpu.SMEM)


def shape(*dims):
    return jax.ShapeDtypeStruct(dims, F32)


def lanes(rows=8):
    return lax.broadcasted_iota(jnp.int32, (rows, LANES), 1)


def level_masks(rows=8):
    level = lanes(rows) & (NZ - 1)
    return level == 0, level == NZ - 1


def below(f, first):
    return jnp.where(first, f, pltpu.roll(f, 1, axis=1))


def above(f, last):
    return jnp.where(last, f, pltpu.roll(f, LANES - 1, axis=1))


def call(kernel, out_shape, in_specs, scratch=(), flops=10_000_000, **kwargs):
    return pl.pallas_call(
        kernel,
        out_shape=out_shape,
        in_specs=in_specs,
        out_specs=jax.tree.map(lambda _: VMEM, out_shape),
        scratch_shapes=list(scratch),
        compiler_params=pltpu.CompilerParams(vmem_limit_bytes=VLIMIT),
        cost_estimate=pl.CostEstimate(flops=flops, bytes_accessed=4_000_000, transcendentals=0),
        **kwargs,
    )


def rows(name, body, carry=0):
    count = UNROLL[name]

    def some(index, carry):
        for offset in range(count):
            carry = body(index * count + offset, carry)
        return carry

    return lax.fori_loop(0, XI // count, some, carry)


def group_matrix(banded):
    row = lax.broadcasted_iota(jnp.int32, (LANES, LANES), 0)
    column = lax.broadcasted_iota(jnp.int32, (LANES, LANES), 1)
    level = (row if banded == "row" else column) & (NZ - 1)
    inside = (level >= LOWEST) & (level < LOWEST + WIDTH)
    return jnp.where(((row >> 5) == (column >> 5)) & inside, 1.0, 0.0).astype(F32)


def exact_dot(a, b):
    return jnp.dot(a, b, precision=lax.Precision.HIGHEST, preferred_element_type=F32)


def band_sums(fields, su, sd, sums):
    matrix = group_matrix("row")
    level = lanes(OWN) & (NZ - 1)
    for c in range(2):
        total = exact_dot(fields[c].reshape(XI * OWN, LANES), matrix)
        packed = jnp.zeros((OWN, LANES), F32)
        for xi in range(XI):
            packed = jnp.where(level == xi, total[xi * OWN : (xi + 1) * OWN], packed)
        sums[c] = packed
        for t in range(2):
            sd[TILES + 2 * c + t] = packed[t * 8 : t * 8 + 8]
            su[TILES + 2 * c + t] = packed[16 + t * 8 : 24 + t * 8]


def block_transposed(sources, group, masks):
    out = None
    for c, value in enumerate(sources):
        moved = pltpu.roll(value, ((c - group) & 3) * 32, axis=1)
        out = moved if out is None else jnp.where(masks[c], moved, out)
    return out


def pack_kernel(scal, state, planes, s0, s1, s2, s3, pl_out):
    slab = scal[1]
    group = lanes() >> 5
    masks = [group == c for c in range(4)]

    def per_row(x, carry):
        for kt in range(4):
            sources = [state[c, x, kt * 8 : kt * 8 + 8, :] for c in range(4)]
            for s, out in enumerate((s0, s1, s2, s3)):
                out[x * 4 + kt] = block_transposed(sources, slab ^ s, masks)
        return carry

    lax.fori_loop(0, XI, per_row, 0)
    for plane in range(planes.shape[0]):
        for kt in range(4):
            sources = [planes[plane, c, kt * 8 : kt * 8 + 8, :] for c in range(4)]
            pl_out[plane * 4 + kt] = block_transposed(sources, slab, masks)


def maps_kernel(ints, ids, maps):
    own, slab = ints[0], ints[1]
    lane = lanes(NZ)
    pieces = []
    for g in range(GX):
        source = own ^ g
        moved_mid = pltpu.roll(ids[source, 0], (16 - 32 * slab) & (LANES - 1), axis=1)
        moved_left = pltpu.roll(ids[source, 1], 16, axis=1)
        moved_right = pltpu.roll(ids[source, 2], OWN + 16, axis=1)
        here = jnp.where((lane[:XI] < 16) & (slab == 0), moved_left, moved_mid)
        here = jnp.where((lane[:XI] >= OWN + 16) & (slab == 3), moved_right, here)
        pieces += [here, jnp.full((XI, LANES), -1.0, F32)]
    here = jnp.concatenate(pieces, axis=0)
    turbines = (ints.shape[0] - INTS) // 2

    def per_turbine(t, carry):
        sector, running = carry
        match = here == t.astype(F32)
        return (
            jnp.where(match, ints[INTS + turbines + t].astype(F32), sector),
            jnp.where(match, ints[INTS + t].astype(F32), running),
        )

    sector, running = lax.fori_loop(
        0, turbines, per_turbine, (jnp.full((LANES, LANES), -1.0, F32), jnp.zeros((LANES, LANES), F32))
    )
    cosine = jnp.zeros((LANES, LANES), F32)
    sine = jnp.zeros((LANES, LANES), F32)
    for value in range(8):
        angle = (value - 3.5) * YAW_INCREMENT
        cosine = jnp.where(sector == value, F32(math.cos(angle)), cosine)
        sine = jnp.where(sector == value, F32(math.sin(angle)), sine)
    thrust = running * F32(-0.5 * THRUST_COEFF * TIME_STEP / float(WIDTH**2) ** 2)
    low = lanes(LANES) < 64
    first = jnp.where(low, here, pltpu.roll(thrust, 64, axis=1)).T
    second = jnp.where(low, cosine, pltpu.roll(sine, 64, axis=1)).T
    maps[0], maps[3] = first[:64], first[64:]
    maps[1], maps[2] = second[:64], second[64:]


def over_groups(row):
    row = row + pltpu.roll(row, 64, axis=1)
    return row + pltpu.roll(row, 32, axis=1)


def unpack_kernel(
    scal, profile, s0, r1, r2, r3, p0, *rest, layouts, per_layout
):
    plane_refs = (p0,) + rest[: layouts - 1]
    fields, inflow, su, sd, bands, sums, held, planes = rest[layouts - 1 :]
    own, here = scal[0], scal[2]
    for s, source in enumerate((s0, r1, r2, r3)):
        held[own ^ s] = source[...]
    for s, source in enumerate(plane_refs):
        planes[here ^ s] = source[...]

    def per_row(xi, total):
        parts = [held[g, pl.ds(xi * 4, 4)].reshape(NZ, LANES) for g in range(GX)]
        turned = jnp.concatenate(parts, axis=0).T
        for c in range(4):
            value = turned[c * 32 : c * 32 + 32] + profile[c : c + 1, :]
            fields[c, xi] = value
            sd[c * XI + xi] = value[:HALO]
            su[c * XI + xi] = value[OWN - HALO :]
            if c == 3:
                total = total + jnp.sum(value, axis=0, keepdims=True)
        return total

    total = rows("fill", per_row, jnp.zeros((1, LANES), F32))
    sums[...] = jnp.broadcast_to(over_groups(total), (8, LANES))
    parts = []
    for step in range(STEPS):
        plane = scal[3 + step]
        parts.append(
            planes[plane // per_layout, pl.ds((plane % per_layout) * 4, 4)].reshape(NZ, LANES)
        )
    turned = jnp.concatenate(parts, axis=0).T
    for c in range(4):
        value = turned[c * 32 : c * 32 + 32] + profile[c : c + 1, :]
        inflow[c] = value
        sd[TILES + MORE + c] = value[:HALO]
        su[TILES + MORE + c] = value[OWN - HALO :]
    band_sums(fields, su, sd, bands)


def mean_response(mean):
    lane = lanes(XI)
    row = lax.broadcasted_iota(jnp.int32, (XI, LANES), 0)
    level = lane & (NZ - 1)
    first, last = level == 0, level == NZ - 1

    def x_pair(p):
        lower = pltpu.roll(p, 1, axis=0)
        edge = jnp.where(lane < 32, 0.0, pltpu.roll(lower, 32, axis=1))
        lower = jnp.where(row == 0, edge, lower)
        upper = pltpu.roll(p, XI - 1, axis=0)
        edge = jnp.where(lane >= 96, 0.0, pltpu.roll(upper, 96, axis=1))
        upper = jnp.where(row == XI - 1, edge, upper)
        return lower, upper

    vertical = jnp.broadcast_to(mean, (XI, LANES)) * F32(-TIME_STEP * BUOYANCY)
    up = jnp.where(last, 0.0, pltpu.roll(vertical, LANES - 1, axis=1))
    down = jnp.where(first, 0.0, pltpu.roll(vertical, 1, axis=1))
    source = (up - down) * 0.5
    p = source * F32(-SIXTH)
    for sweep in range(SWEEPS):
        lower, upper = x_pair(p)
        p = (lower + upper + 2.0 * p + above(p, last) + below(p, first) - source) * F32(SIXTH)
    lower, upper = x_pair(p)
    return (upper - lower) * -0.5, vertical - (above(p, last) - below(p, first)) * 0.5


def step_kernel(*refs, step, cells):
    refs = list(refs)
    fields_in, lo, hi, maps, bands_in, inflow_in = refs[:6]
    del refs[:6]
    mean = None
    if step > 0:
        mean = refs.pop(0)
    out = refs.pop(0)
    su = sd = bands = sums = inflow_out = None
    if step < STEPS - 1:
        su, sd, bands, sums = refs[:4]
        del refs[:4]
    if step == 0:
        inflow_out = refs.pop(0)
    f, v, r, pa, pb, ns, change, inflow = refs
    first, last = level_masks()
    lane_ext = lanes(EXT)
    body = slice(8, 8 + EXT)

    if step > 0:
        du, dw = mean_response(mean[0:1, :] * F32(1.0 / cells))
        change[0] = du
        change[1] = dw
        inflow[...] = inflow_in[...]
    else:
        for c in range(4):
            inflow[c, 0:8] = lo[TILES + MORE + c]
            inflow[c, 8 : 8 + OWN] = inflow_in[c]
            inflow[c, 8 + OWN : EXT] = hi[TILES + MORE + c]
        inflow_out[...] = inflow[...]

    def fill(xi, carry):
        for c in range(4):
            low, mid, high = lo[c * XI + xi], fields_in[c, xi], hi[c * XI + xi]
            if step > 0 and c in (0, 2):
                d = change[c // 2, pl.ds(xi, 1), :]
                low, mid, high = low + d, mid + d, high + d
            f[c, xi + 1, 8:16] = low
            f[c, xi + 1, 16 : 16 + OWN] = mid
            f[c, xi + 1, 16 + OWN : 8 + EXT] = high
        return carry

    rows("fill", fill)
    shift = (LANES - 32 * step) % LANES

    def entry(c):
        value = inflow[c]
        return pltpu.roll(value, shift, axis=1) if shift else value

    for c in range(4):
        f[c, 0, body] = jnp.where(
            lane_ext < 32, entry(c), pltpu.roll(f[c, XI, body], 32, axis=1)
        )
        f[c, XI + 1, body] = jnp.where(
            lane_ext >= 96, f[c, XI, body], pltpu.roll(f[c, 1, body], 96, axis=1)
        )

    packed = []
    for c in range(2):
        parts = [lo[TILES + 2 * c + t] for t in range(2)] + [bands_in[c]]
        parts += [hi[TILES + 2 * c + t] for t in range(2)]
        packed.append(jnp.concatenate(parts, axis=0))
    if step > 0:
        level = lanes(XI) & (NZ - 1)
        row = lax.broadcasted_iota(jnp.int32, (XI, LANES), 0)
        shift_u = jnp.where(level == row, exact_dot(change[0], group_matrix("row")), 0.0)
        packed[0] = packed[0] + jnp.sum(shift_u, axis=0, keepdims=True)
    ident, cosine, sine = maps[0], maps[1], maps[2]
    speed = cosine * packed[0] + sine * packed[1]
    forward = backward = speed
    size = ident.shape[0]
    row = lax.broadcasted_iota(jnp.int32, ident.shape, 0)
    for d in (1, 2, 4, 8):
        same = (ident == pltpu.roll(ident, d, axis=0)) & (row >= d)
        forward = forward + jnp.where(same, pltpu.roll(forward, d, axis=0), 0.0)
        same = (ident == pltpu.roll(ident, size - d, axis=0)) & (row < size - d)
        backward = backward + jnp.where(same, pltpu.roll(backward, size - d, axis=0), 0.0)
    total = forward + backward - speed
    thrust = maps[3] * total * jnp.abs(total)
    level = lanes(EXT) & (NZ - 1)
    matrix = group_matrix("column")
    for c, direction in enumerate((cosine, sine)):
        pushed = (thrust * direction)[8 : 8 + EXT]
        for part in range(0, XI, 4):
            spread = [jnp.where(level == xi, pushed, 0.0) for xi in range(part, part + 4)]
            result = exact_dot(jnp.concatenate(spread, axis=0), matrix)
            ns[c, part : part + 4] = result.reshape(4, EXT, LANES)

    def tendencies(xi, total):
        for tile in range(EXT // 8):
            base = 8 + tile * 8
            centre, gx, gy, gz, lap = [], [], [], [], []
            for c in range(4):
                mid = f[c, xi + 1, base : base + 8, :]
                xm = f[c, xi, base : base + 8, :]
                xp = f[c, xi + 2, base : base + 8, :]
                ym = f[c, xi + 1, base - 1 : base + 7, :]
                yp = f[c, xi + 1, base + 1 : base + 9, :]
                if c == 2:
                    zm = jnp.where(first, 0.0, pltpu.roll(mid, 1, axis=1))
                    zp = jnp.where(last, 0.0, pltpu.roll(mid, LANES - 1, axis=1))
                else:
                    zm, zp = below(mid, first), above(mid, last)
                centre.append(mid)
                gx.append(xp - xm)
                gy.append(yp - ym)
                gz.append(zp - zm)
                lap.append((xp + xm) + (yp + ym) + (zp + zm) - 6.0 * mid)
            s_xy = gy[0] + gx[1]
            s_xz = gz[0] + gx[2]
            s_yz = gz[1] + gy[2]
            strain = jnp.sqrt(
                2.0 * (gx[0] * gx[0] + gy[1] * gy[1] + gz[2] * gz[2])
                + (s_xy * s_xy + s_xz * s_xz + s_yz * s_yz)
            )
            nu = F32(TIME_STEP * VISCOSITY) + F32(0.5 * TIME_STEP * SMAGORINSKY) * strain
            half = F32(0.5 * TIME_STEP)
            au, av, aw = half * centre[0], half * centre[1], half * centre[2]
            for c in range(4):
                scale = nu * F32(DIFFUSIVITY_RATIO) if c == 3 else nu
                new = centre[c] + (scale * lap[c] - (au * gx[c] + av * gy[c] + aw * gz[c]))
                if c < 2:
                    new = new + ns[c, xi, tile * 8 : tile * 8 + 8, :]
                elif c == 2:
                    new = new + F32(TIME_STEP * BUOYANCY) * centre[3]
                if c < 3:
                    v[c, xi + 1, base : base + 8, :] = new
                elif 1 <= tile <= 4:
                    out[3, xi, tile * 8 - 8 : tile * 8, :] = new
                    if sums is not None:
                        total = total + new
                        if tile == 1:
                            sd[3 * XI + xi] = new
                        if tile == 4:
                            su[3 * XI + xi] = new
        return total

    total = rows("tend", tendencies, jnp.zeros((8, LANES), F32))
    if sums is not None:
        total = over_groups(jnp.sum(total, axis=0, keepdims=True))
        sums[...] = jnp.broadcast_to(total, (8, LANES))

    v[0, 0, body] = jnp.where(lane_ext < 32, entry(0), pltpu.roll(v[0, XI, body], 32, axis=1))
    v[0, XI + 1, body] = jnp.where(
        lane_ext >= 96, v[0, XI, body], pltpu.roll(v[0, 1, body], 96, axis=1)
    )

    def divergence(xi, carry):
        for tile in range(EXT // 8):
            base = 8 + tile * 8
            here = slice(base, base + 8)
            w = v[2, xi + 1, here, :]
            up = jnp.where(last, 0.0, pltpu.roll(w, LANES - 1, axis=1))
            down = jnp.where(first, 0.0, pltpu.roll(w, 1, axis=1))
            total = (v[0, xi + 2, here, :] - v[0, xi, here, :]) + (up - down)
            total = total + (
                v[1, xi + 1, base + 1 : base + 9, :] - v[1, xi + 1, base - 1 : base + 7, :]
            )
            source = total * F32(0.5 * SIXTH)
            r[xi, tile * 8 : tile * 8 + 8, :] = source
            pa[xi + 1, here, :] = -source
        return carry

    rows("div", divergence)

    def ends(p):
        p[0, body] = jnp.where(lane_ext < 32, 0.0, pltpu.roll(p[XI, body], 32, axis=1))
        p[XI + 1, body] = jnp.where(lane_ext >= 96, 0.0, pltpu.roll(p[1, body], 96, axis=1))

    for sweep in range(SWEEPS):
        p, q = (pa, pb) if sweep % 2 == 0 else (pb, pa)
        ends(p)

        def relax(xi, carry, p=p, q=q):
            for tile in range(EXT // 8):
                base = 8 + tile * 8
                here = slice(base, base + 8)
                mid = p[xi + 1, here, :]
                beside = (p[xi, here, :] + p[xi + 2, here, :]) + (
                    p[xi + 1, base - 1 : base + 7, :] + p[xi + 1, base + 1 : base + 9, :]
                )
                beside = beside + (below(mid, first) + above(mid, last))
                q[xi + 1, here, :] = beside * F32(SIXTH) - r[xi, tile * 8 : tile * 8 + 8, :]
            return carry

        rows("relax", relax)
    p = pa if SWEEPS % 2 == 0 else pb
    ends(p)

    def correct(xi, carry):
        for tile in range(1, 5):
            base = 8 + tile * 8
            here = slice(base, base + 8)
            mid = p[xi + 1, here, :]
            slopes = (
                p[xi + 2, here, :] - p[xi, here, :],
                p[xi + 1, base + 1 : base + 9, :] - p[xi + 1, base - 1 : base + 7, :],
                above(mid, last) - below(mid, first),
            )
            for c in range(3):
                new = v[c, xi + 1, here, :] - 0.5 * slopes[c]
                out[c, xi, tile * 8 - 8 : tile * 8, :] = new
                if sums is not None:
                    if tile == 1:
                        sd[c * XI + xi] = new
                    if tile == 4:
                        su[c * XI + xi] = new
        return carry

    rows("correct", correct)
    if sums is not None:
        band_sums(out, su, sd, bands)


def step_scratch():
    return [
        pltpu.VMEM((4, XI + 2, PAD, LANES), F32),
        pltpu.VMEM((3, XI + 2, PAD, LANES), F32),
        pltpu.VMEM((XI, EXT, LANES), F32),
        pltpu.VMEM((XI + 2, PAD, LANES), F32),
        pltpu.VMEM((XI + 2, PAD, LANES), F32),
        pltpu.VMEM((2, XI, EXT, LANES), F32),
        pltpu.VMEM((2, XI, LANES), F32),
        pltpu.VMEM((4, EXT, LANES), F32),
    ]


def send_kernel(scal, fields, s0, s1, s2, s3, turned):
    own = scal[0]

    def per_row(xi, carry):
        stacked = jnp.concatenate([fields[c, xi] for c in range(4)], axis=0)
        turned[...] = stacked.T.reshape(GX, 4, 8, LANES)
        for s, out in enumerate((s0, s1, s2, s3)):
            out[pl.ds(xi * 4, 4)] = turned[own ^ s]
        return carry

    lax.fori_loop(0, XI, per_row, 0)


def final_kernel(scal, mean, s0, r1, r2, r3, out, columns, *, cells):
    own, slab = scal[0], scal[1]
    du, dw = mean_response(mean[0:1, :] * F32(1.0 / cells))
    pad = jnp.zeros((LANES - 2 * XI, LANES), F32)
    columns[...] = jnp.concatenate([du, dw, pad], axis=0).T
    own_columns = columns[pl.ds(pl.multiple_of(own * NZ, NZ), NZ), :]
    group = lanes() >> 5
    masks = [group == (slab ^ s) for s in range(4)]
    for x in range(XI):
        for kt in range(4):
            sources = [ref[x * 4 + kt] for ref in (s0, r1, r2, r3)]
            for c in range(4):
                value = None
                for s, source in enumerate(sources):
                    moved = pltpu.roll(source, (((slab ^ s) - c) & 3) * 32, axis=1)
                    value = moved if value is None else jnp.where(masks[s], moved, value)
                if c in (0, 2):
                    column = (0 if c == 0 else XI) + x
                    value = value + own_columns[kt * 8 : kt * 8 + 8, column : column + 1]
                out[c, x, kt * 8 : kt * 8 + 8, :] = value


def ring(groups):
    place = []
    for j in range(groups):
        for b in range(GX):
            i = b ^ (3 * (j & 1))
            place.append(i * groups + j)
    size = len(place)
    up = [(place[s], place[(s + 1) % size]) for s in range(size)]
    return up, [(b, a) for a, b in up]


def swapped(value, axis, size, distance):
    return lax.ppermute(value, axis, [(i, i ^ distance) for i in range(size)])


def local(state, planes, turbine_cell, active, yaw_sector, slot, *, layouts, groups):
    gx_index, gy_index = lax.axis_index("gx"), lax.axis_index("gy")
    slab = gx_index ^ (3 * (gy_index & 1))
    scal = jnp.stack([gx_index, slab, lax.axis_index("layout")]).astype(jnp.int32)
    scal = jnp.concatenate([scal, slot, active[0], yaw_sector[0]])
    cells = float(GX * XI * GX * OWN * groups)
    per_layout = planes.shape[0]
    height = (jnp.arange(NZ).astype(F32) + 0.5) / NZ
    zeros = jnp.zeros((NZ,), F32)
    profile = jnp.tile(jnp.stack([height ** (1.0 / 7.0), zeros, zeros, 0.5 * height]), (1, GX))
    profile = jnp.pad(profile, ((0, 4), (0, 0)))
    up, down = ring(groups)
    gy_up = [(j, (j + 1) % groups) for j in range(groups)]
    gy_down = [(b, a) for a, b in gy_up]

    ids = turbine_cell[0, :, NZ // 2, :].astype(F32)
    ids = jnp.stack([ids, lax.ppermute(ids, "gy", gy_up), lax.ppermute(ids, "gy", gy_down)])

    chunk = shape(TILES, 8, LANES)
    s0, s1, s2, s3, plane = call(
        pack_kernel,
        (chunk, chunk, chunk, chunk, shape(per_layout * 4, 8, LANES)),
        [SMEM, VMEM, VMEM],
        name="pack",
    )(scal, state[0], planes)
    ids = jnp.stack([ids] + [swapped(ids, "gx", GX, s) for s in (1, 2, 3)])
    received = [swapped(value, "gx", GX, s) for s, value in ((1, s1), (2, s2), (3, s3))]
    plane_received = [swapped(plane, "layout", layouts, s) for s in range(1, layouts)]
    maps = call(maps_kernel, shape(4, 2 * OWN, LANES), [SMEM, VMEM], name="maps")(scal, ids)

    first_payload = shape(TILES + MORE + 4, 8, LANES)
    fields, inflow, su, sd, bands, sums = call(
        functools.partial(unpack_kernel, layouts=layouts, per_layout=per_layout),
        (
            shape(4, XI, OWN, LANES),
            shape(4, OWN, LANES),
            first_payload,
            first_payload,
            shape(2, OWN, LANES),
            shape(8, LANES),
        ),
        [SMEM, VMEM] + [VMEM] * (4 + layouts),
        [
            pltpu.VMEM((GX, TILES, 8, LANES), F32),
            pltpu.VMEM((layouts, per_layout * 4, 8, LANES), F32),
        ],
        name="unpack",
    )(scal, profile, s0, *received, plane, *plane_received)

    half = groups // 2
    mean = pending = None
    for step in range(STEPS):
        lo = lax.ppermute(su, ("gx", "gy"), up)
        hi = lax.ppermute(sd, ("gx", "gy"), down)
        if pending is not None:
            mean = pending
            distance = 1
            while distance < half:
                mean = mean + swapped(mean, "gy", groups, distance)
                distance *= 2
        partial = sums + swapped(sums, "gx", GX, 1)
        partial = partial + swapped(partial, "gy", groups, half)
        fields, partial = lax.optimization_barrier((fields, partial))
        arriving = swapped(partial, "gx", GX, 2)
        outs = [shape(4, XI, OWN, LANES)]
        if step < STEPS - 1:
            payload = shape(TILES + MORE, 8, LANES)
            outs += [payload, payload, shape(2, OWN, LANES), shape(8, LANES)]
        if step == 0:
            outs += [shape(4, EXT, LANES)]
        operands = [fields, lo, hi, maps, bands, inflow] + ([mean] if step > 0 else [])
        results = call(
            functools.partial(step_kernel, step=step, cells=cells),
            tuple(outs),
            [VMEM] * len(operands),
            step_scratch(),
            flops=30_000_000,
            name="step%d" % step,
        )(*operands)
        results = list(results)
        fields = results.pop(0)
        if step < STEPS - 1:
            su, sd, bands, sums = results[:4]
            del results[:4]
        if step == 0:
            inflow = results.pop(0)
        fields, arriving = lax.optimization_barrier((fields, arriving))
        pending = partial + arriving
    mean = pending
    distance = 1
    while distance < half:
        mean = mean + swapped(mean, "gy", groups, distance)
        distance *= 2

    s0, s1, s2, s3 = call(
        send_kernel,
        (chunk, chunk, chunk, chunk),
        [SMEM, VMEM],
        [pltpu.VMEM((GX, 4, 8, LANES), F32)],
        name="send",
    )(scal, fields)
    received = [swapped(value, "gx", GX, s) for s, value in ((1, s1), (2, s2), (3, s3))]
    fields = call(
        functools.partial(final_kernel, cells=cells),
        shape(4, XI, NZ, LANES),
        [SMEM, VMEM] + [VMEM] * 4,
        [pltpu.VMEM((LANES, LANES), F32)],
        name="final",
    )(scal, mean, s0, *received)
    return fields[None]


def solution(mesh):
    body = functools.partial(local, layouts=mesh.shape["layout"], groups=mesh.shape["gy"])
    return jax.shard_map(
        body,
        mesh=mesh,
        in_specs=(
            P("layout", None, "gx", None, "gy"),
            P("layout", None, None, "gy"),
            P("layout", "gx", None, "gy"),
            P("layout", None),
            P("layout", None),
            P(),
        ),
        out_specs=P("layout", None, "gx", None, "gy"),
        check_vma=False,
    )
```

```python
import functools
import math

import jax
import jax.numpy as jnp
from jax import lax
from jax.experimental import pallas as pl
from jax.experimental.pallas import tpu as pltpu
from jax.sharding import PartitionSpec as P

STEPS = 4
SWEEPS = 4
RADIUS = 5
NZ = 32
XI = 16
GX = 4
OWN = 32
HALO = 8
EXT = OWN + 2 * HALO
PAD = EXT + 16
LANES = 128
WIDTH = 2 * RADIUS + 1
LOWEST = NZ // 2 - RADIUS
TILES = 4 * XI
MORE = 4
UNROLL = {"fill": 4, "tend": 4, "div": 16, "relax": 16, "correct": 16}

TIME_STEP = 0.25
VISCOSITY = 0.02
SMAGORINSKY = 0.0289
DIFFUSIVITY_RATIO = 1.0 / 0.7
BUOYANCY = 0.5
THRUST_COEFF = 1.33
YAW_INCREMENT = 0.1
SIXTH = 1.0 / 6.0
F32 = jnp.float32
INTS = 7
VLIMIT = 40 * 1024 * 1024

VMEM = pl.BlockSpec(memory_space=pltpu.VMEM)
SMEM = pl.BlockSpec(memory_space=pltpu.SMEM)


def shape(*dims):
    return jax.ShapeDtypeStruct(dims, F32)


def lanes(rows=8):
    return lax.broadcasted_iota(jnp.int32, (rows, LANES), 1)


def level_masks(rows=8):
    level = lanes(rows) & (NZ - 1)
    return level == 0, level == NZ - 1


def below(f, first):
    return jnp.where(first, f, pltpu.roll(f, 1, axis=1))


def above(f, last):
    return jnp.where(last, f, pltpu.roll(f, LANES - 1, axis=1))


def call(kernel, out_shape, in_specs, scratch=(), flops=2_000_000_000, **kwargs):
    return pl.pallas_call(
        kernel,
        out_shape=out_shape,
        in_specs=in_specs,
        out_specs=jax.tree.map(lambda _: VMEM, out_shape),
        scratch_shapes=list(scratch),
        compiler_params=pltpu.CompilerParams(vmem_limit_bytes=VLIMIT),
        cost_estimate=pl.CostEstimate(flops=flops, bytes_accessed=4_000_000, transcendentals=0),
        **kwargs,
    )


def rows(name, body, carry=0):
    count = UNROLL[name]

    def some(index, carry):
        for offset in range(count):
            carry = body(index * count + offset, carry)
        return carry

    return lax.fori_loop(0, XI // count, some, carry)


def group_matrix(banded):
    row = lax.broadcasted_iota(jnp.int32, (LANES, LANES), 0)
    column = lax.broadcasted_iota(jnp.int32, (LANES, LANES), 1)
    level = (row if banded == "row" else column) & (NZ - 1)
    inside = (level >= LOWEST) & (level < LOWEST + WIDTH)
    return jnp.where(((row >> 5) == (column >> 5)) & inside, 1.0, 0.0).astype(F32)


def exact_dot(a, b):
    return jnp.dot(a, b, precision=lax.Precision.HIGHEST, preferred_element_type=F32)


def band_sums(fields, su, sd, sums):
    matrix = group_matrix("row")
    level = lanes(OWN) & (NZ - 1)
    for c in range(2):
        total = exact_dot(fields[c].reshape(XI * OWN, LANES), matrix)
        packed = jnp.zeros((OWN, LANES), F32)
        for xi in range(XI):
            packed = jnp.where(level == xi, total[xi * OWN : (xi + 1) * OWN], packed)
        sums[c] = packed
        for t in range(2):
            sd[TILES + 2 * c + t] = packed[t * 8 : t * 8 + 8]
            su[TILES + 2 * c + t] = packed[16 + t * 8 : 24 + t * 8]


def block_transposed(sources, group, masks):
    out = None
    for c, value in enumerate(sources):
        moved = pltpu.roll(value, ((c - group) & 3) * 32, axis=1)
        out = moved if out is None else jnp.where(masks[c], moved, out)
    return out


def pack_kernel(scal, state, planes, ids, s0, s1, s2, s3, pl_out):
    slab = scal[1]
    group = lanes() >> 5
    masks = [group == c for c in range(4)]

    def per_row(x, carry):
        for kt in range(4):
            sources = [state[c, x, kt * 8 : kt * 8 + 8, :] for c in range(4)]
            for s, out in enumerate((s0, s1, s2, s3)):
                out[x * 4 + kt] = block_transposed(sources, slab ^ s, masks)
        return carry

    rows("fill", per_row)
    for half in range(2):
        for out in (s0, s1, s2, s3):
            out[TILES + half] = ids[half * 8 : half * 8 + 8].astype(F32)
    for plane in range(planes.shape[0]):
        for kt in range(4):
            sources = [planes[plane, c, kt * 8 : kt * 8 + 8, :] for c in range(4)]
            pl_out[plane * 4 + kt] = block_transposed(sources, slab, masks)


def maps_kernel(ints, mid, left, right, maps):
    slab = ints[1]
    lane = lanes(NZ)
    pieces = []
    for g in range(GX):
        moved_mid = pltpu.roll(mid[g], (16 - 32 * slab) & (LANES - 1), axis=1)
        moved_left = pltpu.roll(left[g], 16, axis=1)
        moved_right = pltpu.roll(right[g], OWN + 16, axis=1)
        here = jnp.where((lane[:XI] < 16) & (slab == 0), moved_left, moved_mid)
        here = jnp.where((lane[:XI] >= OWN + 16) & (slab == 3), moved_right, here)
        pieces += [here, jnp.full((XI, LANES), -1.0, F32)]
    here = jnp.concatenate(pieces, axis=0)
    turbines = (ints.shape[0] - INTS) // 2

    def per_turbine(t, carry):
        sector, running = carry
        match = here == t.astype(F32)
        return (
            jnp.where(match, ints[INTS + turbines + t].astype(F32), sector),
            jnp.where(match, ints[INTS + t].astype(F32), running),
        )

    sector, running = lax.fori_loop(
        0, turbines, per_turbine, (jnp.full((LANES, LANES), -1.0, F32), jnp.zeros((LANES, LANES), F32))
    )
    cosine = jnp.zeros((LANES, LANES), F32)
    sine = jnp.zeros((LANES, LANES), F32)
    for value in range(8):
        angle = (value - 3.5) * YAW_INCREMENT
        cosine = jnp.where(sector == value, F32(math.cos(angle)), cosine)
        sine = jnp.where(sector == value, F32(math.sin(angle)), sine)
    thrust = running * F32(-0.5 * THRUST_COEFF * TIME_STEP / float(WIDTH**2) ** 2)
    low = lanes(LANES) < 64
    first = jnp.where(low, here, pltpu.roll(thrust, 64, axis=1)).T
    second = jnp.where(low, cosine, pltpu.roll(sine, 64, axis=1)).T
    maps[0], maps[3] = first[:64], first[64:]
    maps[1], maps[2] = second[:64], second[64:]


def over_groups(row):
    row = row + pltpu.roll(row, 64, axis=1)
    return row + pltpu.roll(row, 32, axis=1)


def unpack_kernel(
    scal, profile, s0, r1, r2, r3, p0, *rest, layouts, per_layout
):
    plane_refs = (p0,) + rest[: layouts - 1]
    fields, inflow, su, sd, bands, sums, ids, held, planes = rest[layouts - 1 :]
    own, here = scal[0], scal[2]
    for s, source in enumerate((s0, r1, r2, r3)):
        held[own ^ s] = source[:TILES]
        for half in range(2):
            ids[own ^ s, half * 8 : half * 8 + 8, :] = source[TILES + half]
    for s, source in enumerate(plane_refs):
        planes[here ^ s] = source[...]

    def per_row(xi, total):
        parts = [held[g, pl.ds(xi * 4, 4)].reshape(NZ, LANES) for g in range(GX)]
        turned = jnp.concatenate(parts, axis=0).T
        for c in range(4):
            value = turned[c * 32 : c * 32 + 32] + profile[c : c + 1, :]
            fields[c, xi] = value
            sd[c * XI + xi] = value[:HALO]
            su[c * XI + xi] = value[OWN - HALO :]
            if c == 3:
                total = total + jnp.sum(value, axis=0, keepdims=True)
        return total

    total = rows("fill", per_row, jnp.zeros((1, LANES), F32))
    sums[...] = jnp.broadcast_to(over_groups(total), (8, LANES))
    parts = []
    for step in range(STEPS):
        plane = scal[3 + step]
        parts.append(
            planes[plane // per_layout, pl.ds((plane % per_layout) * 4, 4)].reshape(NZ, LANES)
        )
    turned = jnp.concatenate(parts, axis=0).T
    for c in range(4):
        value = turned[c * 32 : c * 32 + 32] + profile[c : c + 1, :]
        inflow[c] = value
        sd[TILES + MORE + c] = value[:HALO]
        su[TILES + MORE + c] = value[OWN - HALO :]
    band_sums(fields, su, sd, bands)


def mean_response(mean):
    lane = lanes(XI)
    row = lax.broadcasted_iota(jnp.int32, (XI, LANES), 0)
    level = lane & (NZ - 1)
    first, last = level == 0, level == NZ - 1

    def x_pair(p):
        lower = pltpu.roll(p, 1, axis=0)
        edge = jnp.where(lane < 32, 0.0, pltpu.roll(lower, 32, axis=1))
        lower = jnp.where(row == 0, edge, lower)
        upper = pltpu.roll(p, XI - 1, axis=0)
        edge = jnp.where(lane >= 96, 0.0, pltpu.roll(upper, 96, axis=1))
        upper = jnp.where(row == XI - 1, edge, upper)
        return lower, upper

    vertical = jnp.broadcast_to(mean, (XI, LANES)) * F32(-TIME_STEP * BUOYANCY)
    up = jnp.where(last, 0.0, pltpu.roll(vertical, LANES - 1, axis=1))
    down = jnp.where(first, 0.0, pltpu.roll(vertical, 1, axis=1))
    source = (up - down) * 0.5
    p = source * F32(-SIXTH)
    for sweep in range(SWEEPS):
        lower, upper = x_pair(p)
        p = (lower + upper + 2.0 * p + above(p, last) + below(p, first) - source) * F32(SIXTH)
    lower, upper = x_pair(p)
    return (upper - lower) * -0.5, vertical - (above(p, last) - below(p, first)) * 0.5


def step_kernel(*refs, step, cells):
    refs = list(refs)
    fields_in, lo, hi, maps, bands_in, inflow_in = refs[:6]
    del refs[:6]
    mean = None
    if step > 0:
        mean = refs.pop(0)
    out = refs.pop(0)
    su = sd = bands = sums = inflow_out = None
    if step < STEPS - 1:
        su, sd, bands, sums = refs[:4]
        del refs[:4]
    if step == 0:
        inflow_out = refs.pop(0)
    f, v, r, pa, pb, ns, change, inflow = refs
    first, last = level_masks()
    lane_ext = lanes(EXT)
    body = slice(8, 8 + EXT)

    if step > 0:
        du, dw = mean_response(mean[0:1, :] * F32(1.0 / cells))
        change[0] = du
        change[1] = dw
        inflow[...] = inflow_in[...]
    else:
        for c in range(4):
            inflow[c, 0:8] = lo[TILES + MORE + c]
            inflow[c, 8 : 8 + OWN] = inflow_in[c]
            inflow[c, 8 + OWN : EXT] = hi[TILES + MORE + c]
        inflow_out[...] = inflow[...]

    def fill(xi, carry):
        for c in range(4):
            low, mid, high = lo[c * XI + xi], fields_in[c, xi], hi[c * XI + xi]
            if step > 0 and c in (0, 2):
                d = change[c // 2, pl.ds(xi, 1), :]
                low, mid, high = low + d, mid + d, high + d
            f[c, xi + 1, 8:16] = low
            f[c, xi + 1, 16 : 16 + OWN] = mid
            f[c, xi + 1, 16 + OWN : 8 + EXT] = high
        return carry

    rows("fill", fill)
    shift = (LANES - 32 * step) % LANES

    def entry(c):
        value = inflow[c]
        return pltpu.roll(value, shift, axis=1) if shift else value

    for c in range(4):
        f[c, 0, body] = jnp.where(
            lane_ext < 32, entry(c), pltpu.roll(f[c, XI, body], 32, axis=1)
        )
        f[c, XI + 1, body] = jnp.where(
            lane_ext >= 96, f[c, XI, body], pltpu.roll(f[c, 1, body], 96, axis=1)
        )

    packed = []
    for c in range(2):
        parts = [lo[TILES + 2 * c + t] for t in range(2)] + [bands_in[c]]
        parts += [hi[TILES + 2 * c + t] for t in range(2)]
        packed.append(jnp.concatenate(parts, axis=0))
    if step > 0:
        level = lanes(XI) & (NZ - 1)
        row = lax.broadcasted_iota(jnp.int32, (XI, LANES), 0)
        shift_u = jnp.where(level == row, exact_dot(change[0], group_matrix("row")), 0.0)
        packed[0] = packed[0] + jnp.sum(shift_u, axis=0, keepdims=True)
    ident, cosine, sine = maps[0], maps[1], maps[2]
    speed = cosine * packed[0] + sine * packed[1]
    forward = backward = speed
    size = ident.shape[0]
    row = lax.broadcasted_iota(jnp.int32, ident.shape, 0)
    for d in (1, 2, 4, 8):
        same = (ident == pltpu.roll(ident, d, axis=0)) & (row >= d)
        forward = forward + jnp.where(same, pltpu.roll(forward, d, axis=0), 0.0)
        same = (ident == pltpu.roll(ident, size - d, axis=0)) & (row < size - d)
        backward = backward + jnp.where(same, pltpu.roll(backward, size - d, axis=0), 0.0)
    total = forward + backward - speed
    thrust = maps[3] * total * jnp.abs(total)
    level = lanes(EXT) & (NZ - 1)
    matrix = group_matrix("column")
    for c, direction in enumerate((cosine, sine)):
        pushed = (thrust * direction)[8 : 8 + EXT]
        for part in range(0, XI, 4):
            spread = [jnp.where(level == xi, pushed, 0.0) for xi in range(part, part + 4)]
            result = exact_dot(jnp.concatenate(spread, axis=0), matrix)
            ns[c, part : part + 4] = result.reshape(4, EXT, LANES)

    def tendencies(xi, total):
        for tile in range(EXT // 8):
            base = 8 + tile * 8
            centre, gx, gy, gz, lap = [], [], [], [], []
            for c in range(4):
                mid = f[c, xi + 1, base : base + 8, :]
                xm = f[c, xi, base : base + 8, :]
                xp = f[c, xi + 2, base : base + 8, :]
                ym = f[c, xi + 1, base - 1 : base + 7, :]
                yp = f[c, xi + 1, base + 1 : base + 9, :]
                if c == 2:
                    zm = jnp.where(first, 0.0, pltpu.roll(mid, 1, axis=1))
                    zp = jnp.where(last, 0.0, pltpu.roll(mid, LANES - 1, axis=1))
                else:
                    zm, zp = below(mid, first), above(mid, last)
                centre.append(mid)
                gx.append(xp - xm)
                gy.append(yp - ym)
                gz.append(zp - zm)
                lap.append((xp + xm) + (yp + ym) + (zp + zm) - 6.0 * mid)
            s_xy = gy[0] + gx[1]
            s_xz = gz[0] + gx[2]
            s_yz = gz[1] + gy[2]
            strain = jnp.sqrt(
                2.0 * (gx[0] * gx[0] + gy[1] * gy[1] + gz[2] * gz[2])
                + (s_xy * s_xy + s_xz * s_xz + s_yz * s_yz)
            )
            nu = F32(TIME_STEP * VISCOSITY) + F32(0.5 * TIME_STEP * SMAGORINSKY) * strain
            half = F32(0.5 * TIME_STEP)
            au, av, aw = half * centre[0], half * centre[1], half * centre[2]
            for c in range(4):
                scale = nu * F32(DIFFUSIVITY_RATIO) if c == 3 else nu
                new = centre[c] + (scale * lap[c] - (au * gx[c] + av * gy[c] + aw * gz[c]))
                if c < 2:
                    new = new + ns[c, xi, tile * 8 : tile * 8 + 8, :]
                elif c == 2:
                    new = new + F32(TIME_STEP * BUOYANCY) * centre[3]
                if c < 3:
                    v[c, xi + 1, base : base + 8, :] = new
                elif 1 <= tile <= 4:
                    out[3, xi, tile * 8 - 8 : tile * 8, :] = new
                    if sums is not None:
                        total = total + new
                        if tile == 1:
                            sd[3 * XI + xi] = new
                        if tile == 4:
                            su[3 * XI + xi] = new
        return total

    total = rows("tend", tendencies, jnp.zeros((8, LANES), F32))
    if sums is not None:
        total = over_groups(jnp.sum(total, axis=0, keepdims=True))
        sums[...] = jnp.broadcast_to(total, (8, LANES))

    v[0, 0, body] = jnp.where(lane_ext < 32, entry(0), pltpu.roll(v[0, XI, body], 32, axis=1))
    v[0, XI + 1, body] = jnp.where(
        lane_ext >= 96, v[0, XI, body], pltpu.roll(v[0, 1, body], 96, axis=1)
    )

    def divergence(xi, carry):
        for tile in range(EXT // 8):
            base = 8 + tile * 8
            here = slice(base, base + 8)
            w = v[2, xi + 1, here, :]
            up = jnp.where(last, 0.0, pltpu.roll(w, LANES - 1, axis=1))
            down = jnp.where(first, 0.0, pltpu.roll(w, 1, axis=1))
            total = (v[0, xi + 2, here, :] - v[0, xi, here, :]) + (up - down)
            total = total + (
                v[1, xi + 1, base + 1 : base + 9, :] - v[1, xi + 1, base - 1 : base + 7, :]
            )
            source = total * F32(0.5 * SIXTH)
            r[xi, tile * 8 : tile * 8 + 8, :] = source
            pa[xi + 1, here, :] = -source
        return carry

    rows("div", divergence)

    def ends(p):
        p[0, body] = jnp.where(lane_ext < 32, 0.0, pltpu.roll(p[XI, body], 32, axis=1))
        p[XI + 1, body] = jnp.where(lane_ext >= 96, 0.0, pltpu.roll(p[1, body], 96, axis=1))

    for sweep in range(SWEEPS):
        p, q = (pa, pb) if sweep % 2 == 0 else (pb, pa)
        ends(p)

        def relax(xi, carry, p=p, q=q):
            for tile in range(EXT // 8):
                base = 8 + tile * 8
                here = slice(base, base + 8)
                mid = p[xi + 1, here, :]
                beside = (p[xi, here, :] + p[xi + 2, here, :]) + (
                    p[xi + 1, base - 1 : base + 7, :] + p[xi + 1, base + 1 : base + 9, :]
                )
                beside = beside + (below(mid, first) + above(mid, last))
                q[xi + 1, here, :] = beside * F32(SIXTH) - r[xi, tile * 8 : tile * 8 + 8, :]
            return carry

        rows("relax", relax)
    p = pa if SWEEPS % 2 == 0 else pb
    ends(p)

    def correct(xi, carry):
        for tile in range(1, 5):
            base = 8 + tile * 8
            here = slice(base, base + 8)
            mid = p[xi + 1, here, :]
            slopes = (
                p[xi + 2, here, :] - p[xi, here, :],
                p[xi + 1, base + 1 : base + 9, :] - p[xi + 1, base - 1 : base + 7, :],
                above(mid, last) - below(mid, first),
            )
            for c in range(3):
                new = v[c, xi + 1, here, :] - 0.5 * slopes[c]
                out[c, xi, tile * 8 - 8 : tile * 8, :] = new
                if sums is not None:
                    if tile == 1:
                        sd[c * XI + xi] = new
                    if tile == 4:
                        su[c * XI + xi] = new
        return carry

    rows("correct", correct)
    if sums is not None:
        band_sums(out, su, sd, bands)


def step_scratch():
    return [
        pltpu.VMEM((4, XI + 2, PAD, LANES), F32),
        pltpu.VMEM((3, XI + 2, PAD, LANES), F32),
        pltpu.VMEM((XI, EXT, LANES), F32),
        pltpu.VMEM((XI + 2, PAD, LANES), F32),
        pltpu.VMEM((XI + 2, PAD, LANES), F32),
        pltpu.VMEM((2, XI, EXT, LANES), F32),
        pltpu.VMEM((2, XI, LANES), F32),
        pltpu.VMEM((4, EXT, LANES), F32),
    ]


def send_kernel(scal, fields, s0, s1, s2, s3, turned):
    own = scal[0]

    def per_row(xi, carry):
        stacked = jnp.concatenate([fields[c, xi] for c in range(4)], axis=0)
        turned[...] = stacked.T.reshape(GX, 4, 8, LANES)
        for s, out in enumerate((s0, s1, s2, s3)):
            out[pl.ds(xi * 4, 4)] = turned[own ^ s]
        return carry

    lax.fori_loop(0, XI, per_row, 0)


def final_kernel(scal, mean, s0, r1, r2, r3, out, columns, *, cells):
    own, slab = scal[0], scal[1]
    du, dw = mean_response(mean[0:1, :] * F32(1.0 / cells))
    pad = jnp.zeros((LANES - 2 * XI, LANES), F32)
    columns[...] = jnp.concatenate([du, dw, pad], axis=0).T
    own_columns = columns[pl.ds(pl.multiple_of(own * NZ, NZ), NZ), :]
    group = lanes() >> 5
    masks = [group == (slab ^ s) for s in range(4)]
    for x in range(XI):
        for kt in range(4):
            sources = [ref[x * 4 + kt] for ref in (s0, r1, r2, r3)]
            for c in range(4):
                value = None
                for s, source in enumerate(sources):
                    moved = pltpu.roll(source, (((slab ^ s) - c) & 3) * 32, axis=1)
                    value = moved if value is None else jnp.where(masks[s], moved, value)
                if c in (0, 2):
                    column = (0 if c == 0 else XI) + x
                    value = value + own_columns[kt * 8 : kt * 8 + 8, column : column + 1]
                out[c, x, kt * 8 : kt * 8 + 8, :] = value


def ring(groups):
    place = []
    for j in range(groups):
        for b in range(GX):
            i = b ^ (3 * (j & 1))
            place.append(i * groups + j)
    size = len(place)
    up = [(place[s], place[(s + 1) % size]) for s in range(size)]
    return up, [(b, a) for a, b in up]


def swapped(value, axis, size, distance):
    return lax.ppermute(value, axis, [(i, i ^ distance) for i in range(size)])


def local(state, planes, turbine_cell, active, yaw_sector, slot, *, layouts, groups):
    gx_index, gy_index = lax.axis_index("gx"), lax.axis_index("gy")
    slab = gx_index ^ (3 * (gy_index & 1))
    scal = jnp.stack([gx_index, slab, lax.axis_index("layout")]).astype(jnp.int32)
    scal = jnp.concatenate([scal, slot, active[0], yaw_sector[0]])
    cells = float(GX * XI * GX * OWN * groups)
    per_layout = planes.shape[0]
    height = (jnp.arange(NZ).astype(F32) + 0.5) / NZ
    zeros = jnp.zeros((NZ,), F32)
    profile = jnp.tile(jnp.stack([height ** (1.0 / 7.0), zeros, zeros, 0.5 * height]), (1, GX))
    profile = jnp.pad(profile, ((0, 4), (0, 0)))
    up, down = ring(groups)
    gy_up = [(j, (j + 1) % groups) for j in range(groups)]
    gy_down = [(b, a) for a, b in gy_up]

    chunk = shape(TILES + 2, 8, LANES)
    s0, s1, s2, s3, plane = call(
        pack_kernel,
        (chunk, chunk, chunk, chunk, shape(per_layout * 4, 8, LANES)),
        [SMEM, VMEM, VMEM, VMEM],
        name="pack",
    )(scal, state[0], planes, turbine_cell[0, :, NZ // 2, :])
    received = [swapped(value, "gx", GX, s) for s, value in ((1, s1), (2, s2), (3, s3))]
    received[0], plane = lax.optimization_barrier((received[0], plane))
    plane_received = [swapped(plane, "layout", layouts, s) for s in range(1, layouts)]

    first_payload = shape(TILES + MORE + 4, 8, LANES)
    fields, inflow, su, sd, bands, sums, ids = call(
        functools.partial(unpack_kernel, layouts=layouts, per_layout=per_layout),
        (
            shape(4, XI, OWN, LANES),
            shape(4, OWN, LANES),
            first_payload,
            first_payload,
            shape(2, OWN, LANES),
            shape(8, LANES),
            shape(GX, XI, LANES),
        ),
        [SMEM, VMEM] + [VMEM] * (4 + layouts),
        [
            pltpu.VMEM((GX, TILES, 8, LANES), F32),
            pltpu.VMEM((layouts, per_layout * 4, 8, LANES), F32),
        ],
        name="unpack",
    )(scal, profile, s0, *received, plane, *plane_received)

    maps = call(maps_kernel, shape(4, 2 * OWN, LANES), [SMEM, VMEM, VMEM, VMEM], name="maps")(
        scal, ids, lax.ppermute(ids, "gy", gy_up), lax.ppermute(ids, "gy", gy_down)
    )

    half = groups // 2

    def last_round(value):
        return sum([swapped(value, "gy", groups, d) for d in range(1, half)], value)

    mean = pending = None
    for step in range(STEPS):
        partial = sums + swapped(sums, "gx", GX, 1)
        su, sd, partial = lax.optimization_barrier((su, sd, partial))
        lo = lax.ppermute(su, ("gx", "gy"), up)
        hi = lax.ppermute(sd, ("gx", "gy"), down)
        if pending is not None:
            mean = last_round(pending)
        partial = partial + swapped(partial, "gy", groups, half)
        fields, partial = lax.optimization_barrier((fields, partial))
        arriving = swapped(partial, "gx", GX, 2)
        outs = [shape(4, XI, OWN, LANES)]
        if step < STEPS - 1:
            payload = shape(TILES + MORE, 8, LANES)
            outs += [payload, payload, shape(2, OWN, LANES), shape(8, LANES)]
        if step == 0:
            outs += [shape(4, EXT, LANES)]
        operands = [fields, lo, hi, maps, bands, inflow] + ([mean] if step > 0 else [])
        results = call(
            functools.partial(step_kernel, step=step, cells=cells),
            tuple(outs),
            [VMEM] * len(operands),
            step_scratch(),
            flops=6_000_000_000,
            name="step%d" % step,
        )(*operands)
        results = list(results)
        fields = results.pop(0)
        if step < STEPS - 1:
            su, sd, bands, sums = results[:4]
            del results[:4]
        if step == 0:
            inflow = results.pop(0)
        fields, arriving = lax.optimization_barrier((fields, arriving))
        pending = partial + arriving
    mean = last_round(pending)

    chunk = shape(TILES, 8, LANES)
    s0, s1, s2, s3 = call(
        send_kernel,
        (chunk, chunk, chunk, chunk),
        [SMEM, VMEM],
        [pltpu.VMEM((GX, 4, 8, LANES), F32)],
        name="send",
    )(scal, fields)
    received = [swapped(value, "gx", GX, s) for s, value in ((1, s1), (2, s2), (3, s3))]
    fields = call(
        functools.partial(final_kernel, cells=cells),
        shape(4, XI, NZ, LANES),
        [SMEM, VMEM] + [VMEM] * 4,
        [pltpu.VMEM((LANES, LANES), F32)],
        name="final",
    )(scal, mean, s0, *received)
    return fields[None]


def solution(mesh):
    body = functools.partial(local, layouts=mesh.shape["layout"], groups=mesh.shape["gy"])
    return jax.shard_map(
        body,
        mesh=mesh,
        in_specs=(
            P("layout", None, "gx", None, "gy"),
            P("layout", None, None, "gy"),
            P("layout", "gx", None, "gy"),
            P("layout", None),
            P("layout", None),
            P(),
        ),
        out_specs=P("layout", None, "gx", None, "gy"),
        check_vma=False,
    )
```

```python
import functools
import math

import jax
import jax.numpy as jnp
from jax import lax
from jax.experimental import pallas as pl
from jax.experimental.pallas import tpu as pltpu
from jax.sharding import PartitionSpec as P

STEPS = 4
SWEEPS = 4
RADIUS = 5
NZ = 32
XI = 16
GX = 4
OWN = 32
HALO = 8
EXT = OWN + 2 * HALO
PAD = EXT + 16
LANES = 128
WIDTH = 2 * RADIUS + 1
LOWEST = NZ // 2 - RADIUS
TILES = 4 * XI
MORE = 4
UNROLL = {"fill": 4, "tend": 4, "div": 16, "relax": 16, "correct": 16}

TIME_STEP = 0.25
VISCOSITY = 0.02
SMAGORINSKY = 0.0289
DIFFUSIVITY_RATIO = 1.0 / 0.7
BUOYANCY = 0.5
THRUST_COEFF = 1.33
YAW_INCREMENT = 0.1
SIXTH = 1.0 / 6.0
F32 = jnp.float32
INTS = 7
VLIMIT = 40 * 1024 * 1024

VMEM = pl.BlockSpec(memory_space=pltpu.VMEM)
SMEM = pl.BlockSpec(memory_space=pltpu.SMEM)


def shape(*dims):
    return jax.ShapeDtypeStruct(dims, F32)


def lanes(rows=8):
    return lax.broadcasted_iota(jnp.int32, (rows, LANES), 1)


def level_masks(rows=8):
    level = lanes(rows) & (NZ - 1)
    return level == 0, level == NZ - 1


def below(f, first):
    return jnp.where(first, f, pltpu.roll(f, 1, axis=1))


def above(f, last):
    return jnp.where(last, f, pltpu.roll(f, LANES - 1, axis=1))


def call(kernel, out_shape, in_specs, scratch=(), flops=2_000_000_000, **kwargs):
    return pl.pallas_call(
        kernel,
        out_shape=out_shape,
        in_specs=in_specs,
        out_specs=jax.tree.map(lambda _: VMEM, out_shape),
        scratch_shapes=list(scratch),
        compiler_params=pltpu.CompilerParams(vmem_limit_bytes=VLIMIT),
        cost_estimate=pl.CostEstimate(flops=flops, bytes_accessed=4_000_000, transcendentals=0),
        **kwargs,
    )


def rows(name, body, carry=0):
    count = UNROLL[name]

    def some(index, carry):
        for offset in range(count):
            carry = body(index * count + offset, carry)
        return carry

    return lax.fori_loop(0, XI // count, some, carry)


def group_matrix(banded):
    row = lax.broadcasted_iota(jnp.int32, (LANES, LANES), 0)
    column = lax.broadcasted_iota(jnp.int32, (LANES, LANES), 1)
    level = (row if banded == "row" else column) & (NZ - 1)
    inside = (level >= LOWEST) & (level < LOWEST + WIDTH)
    return jnp.where(((row >> 5) == (column >> 5)) & inside, 1.0, 0.0).astype(F32)


def exact_dot(a, b):
    return jnp.dot(a, b, precision=lax.Precision.HIGHEST, preferred_element_type=F32)


def band_sums(fields, su, sd, sums):
    matrix = group_matrix("row")
    level = lanes(OWN) & (NZ - 1)
    for c in range(2):
        total = exact_dot(fields[c].reshape(XI * OWN, LANES), matrix)
        packed = jnp.zeros((OWN, LANES), F32)
        for xi in range(XI):
            packed = jnp.where(level == xi, total[xi * OWN : (xi + 1) * OWN], packed)
        sums[c] = packed
        for t in range(2):
            sd[TILES + 2 * c + t] = packed[t * 8 : t * 8 + 8]
            su[TILES + 2 * c + t] = packed[16 + t * 8 : 24 + t * 8]


def block_transposed(sources, group, masks):
    out = None
    for c, value in enumerate(sources):
        moved = pltpu.roll(value, ((c - group) & 3) * 32, axis=1)
        out = moved if out is None else jnp.where(masks[c], moved, out)
    return out


def pack_kernel(scal, state, planes, ids, s0, s1, s2, s3, pl_out):
    slab = scal[1]
    group = lanes() >> 5
    masks = [group == c for c in range(4)]

    def per_row(x, carry):
        for kt in range(4):
            sources = [state[c, x, kt * 8 : kt * 8 + 8, :] for c in range(4)]
            for s, out in enumerate((s0, s1, s2, s3)):
                out[x * 4 + kt] = block_transposed(sources, slab ^ s, masks)
        return carry

    rows("fill", per_row)
    for half in range(6):
        for out in (s0, s1, s2, s3):
            out[TILES + half] = ids[half // 2, (half % 2) * 8 : (half % 2) * 8 + 8]
    for plane in range(planes.shape[0]):
        for kt in range(4):
            sources = [planes[plane, c, kt * 8 : kt * 8 + 8, :] for c in range(4)]
            pl_out[plane * 4 + kt] = block_transposed(sources, slab, masks)


def maps_kernel(ints, ids, maps):
    slab = ints[1]
    lane = lanes(NZ)
    pieces = []
    for g in range(GX):
        moved_mid = pltpu.roll(ids[0, g], (16 - 32 * slab) & (LANES - 1), axis=1)
        moved_left = pltpu.roll(ids[1, g], 16, axis=1)
        moved_right = pltpu.roll(ids[2, g], OWN + 16, axis=1)
        here = jnp.where((lane[:XI] < 16) & (slab == 0), moved_left, moved_mid)
        here = jnp.where((lane[:XI] >= OWN + 16) & (slab == 3), moved_right, here)
        pieces += [here, jnp.full((XI, LANES), -1.0, F32)]
    here = jnp.concatenate(pieces, axis=0)
    turbines = (ints.shape[0] - INTS) // 2

    def per_turbine(t, carry):
        sector, running = carry
        match = here == t.astype(F32)
        return (
            jnp.where(match, ints[INTS + turbines + t].astype(F32), sector),
            jnp.where(match, ints[INTS + t].astype(F32), running),
        )

    sector, running = lax.fori_loop(
        0, turbines, per_turbine, (jnp.full((LANES, LANES), -1.0, F32), jnp.zeros((LANES, LANES), F32))
    )
    cosine = jnp.zeros((LANES, LANES), F32)
    sine = jnp.zeros((LANES, LANES), F32)
    for value in range(8):
        angle = (value - 3.5) * YAW_INCREMENT
        cosine = jnp.where(sector == value, F32(math.cos(angle)), cosine)
        sine = jnp.where(sector == value, F32(math.sin(angle)), sine)
    thrust = running * F32(-0.5 * THRUST_COEFF * TIME_STEP / float(WIDTH**2) ** 2)
    low = lanes(LANES) < 64
    first = jnp.where(low, here, pltpu.roll(thrust, 64, axis=1)).T
    second = jnp.where(low, cosine, pltpu.roll(sine, 64, axis=1)).T
    maps[0], maps[3] = first[:64], first[64:]
    maps[1], maps[2] = second[:64], second[64:]


def over_groups(row):
    row = row + pltpu.roll(row, 64, axis=1)
    return row + pltpu.roll(row, 32, axis=1)


def unpack_kernel(
    scal, profile, s0, r1, r2, r3, p0, *rest, layouts, per_layout
):
    plane_refs = (p0,) + rest[: layouts - 1]
    fields, inflow, su, sd, bands, sums, ids, held, planes = rest[layouts - 1 :]
    own, here = scal[0], scal[2]
    for s, source in enumerate((s0, r1, r2, r3)):
        held[own ^ s] = source[:TILES]
        for half in range(6):
            ids[half // 2, own ^ s, (half % 2) * 8 : (half % 2) * 8 + 8, :] = source[TILES + half]
    for s, source in enumerate(plane_refs):
        planes[here ^ s] = source[...]

    def per_row(xi, total):
        parts = [held[g, pl.ds(xi * 4, 4)].reshape(NZ, LANES) for g in range(GX)]
        turned = jnp.concatenate(parts, axis=0).T
        for c in range(4):
            value = turned[c * 32 : c * 32 + 32] + profile[c : c + 1, :]
            fields[c, xi] = value
            sd[c * XI + xi] = value[:HALO]
            su[c * XI + xi] = value[OWN - HALO :]
            if c == 3:
                total = total + jnp.sum(value, axis=0, keepdims=True)
        return total

    total = rows("fill", per_row, jnp.zeros((1, LANES), F32))
    sums[...] = jnp.broadcast_to(over_groups(total), (8, LANES))
    parts = []
    for step in range(STEPS):
        plane = scal[3 + step]
        parts.append(
            planes[plane // per_layout, pl.ds((plane % per_layout) * 4, 4)].reshape(NZ, LANES)
        )
    turned = jnp.concatenate(parts, axis=0).T
    for c in range(4):
        value = turned[c * 32 : c * 32 + 32] + profile[c : c + 1, :]
        inflow[c] = value
        sd[TILES + MORE + c] = value[:HALO]
        su[TILES + MORE + c] = value[OWN - HALO :]
    band_sums(fields, su, sd, bands)


def mean_response(mean):
    lane = lanes(XI)
    row = lax.broadcasted_iota(jnp.int32, (XI, LANES), 0)
    level = lane & (NZ - 1)
    first, last = level == 0, level == NZ - 1

    def x_pair(p):
        lower = pltpu.roll(p, 1, axis=0)
        edge = jnp.where(lane < 32, 0.0, pltpu.roll(lower, 32, axis=1))
        lower = jnp.where(row == 0, edge, lower)
        upper = pltpu.roll(p, XI - 1, axis=0)
        edge = jnp.where(lane >= 96, 0.0, pltpu.roll(upper, 96, axis=1))
        upper = jnp.where(row == XI - 1, edge, upper)
        return lower, upper

    vertical = jnp.broadcast_to(mean, (XI, LANES)) * F32(-TIME_STEP * BUOYANCY)
    up = jnp.where(last, 0.0, pltpu.roll(vertical, LANES - 1, axis=1))
    down = jnp.where(first, 0.0, pltpu.roll(vertical, 1, axis=1))
    source = (up - down) * 0.5
    p = source * F32(-SIXTH)
    for sweep in range(SWEEPS):
        lower, upper = x_pair(p)
        p = (lower + upper + 2.0 * p + above(p, last) + below(p, first) - source) * F32(SIXTH)
    lower, upper = x_pair(p)
    return (upper - lower) * -0.5, vertical - (above(p, last) - below(p, first)) * 0.5


def step_kernel(*refs, step, cells):
    refs = list(refs)
    fields_in, lo, hi, maps, bands_in, inflow_in = refs[:6]
    del refs[:6]
    mean = None
    if step > 0:
        mean = refs.pop(0)
    out = refs.pop(0)
    su = sd = bands = sums = inflow_out = None
    if step < STEPS - 1:
        su, sd, bands, sums = refs[:4]
        del refs[:4]
    if step == 0:
        inflow_out = refs.pop(0)
    f, v, r, pa, pb, ns, change, inflow = refs
    first, last = level_masks()
    lane_ext = lanes(EXT)
    body = slice(8, 8 + EXT)

    if step > 0:
        du, dw = mean_response(mean[0:1, :] * F32(1.0 / cells))
        change[0] = du
        change[1] = dw
        inflow[...] = inflow_in[...]
    else:
        for c in range(4):
            inflow[c, 0:8] = lo[TILES + MORE + c]
            inflow[c, 8 : 8 + OWN] = inflow_in[c]
            inflow[c, 8 + OWN : EXT] = hi[TILES + MORE + c]
        inflow_out[...] = inflow[...]

    def fill(xi, carry):
        for c in range(4):
            low, mid, high = lo[c * XI + xi], fields_in[c, xi], hi[c * XI + xi]
            if step > 0 and c in (0, 2):
                d = change[c // 2, pl.ds(xi, 1), :]
                low, mid, high = low + d, mid + d, high + d
            f[c, xi + 1, 8:16] = low
            f[c, xi + 1, 16 : 16 + OWN] = mid
            f[c, xi + 1, 16 + OWN : 8 + EXT] = high
        return carry

    rows("fill", fill)
    shift = (LANES - 32 * step) % LANES

    def entry(c):
        value = inflow[c]
        return pltpu.roll(value, shift, axis=1) if shift else value

    for c in range(4):
        f[c, 0, body] = jnp.where(
            lane_ext < 32, entry(c), pltpu.roll(f[c, XI, body], 32, axis=1)
        )
        f[c, XI + 1, body] = jnp.where(
            lane_ext >= 96, f[c, XI, body], pltpu.roll(f[c, 1, body], 96, axis=1)
        )

    packed = []
    for c in range(2):
        parts = [lo[TILES + 2 * c + t] for t in range(2)] + [bands_in[c]]
        parts += [hi[TILES + 2 * c + t] for t in range(2)]
        packed.append(jnp.concatenate(parts, axis=0))
    if step > 0:
        level = lanes(XI) & (NZ - 1)
        row = lax.broadcasted_iota(jnp.int32, (XI, LANES), 0)
        shift_u = jnp.where(level == row, exact_dot(change[0], group_matrix("row")), 0.0)
        packed[0] = packed[0] + jnp.sum(shift_u, axis=0, keepdims=True)
    ident, cosine, sine = maps[0], maps[1], maps[2]
    speed = cosine * packed[0] + sine * packed[1]
    forward = backward = speed
    size = ident.shape[0]
    row = lax.broadcasted_iota(jnp.int32, ident.shape, 0)
    for d in (1, 2, 4, 8):
        same = (ident == pltpu.roll(ident, d, axis=0)) & (row >= d)
        forward = forward + jnp.where(same, pltpu.roll(forward, d, axis=0), 0.0)
        same = (ident == pltpu.roll(ident, size - d, axis=0)) & (row < size - d)
        backward = backward + jnp.where(same, pltpu.roll(backward, size - d, axis=0), 0.0)
    total = forward + backward - speed
    thrust = maps[3] * total * jnp.abs(total)
    level = lanes(EXT) & (NZ - 1)
    matrix = group_matrix("column")
    for c, direction in enumerate((cosine, sine)):
        pushed = (thrust * direction)[8 : 8 + EXT]
        for part in range(0, XI, 4):
            spread = [jnp.where(level == xi, pushed, 0.0) for xi in range(part, part + 4)]
            result = exact_dot(jnp.concatenate(spread, axis=0), matrix)
            ns[c, part : part + 4] = result.reshape(4, EXT, LANES)

    def tendencies(xi, total):
        for tile in range(EXT // 8):
            base = 8 + tile * 8
            centre, gx, gy, gz, lap = [], [], [], [], []
            for c in range(4):
                mid = f[c, xi + 1, base : base + 8, :]
                xm = f[c, xi, base : base + 8, :]
                xp = f[c, xi + 2, base : base + 8, :]
                ym = f[c, xi + 1, base - 1 : base + 7, :]
                yp = f[c, xi + 1, base + 1 : base + 9, :]
                if c == 2:
                    zm = jnp.where(first, 0.0, pltpu.roll(mid, 1, axis=1))
                    zp = jnp.where(last, 0.0, pltpu.roll(mid, LANES - 1, axis=1))
                else:
                    zm, zp = below(mid, first), above(mid, last)
                centre.append(mid)
                gx.append(xp - xm)
                gy.append(yp - ym)
                gz.append(zp - zm)
                lap.append((xp + xm) + (yp + ym) + (zp + zm) - 6.0 * mid)
            s_xy = gy[0] + gx[1]
            s_xz = gz[0] + gx[2]
            s_yz = gz[1] + gy[2]
            strain = jnp.sqrt(
                2.0 * (gx[0] * gx[0] + gy[1] * gy[1] + gz[2] * gz[2])
                + (s_xy * s_xy + s_xz * s_xz + s_yz * s_yz)
            )
            nu = F32(TIME_STEP * VISCOSITY) + F32(0.5 * TIME_STEP * SMAGORINSKY) * strain
            half = F32(0.5 * TIME_STEP)
            au, av, aw = half * centre[0], half * centre[1], half * centre[2]
            for c in range(4):
                scale = nu * F32(DIFFUSIVITY_RATIO) if c == 3 else nu
                new = centre[c] + (scale * lap[c] - (au * gx[c] + av * gy[c] + aw * gz[c]))
                if c < 2:
                    new = new + ns[c, xi, tile * 8 : tile * 8 + 8, :]
                elif c == 2:
                    new = new + F32(TIME_STEP * BUOYANCY) * centre[3]
                if c < 3:
                    v[c, xi + 1, base : base + 8, :] = new
                elif 1 <= tile <= 4:
                    out[3, xi, tile * 8 - 8 : tile * 8, :] = new
                    if sums is not None:
                        total = total + new
                        if tile == 1:
                            sd[3 * XI + xi] = new
                        if tile == 4:
                            su[3 * XI + xi] = new
        return total

    total = rows("tend", tendencies, jnp.zeros((8, LANES), F32))
    if sums is not None:
        total = over_groups(jnp.sum(total, axis=0, keepdims=True))
        sums[...] = jnp.broadcast_to(total, (8, LANES))

    v[0, 0, body] = jnp.where(lane_ext < 32, entry(0), pltpu.roll(v[0, XI, body], 32, axis=1))
    v[0, XI + 1, body] = jnp.where(
        lane_ext >= 96, v[0, XI, body], pltpu.roll(v[0, 1, body], 96, axis=1)
    )

    def divergence(xi, carry):
        for tile in range(EXT // 8):
            base = 8 + tile * 8
            here = slice(base, base + 8)
            w = v[2, xi + 1, here, :]
            up = jnp.where(last, 0.0, pltpu.roll(w, LANES - 1, axis=1))
            down = jnp.where(first, 0.0, pltpu.roll(w, 1, axis=1))
            total = (v[0, xi + 2, here, :] - v[0, xi, here, :]) + (up - down)
            total = total + (
                v[1, xi + 1, base + 1 : base + 9, :] - v[1, xi + 1, base - 1 : base + 7, :]
            )
            source = total * F32(0.5 * SIXTH)
            r[xi, tile * 8 : tile * 8 + 8, :] = source
            pa[xi + 1, here, :] = -source
        return carry

    rows("div", divergence)

    def ends(p):
        p[0, body] = jnp.where(lane_ext < 32, 0.0, pltpu.roll(p[XI, body], 32, axis=1))
        p[XI + 1, body] = jnp.where(lane_ext >= 96, 0.0, pltpu.roll(p[1, body], 96, axis=1))

    for sweep in range(SWEEPS):
        p, q = (pa, pb) if sweep % 2 == 0 else (pb, pa)
        ends(p)

        def relax(xi, carry, p=p, q=q):
            for tile in range(EXT // 8):
                base = 8 + tile * 8
                here = slice(base, base + 8)
                mid = p[xi + 1, here, :]
                beside = (p[xi, here, :] + p[xi + 2, here, :]) + (
                    p[xi + 1, base - 1 : base + 7, :] + p[xi + 1, base + 1 : base + 9, :]
                )
                beside = beside + (below(mid, first) + above(mid, last))
                q[xi + 1, here, :] = beside * F32(SIXTH) - r[xi, tile * 8 : tile * 8 + 8, :]
            return carry

        rows("relax", relax)
    p = pa if SWEEPS % 2 == 0 else pb
    ends(p)

    def correct(xi, carry):
        for tile in range(1, 5):
            base = 8 + tile * 8
            here = slice(base, base + 8)
            mid = p[xi + 1, here, :]
            slopes = (
                p[xi + 2, here, :] - p[xi, here, :],
                p[xi + 1, base + 1 : base + 9, :] - p[xi + 1, base - 1 : base + 7, :],
                above(mid, last) - below(mid, first),
            )
            for c in range(3):
                new = v[c, xi + 1, here, :] - 0.5 * slopes[c]
                out[c, xi, tile * 8 - 8 : tile * 8, :] = new
                if sums is not None:
                    if tile == 1:
                        sd[c * XI + xi] = new
                    if tile == 4:
                        su[c * XI + xi] = new
        return carry

    rows("correct", correct)
    if sums is not None:
        band_sums(out, su, sd, bands)


def step_scratch():
    return [
        pltpu.VMEM((4, XI + 2, PAD, LANES), F32),
        pltpu.VMEM((3, XI + 2, PAD, LANES), F32),
        pltpu.VMEM((XI, EXT, LANES), F32),
        pltpu.VMEM((XI + 2, PAD, LANES), F32),
        pltpu.VMEM((XI + 2, PAD, LANES), F32),
        pltpu.VMEM((2, XI, EXT, LANES), F32),
        pltpu.VMEM((2, XI, LANES), F32),
        pltpu.VMEM((4, EXT, LANES), F32),
    ]


def send_kernel(scal, fields, s0, s1, s2, s3, turned):
    own = scal[0]

    def per_row(xi, carry):
        stacked = jnp.concatenate([fields[c, xi] for c in range(4)], axis=0)
        turned[...] = stacked.T.reshape(GX, 4, 8, LANES)
        for s, out in enumerate((s0, s1, s2, s3)):
            out[pl.ds(xi * 4, 4)] = turned[own ^ s]
        return carry

    lax.fori_loop(0, XI, per_row, 0)


def final_kernel(scal, mean, s0, r1, r2, r3, out, columns, *, cells):
    own, slab = scal[0], scal[1]
    du, dw = mean_response(mean[0:1, :] * F32(1.0 / cells))
    pad = jnp.zeros((LANES - 2 * XI, LANES), F32)
    columns[...] = jnp.concatenate([du, dw, pad], axis=0).T
    own_columns = columns[pl.ds(pl.multiple_of(own * NZ, NZ), NZ), :]
    group = lanes() >> 5
    masks = [group == (slab ^ s) for s in range(4)]
    for x in range(XI):
        for kt in range(4):
            sources = [ref[x * 4 + kt] for ref in (s0, r1, r2, r3)]
            for c in range(4):
                value = None
                for s, source in enumerate(sources):
                    moved = pltpu.roll(source, (((slab ^ s) - c) & 3) * 32, axis=1)
                    value = moved if value is None else jnp.where(masks[s], moved, value)
                if c in (0, 2):
                    column = (0 if c == 0 else XI) + x
                    value = value + own_columns[kt * 8 : kt * 8 + 8, column : column + 1]
                out[c, x, kt * 8 : kt * 8 + 8, :] = value


def ring(groups):
    place = []
    for j in range(groups):
        for b in range(GX):
            i = b ^ (3 * (j & 1))
            place.append(i * groups + j)
    size = len(place)
    up = [(place[s], place[(s + 1) % size]) for s in range(size)]
    return up, [(b, a) for a, b in up]


def swapped(value, axis, size, distance):
    return lax.ppermute(value, axis, [(i, i ^ distance) for i in range(size)])


def local(state, planes, turbine_cell, active, yaw_sector, slot, *, layouts, groups):
    gx_index, gy_index = lax.axis_index("gx"), lax.axis_index("gy")
    slab = gx_index ^ (3 * (gy_index & 1))
    scal = jnp.stack([gx_index, slab, lax.axis_index("layout")]).astype(jnp.int32)
    scal = jnp.concatenate([scal, slot, active[0], yaw_sector[0]])
    cells = float(GX * XI * GX * OWN * groups)
    per_layout = planes.shape[0]
    height = (jnp.arange(NZ).astype(F32) + 0.5) / NZ
    zeros = jnp.zeros((NZ,), F32)
    profile = jnp.tile(jnp.stack([height ** (1.0 / 7.0), zeros, zeros, 0.5 * height]), (1, GX))
    profile = jnp.pad(profile, ((0, 4), (0, 0)))
    up, down = ring(groups)
    gy_up = [(j, (j + 1) % groups) for j in range(groups)]
    gy_down = [(b, a) for a, b in gy_up]

    ids = turbine_cell[0, :, NZ // 2, :].astype(F32)
    ids = jnp.stack([ids, lax.ppermute(ids, "gy", gy_up), lax.ppermute(ids, "gy", gy_down)])
    chunk = shape(TILES + 6, 8, LANES)
    s0, s1, s2, s3, plane = call(
        pack_kernel,
        (chunk, chunk, chunk, chunk, shape(per_layout * 4, 8, LANES)),
        [SMEM, VMEM, VMEM, VMEM],
        name="pack",
    )(scal, state[0], planes, ids)
    received = [swapped(value, "gx", GX, s) for s, value in ((1, s1), (2, s2), (3, s3))]
    received[0], plane = lax.optimization_barrier((received[0], plane))
    plane_received = [swapped(plane, "layout", layouts, s) for s in range(1, layouts)]

    first_payload = shape(TILES + MORE + 4, 8, LANES)
    fields, inflow, su, sd, bands, sums, ids = call(
        functools.partial(unpack_kernel, layouts=layouts, per_layout=per_layout),
        (
            shape(4, XI, OWN, LANES),
            shape(4, OWN, LANES),
            first_payload,
            first_payload,
            shape(2, OWN, LANES),
            shape(8, LANES),
            shape(3, GX, XI, LANES),
        ),
        [SMEM, VMEM] + [VMEM] * (4 + layouts),
        [
            pltpu.VMEM((GX, TILES, 8, LANES), F32),
            pltpu.VMEM((layouts, per_layout * 4, 8, LANES), F32),
        ],
        name="unpack",
    )(scal, profile, s0, *received, plane, *plane_received)

    maps = call(maps_kernel, shape(4, 2 * OWN, LANES), [SMEM, VMEM], name="maps")(scal, ids)

    half = groups // 2

    def last_round(value):
        return sum([swapped(value, "gy", groups, d) for d in range(1, half)], value)

    mean = pending = None
    for step in range(STEPS):
        partial = sums + swapped(sums, "gx", GX, 1)
        su, sd, partial = lax.optimization_barrier((su, sd, partial))
        lo = lax.ppermute(su, ("gx", "gy"), up)
        hi = lax.ppermute(sd, ("gx", "gy"), down)
        if pending is not None:
            mean = last_round(pending)
        partial = partial + swapped(partial, "gy", groups, half)
        fields, partial = lax.optimization_barrier((fields, partial))
        arriving = swapped(partial, "gx", GX, 2)
        outs = [shape(4, XI, OWN, LANES)]
        if step < STEPS - 1:
            payload = shape(TILES + MORE, 8, LANES)
            outs += [payload, payload, shape(2, OWN, LANES), shape(8, LANES)]
        if step == 0:
            outs += [shape(4, EXT, LANES)]
        operands = [fields, lo, hi, maps, bands, inflow] + ([mean] if step > 0 else [])
        results = call(
            functools.partial(step_kernel, step=step, cells=cells),
            tuple(outs),
            [VMEM] * len(operands),
            step_scratch(),
            flops=6_000_000_000,
            name="step%d" % step,
        )(*operands)
        results = list(results)
        fields = results.pop(0)
        if step < STEPS - 1:
            su, sd, bands, sums = results[:4]
            del results[:4]
        if step == 0:
            inflow = results.pop(0)
        su, sd, fields, arriving = lax.optimization_barrier((su, sd, fields, arriving))
        pending = partial + arriving
    mean = last_round(pending)

    chunk = shape(TILES, 8, LANES)
    s0, s1, s2, s3 = call(
        send_kernel,
        (chunk, chunk, chunk, chunk),
        [SMEM, VMEM],
        [pltpu.VMEM((GX, 4, 8, LANES), F32)],
        name="send",
    )(scal, fields)
    received = [swapped(value, "gx", GX, s) for s, value in ((1, s1), (2, s2), (3, s3))]
    fields = call(
        functools.partial(final_kernel, cells=cells),
        shape(4, XI, NZ, LANES),
        [SMEM, VMEM] + [VMEM] * 4,
        [pltpu.VMEM((LANES, LANES), F32)],
        name="final",
    )(scal, mean, s0, *received)
    return fields[None]


def solution(mesh):
    body = functools.partial(local, layouts=mesh.shape["layout"], groups=mesh.shape["gy"])
    return jax.shard_map(
        body,
        mesh=mesh,
        in_specs=(
            P("layout", None, "gx", None, "gy"),
            P("layout", None, None, "gy"),
            P("layout", "gx", None, "gy"),
            P("layout", None),
            P("layout", None),
            P(),
        ),
        out_specs=P("layout", None, "gx", None, "gy"),
        check_vma=False,
    )
```

```python
import functools
import math

import jax
import jax.numpy as jnp
from jax import lax
from jax.experimental import pallas as pl
from jax.experimental.pallas import tpu as pltpu
from jax.sharding import PartitionSpec as P

STEPS = 4
SWEEPS = 4
RADIUS = 5
NZ = 32
XI = 16
GX = 4
OWN = 32
WIDE, NARROW = 24, 8
DEEP = WIDE // 8
LANES = 128
WIDTH = 2 * RADIUS + 1
LOWEST = NZ // 2 - RADIUS
TILES = 4 * XI * DEEP
MORE = 2 * OWN // 8
CHUNK = 4 * XI
UNROLL = {"fill": 4, "tend": 4, "div": 16, "relax": 16, "correct": 16}

TIME_STEP = 0.25
VISCOSITY = 0.02
SMAGORINSKY = 0.0289
DIFFUSIVITY_RATIO = 1.0 / 0.7
BUOYANCY = 0.5
THRUST_COEFF = 1.33
YAW_INCREMENT = 0.1
SIXTH = 1.0 / 6.0
F32 = jnp.float32
INTS = 7
VLIMIT = 40 * 1024 * 1024

VMEM = pl.BlockSpec(memory_space=pltpu.VMEM)
SMEM = pl.BlockSpec(memory_space=pltpu.SMEM)


def shape(*dims):
    return jax.ShapeDtypeStruct(dims, F32)


def lanes(rows=8):
    return lax.broadcasted_iota(jnp.int32, (rows, LANES), 1)


def level_masks(rows=8):
    level = lanes(rows) & (NZ - 1)
    return level == 0, level == NZ - 1


def below(f, first):
    return jnp.where(first, f, pltpu.roll(f, 1, axis=1))


def above(f, last):
    return jnp.where(last, f, pltpu.roll(f, LANES - 1, axis=1))


def call(kernel, out_shape, in_specs, scratch=(), flops=2_000_000_000, **kwargs):
    return pl.pallas_call(
        kernel,
        out_shape=out_shape,
        in_specs=in_specs,
        out_specs=jax.tree.map(lambda _: VMEM, out_shape),
        scratch_shapes=list(scratch),
        compiler_params=pltpu.CompilerParams(vmem_limit_bytes=VLIMIT),
        cost_estimate=pl.CostEstimate(flops=flops, bytes_accessed=4_000_000, transcendentals=0),
        **kwargs,
    )


def rows(name, body, carry=0):
    count = UNROLL[name]

    def some(index, carry):
        for offset in range(count):
            carry = body(index * count + offset, carry)
        return carry

    return lax.fori_loop(0, XI // count, some, carry)


def group_matrix(banded):
    row = lax.broadcasted_iota(jnp.int32, (LANES, LANES), 0)
    column = lax.broadcasted_iota(jnp.int32, (LANES, LANES), 1)
    level = (row if banded == "row" else column) & (NZ - 1)
    inside = (level >= LOWEST) & (level < LOWEST + WIDTH)
    return jnp.where(((row >> 5) == (column >> 5)) & inside, 1.0, 0.0).astype(F32)


def exact_dot(a, b):
    return jnp.dot(a, b, precision=lax.Precision.HIGHEST, preferred_element_type=F32)


def band_sums(fields, sums, sent=()):
    matrix = group_matrix("row")
    count = sums.shape[1]
    level = lanes(count) & (NZ - 1)
    for c in range(2):
        total = exact_dot(fields[c].reshape(XI * count, LANES), matrix)
        packed = jnp.zeros((count, LANES), F32)
        for xi in range(XI):
            packed = jnp.where(level == xi, total[xi * count : (xi + 1) * count], packed)
        sums[c] = packed
        for t in range(OWN // 8):
            for out in sent:
                out[TILES + c * (OWN // 8) + t] = packed[t * 8 : t * 8 + 8]


def send_tile(su, sd, index, tile, value):
    if tile < DEEP:
        sd[index * DEEP + tile] = value
    if tile >= OWN // 8 - DEEP:
        su[index * DEEP + tile - (OWN // 8 - DEEP)] = value


def block_transposed(sources, group, masks):
    out = None
    for c, value in enumerate(sources):
        moved = pltpu.roll(value, ((c - group) & 3) * 32, axis=1)
        out = moved if out is None else jnp.where(masks[c], moved, out)
    return out


def pack_kernel(scal, state, planes, ids, s0, s1, s2, s3, pl_out):
    slab = scal[1]
    group = lanes() >> 5
    masks = [group == c for c in range(4)]

    def per_row(x, carry):
        for kt in range(4):
            sources = [state[c, x, kt * 8 : kt * 8 + 8, :] for c in range(4)]
            for s, out in enumerate((s0, s1, s2, s3)):
                out[x * 4 + kt] = block_transposed(sources, slab ^ s, masks)
        return carry

    rows("fill", per_row)
    for half in range(6):
        for out in (s0, s1, s2, s3):
            out[CHUNK + half] = ids[half // 2, (half % 2) * 8 : (half % 2) * 8 + 8]
    for plane in range(planes.shape[0]):
        for kt in range(4):
            sources = [planes[plane, c, kt * 8 : kt * 8 + 8, :] for c in range(4)]
            pl_out[plane * 4 + kt] = block_transposed(sources, slab, masks)


def maps_kernel(ints, ids, maps):
    slab = ints[1]
    lane = lanes(NZ)
    pieces = []
    for g in range(GX):
        moved_mid = pltpu.roll(ids[0, g], (32 - 32 * slab) & (LANES - 1), axis=1)
        moved_left = pltpu.roll(ids[1, g], OWN, axis=1)
        moved_right = pltpu.roll(ids[2, g], 2 * OWN, axis=1)
        here = jnp.where((lane[:XI] < OWN) & (slab == 0), moved_left, moved_mid)
        here = jnp.where((lane[:XI] >= 2 * OWN) & (slab == 3), moved_right, here)
        pieces += [here, jnp.full((XI, LANES), -1.0, F32)]
    here = jnp.concatenate(pieces, axis=0)
    turbines = (ints.shape[0] - INTS) // 2

    def per_turbine(t, carry):
        sector, running = carry
        match = here == t.astype(F32)
        return (
            jnp.where(match, ints[INTS + turbines + t].astype(F32), sector),
            jnp.where(match, ints[INTS + t].astype(F32), running),
        )

    sector, running = lax.fori_loop(
        0, turbines, per_turbine, (jnp.full((LANES, LANES), -1.0, F32), jnp.zeros((LANES, LANES), F32))
    )
    cosine = jnp.zeros((LANES, LANES), F32)
    sine = jnp.zeros((LANES, LANES), F32)
    for value in range(8):
        angle = (value - 3.5) * YAW_INCREMENT
        cosine = jnp.where(sector == value, F32(math.cos(angle)), cosine)
        sine = jnp.where(sector == value, F32(math.sin(angle)), sine)
    thrust = running * F32(-0.5 * THRUST_COEFF * TIME_STEP / float(WIDTH**2) ** 2)
    for which, value in enumerate((here, cosine, sine, thrust)):
        maps[which] = value.T[: 3 * OWN]


def over_groups(row):
    row = row + pltpu.roll(row, 64, axis=1)
    return row + pltpu.roll(row, 32, axis=1)


def unpack_kernel(
    scal, profile, s0, r1, r2, r3, p0, *rest, layouts, per_layout
):
    plane_refs = (p0,) + rest[: layouts - 1]
    fields, inflow, su, sd, bands, sums, ids, held, planes = rest[layouts - 1 :]
    own, here = scal[0], scal[2]
    for s, source in enumerate((s0, r1, r2, r3)):
        held[own ^ s] = source[:CHUNK]
        for half in range(6):
            ids[half // 2, own ^ s, (half % 2) * 8 : (half % 2) * 8 + 8, :] = source[CHUNK + half]
    for s, source in enumerate(plane_refs):
        planes[here ^ s] = source[...]

    def per_row(xi, total):
        parts = [held[g, pl.ds(xi * 4, 4)].reshape(NZ, LANES) for g in range(GX)]
        turned = jnp.concatenate(parts, axis=0).T
        for c in range(4):
            value = turned[c * 32 : c * 32 + 32] + profile[c : c + 1, :]
            fields[c, xi] = value
            for t in range(OWN // 8):
                send_tile(su, sd, c * XI + xi, t, value[t * 8 : t * 8 + 8])
            if c == 3:
                total = total + jnp.sum(value, axis=0, keepdims=True)
        return total

    total = rows("fill", per_row, jnp.zeros((1, LANES), F32))
    sums[...] = jnp.broadcast_to(over_groups(total), (8, LANES))
    parts = []
    for step in range(STEPS):
        plane = scal[3 + step]
        parts.append(
            planes[plane // per_layout, pl.ds((plane % per_layout) * 4, 4)].reshape(NZ, LANES)
        )
    turned = jnp.concatenate(parts, axis=0).T
    for c in range(4):
        value = turned[c * 32 : c * 32 + 32] + profile[c : c + 1, :]
        inflow[c] = value
        for t in range(OWN // 8):
            send_tile(su, sd, 4 * XI + MORE // DEEP + 1 + c, t, value[t * 8 : t * 8 + 8])
    band_sums(fields, bands, (su, sd))


def mean_response(mean):
    lane = lanes(XI)
    row = lax.broadcasted_iota(jnp.int32, (XI, LANES), 0)
    level = lane & (NZ - 1)
    first, last = level == 0, level == NZ - 1

    def x_pair(p):
        lower = pltpu.roll(p, 1, axis=0)
        edge = jnp.where(lane < 32, 0.0, pltpu.roll(lower, 32, axis=1))
        lower = jnp.where(row == 0, edge, lower)
        upper = pltpu.roll(p, XI - 1, axis=0)
        edge = jnp.where(lane >= 96, 0.0, pltpu.roll(upper, 96, axis=1))
        upper = jnp.where(row == XI - 1, edge, upper)
        return lower, upper

    vertical = jnp.broadcast_to(mean, (XI, LANES)) * F32(-TIME_STEP * BUOYANCY)
    up = jnp.where(last, 0.0, pltpu.roll(vertical, LANES - 1, axis=1))
    down = jnp.where(first, 0.0, pltpu.roll(vertical, 1, axis=1))
    source = (up - down) * 0.5
    p = source * F32(-SIXTH)
    for sweep in range(SWEEPS):
        lower, upper = x_pair(p)
        p = (lower + upper + 2.0 * p + above(p, last) + below(p, first) - source) * F32(SIXTH)
    lower, upper = x_pair(p)
    return (upper - lower) * -0.5, vertical - (above(p, last) - below(p, first)) * 0.5


def step_kernel(*refs, step, cells):
    refs = list(refs)
    wide = step % 2 == 0
    halo = WIDE if wide else NARROW
    kept = NARROW if wide else 0
    ext = OWN + 2 * halo
    pad = ext + 16
    tiles = ext // 8
    own_tiles = range(halo // 8, halo // 8 + OWN // 8)
    kept_tiles = range((halo - kept) // 8, (halo + OWN + kept) // 8)
    band_tiles = range(1, tiles - 1) if wide else kept_tiles
    fields_in, maps, bands_in, inflow_in = refs[:4]
    del refs[:4]
    lo = hi = mean = None
    if wide:
        lo, hi = refs[:2]
        del refs[:2]
    if step > 0:
        mean = refs.pop(0)
    out = refs.pop(0)
    su = sd = bands = sums = inflow_out = wind = None
    if step < STEPS - 1:
        bands, sums = refs[:2]
        del refs[:2]
        if not wide:
            su, sd = refs[:2]
            del refs[:2]
    if step == 0:
        inflow_out = refs.pop(0)
    f, v, r, pa, pb, ns, change, inflow = refs[:8]
    if wide:
        wind = refs[8]
    first, last = level_masks()
    lane_ext = lanes(ext)
    body = slice(8, 8 + ext)

    if step > 0:
        row = 1 if step == STEPS - 1 else 0
        du, dw = mean_response(mean[row : row + 1, :] * F32(1.0 / cells))
        change[0] = du
        change[1] = dw
        inflow[...] = inflow_in[...] if wide else inflow_in[:, WIDE - NARROW : WIDE + OWN + NARROW]
    else:
        for c in range(4):
            for t in range(DEEP):
                base = TILES + MORE + 1 + c * DEEP
                inflow[c, t * 8 : t * 8 + 8] = lo[base + t]
                inflow[c, WIDE + OWN + t * 8 : WIDE + OWN + t * 8 + 8] = hi[base + t]
            inflow[c, WIDE : WIDE + OWN] = inflow_in[c]
        inflow_out[...] = inflow[...]

    def fill(xi, carry):
        for c in range(4):
            d = change[c // 2, pl.ds(xi, 1), :] if step > 0 and c in (0, 2) else None
            if wide:
                index = (c * XI + xi) * DEEP
                parts = [lo[pl.ds(index, DEEP)].reshape(WIDE, LANES), fields_in[c, xi]]
                parts.append(hi[pl.ds(index, DEEP)].reshape(WIDE, LANES))
            else:
                parts = [fields_in[c, xi]]
            at = 8
            for part in parts:
                f[c, xi + 1, at : at + part.shape[0]] = part if d is None else part + d
                at += part.shape[0]
        return carry

    rows("fill", fill)
    shift = (LANES - 32 * step) % LANES

    def entry(c):
        value = inflow[c]
        return pltpu.roll(value, shift, axis=1) if shift else value

    for c in range(4):
        f[c, 0, body] = jnp.where(
            lane_ext < 32, entry(c), pltpu.roll(f[c, XI, body], 32, axis=1)
        )
        f[c, XI + 1, body] = jnp.where(
            lane_ext >= 96, f[c, XI, body], pltpu.roll(f[c, 1, body], 96, axis=1)
        )

    packed = []
    for c in range(2):
        if wide:
            near = slice(TILES + c * (OWN // 8), TILES + (c + 1) * (OWN // 8))
            parts = [lo[near].reshape(OWN, LANES), bands_in[c], hi[near].reshape(OWN, LANES)]
            packed.append(jnp.concatenate(parts, axis=0))
        else:
            packed.append(bands_in[c])
    if step > 0:
        level = lanes(XI) & (NZ - 1)
        row = lax.broadcasted_iota(jnp.int32, (XI, LANES), 0)
        shift_u = jnp.where(level == row, exact_dot(change[0], group_matrix("row")), 0.0)
        packed[0] = packed[0] + jnp.sum(shift_u, axis=0, keepdims=True)
    size = ext + 16
    span = slice(OWN - halo - 8, OWN - halo - 8 + size)
    ident, cosine, sine, factor = (maps[which, span, :] for which in range(4))
    speed = cosine * packed[0] + sine * packed[1]
    forward = backward = speed
    row = lax.broadcasted_iota(jnp.int32, ident.shape, 0)
    for d in (1, 2, 4, 8):
        same = (ident == pltpu.roll(ident, d, axis=0)) & (row >= d)
        forward = forward + jnp.where(same, pltpu.roll(forward, d, axis=0), 0.0)
        same = (ident == pltpu.roll(ident, size - d, axis=0)) & (row < size - d)
        backward = backward + jnp.where(same, pltpu.roll(backward, size - d, axis=0), 0.0)
    total = forward + backward - speed
    thrust = factor * total * jnp.abs(total)
    level = lanes(ext) & (NZ - 1)
    matrix = group_matrix("column")
    for c, direction in enumerate((cosine, sine)):
        pushed = (thrust * direction)[8 : 8 + ext]
        for part in range(0, XI, 4):
            spread = [jnp.where(level == xi, pushed, 0.0) for xi in range(part, part + 4)]
            result = exact_dot(jnp.concatenate(spread, axis=0), matrix)
            ns[c, part : part + 4] = result.reshape(4, ext, LANES)

    def tendencies(xi, total):
        for tile in range(tiles):
            base = 8 + tile * 8
            centre, gx, gy, gz, lap = [], [], [], [], []
            for c in range(4):
                mid = f[c, xi + 1, base : base + 8, :]
                if c == 3 and tile not in kept_tiles:
                    centre.append(mid)
                    continue
                xm = f[c, xi, base : base + 8, :]
                xp = f[c, xi + 2, base : base + 8, :]
                ym = f[c, xi + 1, base - 1 : base + 7, :]
                yp = f[c, xi + 1, base + 1 : base + 9, :]
                if c == 2:
                    zm = jnp.where(first, 0.0, pltpu.roll(mid, 1, axis=1))
                    zp = jnp.where(last, 0.0, pltpu.roll(mid, LANES - 1, axis=1))
                else:
                    zm, zp = below(mid, first), above(mid, last)
                centre.append(mid)
                gx.append(xp - xm)
                gy.append(yp - ym)
                gz.append(zp - zm)
                lap.append((xp + xm) + (yp + ym) + (zp + zm) - 6.0 * mid)
            s_xy = gy[0] + gx[1]
            s_xz = gz[0] + gx[2]
            s_yz = gz[1] + gy[2]
            strain = jnp.sqrt(
                2.0 * (gx[0] * gx[0] + gy[1] * gy[1] + gz[2] * gz[2])
                + (s_xy * s_xy + s_xz * s_xz + s_yz * s_yz)
            )
            nu = F32(TIME_STEP * VISCOSITY) + F32(0.5 * TIME_STEP * SMAGORINSKY) * strain
            half = F32(0.5 * TIME_STEP)
            au, av, aw = half * centre[0], half * centre[1], half * centre[2]
            for c in range(4 if tile in kept_tiles else 3):
                scale = nu * F32(DIFFUSIVITY_RATIO) if c == 3 else nu
                new = centre[c] + (scale * lap[c] - (au * gx[c] + av * gy[c] + aw * gz[c]))
                if c < 2:
                    new = new + ns[c, xi, tile * 8 : tile * 8 + 8, :]
                elif c == 2:
                    new = new + F32(TIME_STEP * BUOYANCY) * centre[3]
                if c < 3:
                    v[c, xi + 1, base : base + 8, :] = new
                else:
                    at = (tile - kept_tiles[0]) * 8
                    out[3, xi, at : at + 8, :] = new
                    if sums is not None and tile in own_tiles:
                        total = total + new
                        if su is not None:
                            send_tile(su, sd, 3 * XI + xi, tile - own_tiles[0], new)
        return total

    total = rows("tend", tendencies, jnp.zeros((8, LANES), F32))
    if sums is not None:
        total = over_groups(jnp.sum(total, axis=0, keepdims=True))
        sums[...] = jnp.broadcast_to(total, (8, LANES))

    v[0, 0, body] = jnp.where(lane_ext < 32, entry(0), pltpu.roll(v[0, XI, body], 32, axis=1))
    v[0, XI + 1, body] = jnp.where(
        lane_ext >= 96, v[0, XI, body], pltpu.roll(v[0, 1, body], 96, axis=1)
    )

    def divergence(xi, carry):
        for tile in range(tiles):
            base = 8 + tile * 8
            here = slice(base, base + 8)
            w = v[2, xi + 1, here, :]
            up = jnp.where(last, 0.0, pltpu.roll(w, LANES - 1, axis=1))
            down = jnp.where(first, 0.0, pltpu.roll(w, 1, axis=1))
            total = (v[0, xi + 2, here, :] - v[0, xi, here, :]) + (up - down)
            total = total + (
                v[1, xi + 1, base + 1 : base + 9, :] - v[1, xi + 1, base - 1 : base + 7, :]
            )
            source = total * F32(0.5 * SIXTH)
            r[xi, tile * 8 : tile * 8 + 8, :] = source
            pa[xi + 1, here, :] = -source
        return carry

    rows("div", divergence)

    def ends(p):
        p[0, body] = jnp.where(lane_ext < 32, 0.0, pltpu.roll(p[XI, body], 32, axis=1))
        p[XI + 1, body] = jnp.where(lane_ext >= 96, 0.0, pltpu.roll(p[1, body], 96, axis=1))

    for sweep in range(SWEEPS):
        p, q = (pa, pb) if sweep % 2 == 0 else (pb, pa)
        ends(p)

        def relax(xi, carry, p=p, q=q):
            for tile in range(tiles):
                base = 8 + tile * 8
                here = slice(base, base + 8)
                mid = p[xi + 1, here, :]
                beside = (p[xi, here, :] + p[xi + 2, here, :]) + (
                    p[xi + 1, base - 1 : base + 7, :] + p[xi + 1, base + 1 : base + 9, :]
                )
                beside = beside + (below(mid, first) + above(mid, last))
                q[xi + 1, here, :] = beside * F32(SIXTH) - r[xi, tile * 8 : tile * 8 + 8, :]
            return carry

        rows("relax", relax)
    p = pa if SWEEPS % 2 == 0 else pb
    ends(p)

    def correct(xi, carry):
        for tile in band_tiles:
            base = 8 + tile * 8
            here = slice(base, base + 8)
            mid = p[xi + 1, here, :]
            slopes = (
                p[xi + 2, here, :] - p[xi, here, :],
                p[xi + 1, base + 1 : base + 9, :] - p[xi + 1, base - 1 : base + 7, :],
                above(mid, last) - below(mid, first) if tile in kept_tiles else None,
            )
            for c in range(3 if tile in kept_tiles else 2):
                new = v[c, xi + 1, here, :] - 0.5 * slopes[c]
                if wide and c < 2:
                    wind[c, xi, tile * 8 - 8 : tile * 8, :] = new
                if tile in kept_tiles:
                    at = (tile - kept_tiles[0]) * 8
                    out[c, xi, at : at + 8, :] = new
                if su is not None and tile in own_tiles:
                    send_tile(su, sd, c * XI + xi, tile - own_tiles[0], new)
        return carry

    rows("correct", correct)
    if bands is not None:
        band_sums(wind if wide else out, bands, () if wide else (su, sd))


def step_scratch(step):
    wide = step % 2 == 0
    ext = OWN + 2 * (WIDE if wide else NARROW)
    pad = ext + 16
    scratch = [
        pltpu.VMEM((4, XI + 2, pad, LANES), F32),
        pltpu.VMEM((3, XI + 2, pad, LANES), F32),
        pltpu.VMEM((XI, ext, LANES), F32),
        pltpu.VMEM((XI + 2, pad, LANES), F32),
        pltpu.VMEM((XI + 2, pad, LANES), F32),
        pltpu.VMEM((2, XI, ext, LANES), F32),
        pltpu.VMEM((2, XI, LANES), F32),
        pltpu.VMEM((4, ext, LANES), F32),
    ]
    return scratch + ([pltpu.VMEM((2, XI, ext - 16, LANES), F32)] if wide else [])


def send_kernel(scal, fields, s0, s1, s2, s3, turned):
    own = scal[0]

    def per_row(xi, carry):
        stacked = jnp.concatenate([fields[c, xi] for c in range(4)], axis=0)
        turned[...] = stacked.T.reshape(GX, 4, 8, LANES)
        for s, out in enumerate((s0, s1, s2, s3)):
            out[pl.ds(xi * 4, 4)] = turned[own ^ s]
        return carry

    lax.fori_loop(0, XI, per_row, 0)


def final_kernel(scal, mean, s0, r1, r2, r3, out, columns, *, cells):
    own, slab = scal[0], scal[1]
    du, dw = mean_response(mean[0:1, :] * F32(1.0 / cells))
    pad = jnp.zeros((LANES - 2 * XI, LANES), F32)
    columns[...] = jnp.concatenate([du, dw, pad], axis=0).T
    own_columns = columns[pl.ds(pl.multiple_of(own * NZ, NZ), NZ), :]
    group = lanes() >> 5
    masks = [group == (slab ^ s) for s in range(4)]
    for x in range(XI):
        for kt in range(4):
            sources = [ref[x * 4 + kt] for ref in (s0, r1, r2, r3)]
            for c in range(4):
                value = None
                for s, source in enumerate(sources):
                    moved = pltpu.roll(source, (((slab ^ s) - c) & 3) * 32, axis=1)
                    value = moved if value is None else jnp.where(masks[s], moved, value)
                if c in (0, 2):
                    column = (0 if c == 0 else XI) + x
                    value = value + own_columns[kt * 8 : kt * 8 + 8, column : column + 1]
                out[c, x, kt * 8 : kt * 8 + 8, :] = value


def ring(groups):
    place = []
    for j in range(groups):
        for b in range(GX):
            i = b ^ (3 * (j & 1))
            place.append(i * groups + j)
    size = len(place)
    up = [(place[s], place[(s + 1) % size]) for s in range(size)]
    return up, [(b, a) for a, b in up]


def swapped(value, axis, size, distance):
    return lax.ppermute(value, axis, [(i, i ^ distance) for i in range(size)])


def local(state, planes, turbine_cell, active, yaw_sector, slot, *, layouts, groups):
    gx_index, gy_index = lax.axis_index("gx"), lax.axis_index("gy")
    slab = gx_index ^ (3 * (gy_index & 1))
    scal = jnp.stack([gx_index, slab, lax.axis_index("layout")]).astype(jnp.int32)
    scal = jnp.concatenate([scal, slot, active[0], yaw_sector[0]])
    cells = float(GX * XI * GX * OWN * groups)
    per_layout = planes.shape[0]
    height = (jnp.arange(NZ).astype(F32) + 0.5) / NZ
    zeros = jnp.zeros((NZ,), F32)
    profile = jnp.tile(jnp.stack([height ** (1.0 / 7.0), zeros, zeros, 0.5 * height]), (1, GX))
    profile = jnp.pad(profile, ((0, 4), (0, 0)))
    up, down = ring(groups)
    gy_up = [(j, (j + 1) % groups) for j in range(groups)]
    gy_down = [(b, a) for a, b in gy_up]

    ids = turbine_cell[0, :, NZ // 2, :].astype(F32)
    ids = jnp.stack([ids, lax.ppermute(ids, "gy", gy_up), lax.ppermute(ids, "gy", gy_down)])
    chunk = shape(CHUNK + 6, 8, LANES)
    s0, s1, s2, s3, plane = call(
        pack_kernel,
        (chunk, chunk, chunk, chunk, shape(per_layout * 4, 8, LANES)),
        [SMEM, VMEM, VMEM, VMEM],
        name="pack",
    )(scal, state[0], planes, ids)
    received = [swapped(value, "gx", GX, s) for s, value in ((1, s1), (2, s2), (3, s3))]
    received[0], plane = lax.optimization_barrier((received[0], plane))
    plane_received = [swapped(plane, "layout", layouts, s) for s in range(1, layouts)]

    first_payload = shape(TILES + MORE + 1 + 4 * DEEP, 8, LANES)
    fields, inflow, su, sd, bands, sums, ids = call(
        functools.partial(unpack_kernel, layouts=layouts, per_layout=per_layout),
        (
            shape(4, XI, OWN, LANES),
            shape(4, OWN, LANES),
            first_payload,
            first_payload,
            shape(2, OWN, LANES),
            shape(8, LANES),
            shape(3, GX, XI, LANES),
        ),
        [SMEM, VMEM] + [VMEM] * (4 + layouts),
        [
            pltpu.VMEM((GX, CHUNK, 8, LANES), F32),
            pltpu.VMEM((layouts, per_layout * 4, 8, LANES), F32),
        ],
        name="unpack",
    )(scal, profile, s0, *received, plane, *plane_received)

    maps = call(maps_kernel, shape(4, 3 * OWN, LANES), [SMEM, VMEM], name="maps")(scal, ids)

    half = groups // 2

    def among_x(value):
        return sum([swapped(value, "gy", groups, d) for d in range(1, half)], value)

    def run(step, operands):
        wide = step % 2 == 0
        outs = [shape(4, XI, OWN + 2 * (NARROW if wide else 0), LANES)]
        if step < STEPS - 1:
            outs += [shape(2, 2 * OWN if wide else OWN, LANES), shape(8, LANES)]
            if not wide:
                outs += [shape(TILES + MORE, 8, LANES), shape(TILES + MORE, 8, LANES)]
        if step == 0:
            outs += [shape(4, OWN + 2 * WIDE, LANES)]
        return call(
            functools.partial(step_kernel, step=step, cells=cells),
            tuple(outs) if len(outs) > 1 else outs[0],
            [VMEM] * len(operands),
            step_scratch(step),
            flops=6_000_000_000,
            name="step%d" % step,
        )(*operands)

    def exchange(su, sd, fields, value):
        value = value + swapped(value, "gx", GX, 1)
        su, sd, value = lax.optimization_barrier((su, sd, value))
        lo = lax.ppermute(su, ("gx", "gy"), up)
        hi = lax.ppermute(sd, ("gx", "gy"), down)
        value = among_x(value + swapped(value, "gy", groups, half))
        fields, value = lax.optimization_barrier((fields, value))
        return lo, hi, fields, value, swapped(value, "gx", GX, 2)

    lo, hi, fields, partial, arriving = exchange(su, sd, fields, sums)
    fields, bands, sums, inflow = run(0, [fields, maps, bands, inflow, lo, hi])
    fields, arriving = lax.optimization_barrier((fields, arriving))
    early = swapped(sums, "gx", GX, 2)
    fields, bands, late, su, sd = run(1, [fields, maps, bands, inflow, partial + arriving])
    su, sd, fields, early = lax.optimization_barrier((su, sd, fields, early))
    is_early = lax.broadcasted_iota(jnp.int32, (8, LANES), 0) == 0
    both = jnp.where(is_early, sums + early, late)
    lo, hi, fields, partial, arriving = exchange(su, sd, fields, both)
    fields, bands, sums = run(2, [fields, maps, bands, inflow, lo, hi, partial])
    fields, arriving = lax.optimization_barrier((fields, arriving))
    early = swapped(sums, "gx", GX, 2)
    fields = run(3, [fields, maps, bands, inflow, partial + arriving])
    fields, early = lax.optimization_barrier((fields, early))
    mean = sums + early
    mean = among_x(mean + swapped(mean, "gx", GX, 1))
    mean = mean + swapped(mean, "gy", groups, half)

    chunk = shape(CHUNK, 8, LANES)
    s0, s1, s2, s3 = call(
        send_kernel,
        (chunk, chunk, chunk, chunk),
        [SMEM, VMEM],
        [pltpu.VMEM((GX, 4, 8, LANES), F32)],
        name="send",
    )(scal, fields)
    received = [swapped(value, "gx", GX, s) for s, value in ((1, s1), (2, s2), (3, s3))]
    fields = call(
        functools.partial(final_kernel, cells=cells),
        shape(4, XI, NZ, LANES),
        [SMEM, VMEM] + [VMEM] * 4,
        [pltpu.VMEM((LANES, LANES), F32)],
        name="final",
    )(scal, mean, s0, *received)
    return fields[None]


def solution(mesh):
    body = functools.partial(local, layouts=mesh.shape["layout"], groups=mesh.shape["gy"])
    return jax.shard_map(
        body,
        mesh=mesh,
        in_specs=(
            P("layout", None, "gx", None, "gy"),
            P("layout", None, None, "gy"),
            P("layout", "gx", None, "gy"),
            P("layout", None),
            P("layout", None),
            P(),
        ),
        out_specs=P("layout", None, "gx", None, "gy"),
        check_vma=False,
    )
```

```python
import functools
import math

import jax
import jax.numpy as jnp
from jax import lax
from jax.experimental import pallas as pl
from jax.experimental.pallas import tpu as pltpu
from jax.sharding import PartitionSpec as P

STEPS = 4
SWEEPS = 4
RADIUS = 5
NZ = 32
XI = 16
GX = 4
OWN = 32
HALO = 8
EXT = OWN + 2 * HALO
PAD = EXT + 16
LANES = 128
WIDTH = 2 * RADIUS + 1
LOWEST = NZ // 2 - RADIUS
TILES = 4 * XI
MORE = 4
UNROLL = {"fill": 4, "tend": 4, "div": 16, "relax": 16, "correct": 16}

TIME_STEP = 0.25
VISCOSITY = 0.02
SMAGORINSKY = 0.0289
DIFFUSIVITY_RATIO = 1.0 / 0.7
BUOYANCY = 0.5
THRUST_COEFF = 1.33
YAW_INCREMENT = 0.1
SIXTH = 1.0 / 6.0
F32 = jnp.float32
INTS = 7
VLIMIT = 40 * 1024 * 1024

VMEM = pl.BlockSpec(memory_space=pltpu.VMEM)
SMEM = pl.BlockSpec(memory_space=pltpu.SMEM)
HBM = pl.BlockSpec(memory_space=pltpu.HBM)


def shape(*dims):
    return jax.ShapeDtypeStruct(dims, F32)


def lanes(rows=8):
    return lax.broadcasted_iota(jnp.int32, (rows, LANES), 1)


def level_masks(rows=8):
    level = lanes(rows) & (NZ - 1)
    return level == 0, level == NZ - 1


def below(f, first):
    return jnp.where(first, f, pltpu.roll(f, 1, axis=1))


def above(f, last):
    return jnp.where(last, f, pltpu.roll(f, LANES - 1, axis=1))


def call(kernel, out_shape, in_specs, scratch=(), flops=2_000_000_000, **kwargs):
    return pl.pallas_call(
        kernel,
        out_shape=out_shape,
        in_specs=in_specs,
        out_specs=jax.tree.map(lambda _: VMEM, out_shape),
        scratch_shapes=list(scratch),
        compiler_params=pltpu.CompilerParams(vmem_limit_bytes=VLIMIT),
        cost_estimate=pl.CostEstimate(flops=flops, bytes_accessed=4_000_000, transcendentals=0),
        **kwargs,
    )


def rows(name, body, carry=0):
    count = UNROLL[name]

    def some(index, carry):
        for offset in range(count):
            carry = body(index * count + offset, carry)
        return carry

    return lax.fori_loop(0, XI // count, some, carry)


def group_matrix(banded):
    row = lax.broadcasted_iota(jnp.int32, (LANES, LANES), 0)
    column = lax.broadcasted_iota(jnp.int32, (LANES, LANES), 1)
    level = (row if banded == "row" else column) & (NZ - 1)
    inside = (level >= LOWEST) & (level < LOWEST + WIDTH)
    return jnp.where(((row >> 5) == (column >> 5)) & inside, 1.0, 0.0).astype(F32)


def exact_dot(a, b):
    return jnp.dot(a, b, precision=lax.Precision.HIGHEST, preferred_element_type=F32)


def band_sums(fields, su, sd, sums):
    matrix = group_matrix("row")
    level = lanes(OWN) & (NZ - 1)
    for c in range(2):
        total = exact_dot(fields[c].reshape(XI * OWN, LANES), matrix)
        packed = jnp.zeros((OWN, LANES), F32)
        for xi in range(XI):
            packed = jnp.where(level == xi, total[xi * OWN : (xi + 1) * OWN], packed)
        sums[c] = packed
        for t in range(2):
            sd[TILES + 2 * c + t] = packed[t * 8 : t * 8 + 8]
            su[TILES + 2 * c + t] = packed[16 + t * 8 : 24 + t * 8]


def block_transposed(sources, group, masks):
    out = None
    for c, value in enumerate(sources):
        moved = pltpu.roll(value, ((c - group) & 3) * 32, axis=1)
        out = moved if out is None else jnp.where(masks[c], moved, out)
    return out


def pack_kernel(
    scal, state, planes_in, ids, s0, s1, s2, s3, pl_out, sums, tile, planes, state_sems, plane_sem
):
    slab = scal[1]
    group = lanes() >> 5
    masks = [group == c for c in range(4)]
    copies = []
    for part in range(4):
        here = pl.ds(part * 4, 4)
        copies.append(
            pltpu.make_async_copy(state.at[:, here], tile.at[:, here], state_sems.at[part])
        )
        copies[-1].start()
    plane_copy = pltpu.make_async_copy(planes_in, planes, plane_sem)
    plane_copy.start()
    for half in range(6):
        for out in (s0, s1, s2, s3):
            out[TILES + half] = ids[half // 2, (half % 2) * 8 : (half % 2) * 8 + 8]
    total = jnp.zeros((NZ, LANES), F32)
    for part in range(4):
        copies[part].wait()
        for x in range(part * 4, part * 4 + 4):
            total = total + tile[3, x]
            for kt in range(4):
                sources = [tile[c, x, kt * 8 : kt * 8 + 8, :] for c in range(4)]
                for s, out in enumerate((s0, s1, s2, s3)):
                    out[x * 4 + kt] = block_transposed(sources, slab ^ s, masks)
    plane_copy.wait()
    for plane in range(planes.shape[0]):
        for kt in range(4):
            sources = [planes[plane, c, kt * 8 : kt * 8 + 8, :] for c in range(4)]
            pl_out[plane * 4 + kt] = block_transposed(sources, slab, masks)
    levels = jnp.concatenate([total] * GX, axis=0).T
    sums[...] = jnp.broadcast_to(jnp.sum(levels, axis=0, keepdims=True), (8, LANES))


def maps_kernel(ints, ids, maps):
    slab = ints[1]
    lane = lanes(NZ)
    pieces = []
    for g in range(GX):
        moved_mid = pltpu.roll(ids[0, g], (16 - 32 * slab) & (LANES - 1), axis=1)
        moved_left = pltpu.roll(ids[1, g], 16, axis=1)
        moved_right = pltpu.roll(ids[2, g], OWN + 16, axis=1)
        here = jnp.where((lane[:XI] < 16) & (slab == 0), moved_left, moved_mid)
        here = jnp.where((lane[:XI] >= OWN + 16) & (slab == 3), moved_right, here)
        pieces += [here, jnp.full((XI, LANES), -1.0, F32)]
    here = jnp.concatenate(pieces, axis=0)
    turbines = (ints.shape[0] - INTS) // 2

    def per_turbine(t, carry):
        sector, running = carry
        match = here == t.astype(F32)
        return (
            jnp.where(match, ints[INTS + turbines + t].astype(F32), sector),
            jnp.where(match, ints[INTS + t].astype(F32), running),
        )

    sector, running = lax.fori_loop(
        0, turbines, per_turbine, (jnp.full((LANES, LANES), -1.0, F32), jnp.zeros((LANES, LANES), F32))
    )
    cosine = jnp.zeros((LANES, LANES), F32)
    sine = jnp.zeros((LANES, LANES), F32)
    for value in range(8):
        angle = (value - 3.5) * YAW_INCREMENT
        cosine = jnp.where(sector == value, F32(math.cos(angle)), cosine)
        sine = jnp.where(sector == value, F32(math.sin(angle)), sine)
    thrust = running * F32(-0.5 * THRUST_COEFF * TIME_STEP / float(WIDTH**2) ** 2)
    low = lanes(LANES) < 64
    first = jnp.where(low, here, pltpu.roll(thrust, 64, axis=1)).T
    second = jnp.where(low, cosine, pltpu.roll(sine, 64, axis=1)).T
    maps[0], maps[3] = first[:64], first[64:]
    maps[1], maps[2] = second[:64], second[64:]


def over_groups(row):
    row = row + pltpu.roll(row, 64, axis=1)
    return row + pltpu.roll(row, 32, axis=1)


def unpack_kernel(
    scal, profile, s0, r1, r2, r3, p0, *rest, layouts, per_layout
):
    plane_refs = (p0,) + rest[: layouts - 1]
    fields, inflow, su, sd, bands, ids, held, planes = rest[layouts - 1 :]
    own, here = scal[0], scal[2]
    for s, source in enumerate((s0, r1, r2, r3)):
        held[own ^ s] = source[:TILES]
        for half in range(6):
            ids[half // 2, own ^ s, (half % 2) * 8 : (half % 2) * 8 + 8, :] = source[TILES + half]
    for s, source in enumerate(plane_refs):
        planes[here ^ s] = source[...]

    def per_row(xi, carry):
        parts = [held[g, pl.ds(xi * 4, 4)].reshape(NZ, LANES) for g in range(GX)]
        turned = jnp.concatenate(parts, axis=0).T
        for c in range(4):
            value = turned[c * 32 : c * 32 + 32] + profile[c : c + 1, :]
            fields[c, xi] = value
            sd[c * XI + xi] = value[:HALO]
            su[c * XI + xi] = value[OWN - HALO :]
        return carry

    rows("fill", per_row)
    parts = []
    for step in range(STEPS):
        plane = scal[3 + step]
        parts.append(
            planes[plane // per_layout, pl.ds((plane % per_layout) * 4, 4)].reshape(NZ, LANES)
        )
    turned = jnp.concatenate(parts, axis=0).T
    for c in range(4):
        value = turned[c * 32 : c * 32 + 32] + profile[c : c + 1, :]
        inflow[c] = value
        sd[TILES + MORE + c] = value[:HALO]
        su[TILES + MORE + c] = value[OWN - HALO :]
    band_sums(fields, su, sd, bands)


def mean_response(mean):
    lane = lanes(XI)
    row = lax.broadcasted_iota(jnp.int32, (XI, LANES), 0)
    level = lane & (NZ - 1)
    first, last = level == 0, level == NZ - 1

    def x_pair(p):
        lower = pltpu.roll(p, 1, axis=0)
        edge = jnp.where(lane < 32, 0.0, pltpu.roll(lower, 32, axis=1))
        lower = jnp.where(row == 0, edge, lower)
        upper = pltpu.roll(p, XI - 1, axis=0)
        edge = jnp.where(lane >= 96, 0.0, pltpu.roll(upper, 96, axis=1))
        upper = jnp.where(row == XI - 1, edge, upper)
        return lower, upper

    vertical = jnp.broadcast_to(mean, (XI, LANES)) * F32(-TIME_STEP * BUOYANCY)
    up = jnp.where(last, 0.0, pltpu.roll(vertical, LANES - 1, axis=1))
    down = jnp.where(first, 0.0, pltpu.roll(vertical, 1, axis=1))
    source = (up - down) * 0.5
    p = source * F32(-SIXTH)
    for sweep in range(SWEEPS):
        lower, upper = x_pair(p)
        p = (lower + upper + 2.0 * p + above(p, last) + below(p, first) - source) * F32(SIXTH)
    lower, upper = x_pair(p)
    return (upper - lower) * -0.5, vertical - (above(p, last) - below(p, first)) * 0.5


def step_kernel(*refs, step, cells):
    refs = list(refs)
    fields_in, lo, hi, maps, bands_in, inflow_in = refs[:6]
    del refs[:6]
    mean = None
    if step > 0:
        mean = refs.pop(0)
    out = refs.pop(0)
    su = sd = bands = sums = inflow_out = None
    if step < STEPS - 1:
        su, sd, bands, sums = refs[:4]
        del refs[:4]
    if step == 0:
        inflow_out = refs.pop(0)
    f, v, r, pa, pb, ns, change, inflow = refs
    first, last = level_masks()
    lane_ext = lanes(EXT)
    body = slice(8, 8 + EXT)

    if step > 0:
        du, dw = mean_response(mean[0:1, :] * F32(1.0 / cells))
        change[0] = du
        change[1] = dw
        inflow[...] = inflow_in[...]
    else:
        for c in range(4):
            inflow[c, 0:8] = lo[TILES + MORE + c]
            inflow[c, 8 : 8 + OWN] = inflow_in[c]
            inflow[c, 8 + OWN : EXT] = hi[TILES + MORE + c]
        inflow_out[...] = inflow[...]

    def fill(xi, carry):
        for c in range(4):
            low, mid, high = lo[c * XI + xi], fields_in[c, xi], hi[c * XI + xi]
            if step > 0 and c in (0, 2):
                d = change[c // 2, pl.ds(xi, 1), :]
                low, mid, high = low + d, mid + d, high + d
            f[c, xi + 1, 8:16] = low
            f[c, xi + 1, 16 : 16 + OWN] = mid
            f[c, xi + 1, 16 + OWN : 8 + EXT] = high
        return carry

    rows("fill", fill)
    shift = (LANES - 32 * step) % LANES

    def entry(c):
        value = inflow[c]
        return pltpu.roll(value, shift, axis=1) if shift else value

    for c in range(4):
        f[c, 0, body] = jnp.where(
            lane_ext < 32, entry(c), pltpu.roll(f[c, XI, body], 32, axis=1)
        )
        f[c, XI + 1, body] = jnp.where(
            lane_ext >= 96, f[c, XI, body], pltpu.roll(f[c, 1, body], 96, axis=1)
        )

    packed = []
    for c in range(2):
        parts = [lo[TILES + 2 * c + t] for t in range(2)] + [bands_in[c]]
        parts += [hi[TILES + 2 * c + t] for t in range(2)]
        packed.append(jnp.concatenate(parts, axis=0))
    if step > 0:
        level = lanes(XI) & (NZ - 1)
        row = lax.broadcasted_iota(jnp.int32, (XI, LANES), 0)
        shift_u = jnp.where(level == row, exact_dot(change[0], group_matrix("row")), 0.0)
        packed[0] = packed[0] + jnp.sum(shift_u, axis=0, keepdims=True)
    ident, cosine, sine = maps[0], maps[1], maps[2]
    speed = cosine * packed[0] + sine * packed[1]
    forward = backward = speed
    size = ident.shape[0]
    row = lax.broadcasted_iota(jnp.int32, ident.shape, 0)
    for d in (1, 2, 4, 8):
        same = (ident == pltpu.roll(ident, d, axis=0)) & (row >= d)
        forward = forward + jnp.where(same, pltpu.roll(forward, d, axis=0), 0.0)
        same = (ident == pltpu.roll(ident, size - d, axis=0)) & (row < size - d)
        backward = backward + jnp.where(same, pltpu.roll(backward, size - d, axis=0), 0.0)
    total = forward + backward - speed
    thrust = maps[3] * total * jnp.abs(total)
    level = lanes(EXT) & (NZ - 1)
    matrix = group_matrix("column")
    for c, direction in enumerate((cosine, sine)):
        pushed = (thrust * direction)[8 : 8 + EXT]
        for part in range(0, XI, 4):
            spread = [jnp.where(level == xi, pushed, 0.0) for xi in range(part, part + 4)]
            result = exact_dot(jnp.concatenate(spread, axis=0), matrix)
            ns[c, part : part + 4] = result.reshape(4, EXT, LANES)

    def tendencies(xi, total):
        for tile in range(EXT // 8):
            base = 8 + tile * 8
            centre, gx, gy, gz, lap = [], [], [], [], []
            for c in range(4):
                mid = f[c, xi + 1, base : base + 8, :]
                xm = f[c, xi, base : base + 8, :]
                xp = f[c, xi + 2, base : base + 8, :]
                ym = f[c, xi + 1, base - 1 : base + 7, :]
                yp = f[c, xi + 1, base + 1 : base + 9, :]
                if c == 2:
                    zm = jnp.where(first, 0.0, pltpu.roll(mid, 1, axis=1))
                    zp = jnp.where(last, 0.0, pltpu.roll(mid, LANES - 1, axis=1))
                else:
                    zm, zp = below(mid, first), above(mid, last)
                centre.append(mid)
                gx.append(xp - xm)
                gy.append(yp - ym)
                gz.append(zp - zm)
                lap.append((xp + xm) + (yp + ym) + (zp + zm) - 6.0 * mid)
            s_xy = gy[0] + gx[1]
            s_xz = gz[0] + gx[2]
            s_yz = gz[1] + gy[2]
            strain = jnp.sqrt(
                2.0 * (gx[0] * gx[0] + gy[1] * gy[1] + gz[2] * gz[2])
                + (s_xy * s_xy + s_xz * s_xz + s_yz * s_yz)
            )
            nu = F32(TIME_STEP * VISCOSITY) + F32(0.5 * TIME_STEP * SMAGORINSKY) * strain
            half = F32(0.5 * TIME_STEP)
            au, av, aw = half * centre[0], half * centre[1], half * centre[2]
            for c in range(4):
                scale = nu * F32(DIFFUSIVITY_RATIO) if c == 3 else nu
                new = centre[c] + (scale * lap[c] - (au * gx[c] + av * gy[c] + aw * gz[c]))
                if c < 2:
                    new = new + ns[c, xi, tile * 8 : tile * 8 + 8, :]
                elif c == 2:
                    new = new + F32(TIME_STEP * BUOYANCY) * centre[3]
                if c < 3:
                    v[c, xi + 1, base : base + 8, :] = new
                elif 1 <= tile <= 4:
                    out[3, xi, tile * 8 - 8 : tile * 8, :] = new
                    if sums is not None:
                        total = total + new
                        if tile == 1:
                            sd[3 * XI + xi] = new
                        if tile == 4:
                            su[3 * XI + xi] = new
        return total

    total = rows("tend", tendencies, jnp.zeros((8, LANES), F32))
    if sums is not None:
        total = over_groups(jnp.sum(total, axis=0, keepdims=True))
        sums[...] = jnp.broadcast_to(total, (8, LANES))

    v[0, 0, body] = jnp.where(lane_ext < 32, entry(0), pltpu.roll(v[0, XI, body], 32, axis=1))
    v[0, XI + 1, body] = jnp.where(
        lane_ext >= 96, v[0, XI, body], pltpu.roll(v[0, 1, body], 96, axis=1)
    )

    def divergence(xi, carry):
        for tile in range(EXT // 8):
            base = 8 + tile * 8
            here = slice(base, base + 8)
            w = v[2, xi + 1, here, :]
            up = jnp.where(last, 0.0, pltpu.roll(w, LANES - 1, axis=1))
            down = jnp.where(first, 0.0, pltpu.roll(w, 1, axis=1))
            total = (v[0, xi + 2, here, :] - v[0, xi, here, :]) + (up - down)
            total = total + (
                v[1, xi + 1, base + 1 : base + 9, :] - v[1, xi + 1, base - 1 : base + 7, :]
            )
            source = total * F32(0.5 * SIXTH)
            r[xi, tile * 8 : tile * 8 + 8, :] = source
            pa[xi + 1, here, :] = -source
        return carry

    rows("div", divergence)

    def ends(p):
        p[0, body] = jnp.where(lane_ext < 32, 0.0, pltpu.roll(p[XI, body], 32, axis=1))
        p[XI + 1, body] = jnp.where(lane_ext >= 96, 0.0, pltpu.roll(p[1, body], 96, axis=1))

    for sweep in range(SWEEPS):
        p, q = (pa, pb) if sweep % 2 == 0 else (pb, pa)
        ends(p)

        def relax(xi, carry, p=p, q=q):
            for tile in range(EXT // 8):
                base = 8 + tile * 8
                here = slice(base, base + 8)
                mid = p[xi + 1, here, :]
                beside = (p[xi, here, :] + p[xi + 2, here, :]) + (
                    p[xi + 1, base - 1 : base + 7, :] + p[xi + 1, base + 1 : base + 9, :]
                )
                beside = beside + (below(mid, first) + above(mid, last))
                q[xi + 1, here, :] = beside * F32(SIXTH) - r[xi, tile * 8 : tile * 8 + 8, :]
            return carry

        rows("relax", relax)
    p = pa if SWEEPS % 2 == 0 else pb
    ends(p)

    def correct(xi, carry):
        for tile in range(1, 5):
            base = 8 + tile * 8
            here = slice(base, base + 8)
            mid = p[xi + 1, here, :]
            slopes = (
                p[xi + 2, here, :] - p[xi, here, :],
                p[xi + 1, base + 1 : base + 9, :] - p[xi + 1, base - 1 : base + 7, :],
                above(mid, last) - below(mid, first),
            )
            for c in range(3):
                new = v[c, xi + 1, here, :] - 0.5 * slopes[c]
                out[c, xi, tile * 8 - 8 : tile * 8, :] = new
                if sums is not None:
                    if tile == 1:
                        sd[c * XI + xi] = new
                    if tile == 4:
                        su[c * XI + xi] = new
        return carry

    rows("correct", correct)
    if sums is not None:
        band_sums(out, su, sd, bands)


def step_scratch():
    return [
        pltpu.VMEM((4, XI + 2, PAD, LANES), F32),
        pltpu.VMEM((3, XI + 2, PAD, LANES), F32),
        pltpu.VMEM((XI, EXT, LANES), F32),
        pltpu.VMEM((XI + 2, PAD, LANES), F32),
        pltpu.VMEM((XI + 2, PAD, LANES), F32),
        pltpu.VMEM((2, XI, EXT, LANES), F32),
        pltpu.VMEM((2, XI, LANES), F32),
        pltpu.VMEM((4, EXT, LANES), F32),
    ]


def send_kernel(scal, fields, s0, s1, s2, s3, turned):
    own = scal[0]

    def per_row(xi, carry):
        stacked = jnp.concatenate([fields[c, xi] for c in range(4)], axis=0)
        turned[xi] = stacked.T.reshape(GX, 4, 8, LANES)
        for s, out in enumerate((s0, s1, s2, s3)):
            out[pl.ds(xi * 4, 4)] = turned[xi, own ^ s]
        return carry

    rows("fill", per_row)


def final_kernel(scal, mean, s0, r1, r2, r3, out, columns, *, cells):
    own, slab = scal[0], scal[1]
    du, dw = mean_response(mean[0:1, :] * F32(1.0 / cells))
    pad = jnp.zeros((LANES - 2 * XI, LANES), F32)
    columns[...] = jnp.concatenate([du, dw, pad], axis=0).T
    own_columns = columns[pl.ds(pl.multiple_of(own * NZ, NZ), NZ), :]
    group = lanes() >> 5
    masks = [group == (slab ^ s) for s in range(4)]
    for x in range(XI):
        for kt in range(4):
            sources = [ref[x * 4 + kt] for ref in (s0, r1, r2, r3)]
            for c in range(4):
                value = None
                for s, source in enumerate(sources):
                    moved = pltpu.roll(source, (((slab ^ s) - c) & 3) * 32, axis=1)
                    value = moved if value is None else jnp.where(masks[s], moved, value)
                if c in (0, 2):
                    column = (0 if c == 0 else XI) + x
                    value = value + own_columns[kt * 8 : kt * 8 + 8, column : column + 1]
                out[c, x, kt * 8 : kt * 8 + 8, :] = value


def ring(groups):
    place = []
    for j in range(groups):
        for b in range(GX):
            i = b ^ (3 * (j & 1))
            place.append(i * groups + j)
    size = len(place)
    up = [(place[s], place[(s + 1) % size]) for s in range(size)]
    return up, [(b, a) for a, b in up]


def swapped(value, axis, size, distance):
    return lax.ppermute(value, axis, [(i, i ^ distance) for i in range(size)])


def local(state, planes, turbine_cell, active, yaw_sector, slot, *, layouts, groups):
    gx_index, gy_index = lax.axis_index("gx"), lax.axis_index("gy")
    slab = gx_index ^ (3 * (gy_index & 1))
    scal = jnp.stack([gx_index, slab, lax.axis_index("layout")]).astype(jnp.int32)
    scal = jnp.concatenate([scal, slot, active[0], yaw_sector[0]])
    cells = float(GX * XI * GX * OWN * groups)
    per_layout = planes.shape[0]
    height = (jnp.arange(NZ).astype(F32) + 0.5) / NZ
    zeros = jnp.zeros((NZ,), F32)
    profile = jnp.tile(jnp.stack([height ** (1.0 / 7.0), zeros, zeros, 0.5 * height]), (1, GX))
    profile = jnp.pad(profile, ((0, 4), (0, 0)))
    up, down = ring(groups)
    gy_up = [(j, (j + 1) % groups) for j in range(groups)]
    gy_down = [(b, a) for a, b in gy_up]

    ids = turbine_cell[0, :, NZ // 2, :].astype(F32)
    ids = jnp.stack([ids, lax.ppermute(ids, "gy", gy_up), lax.ppermute(ids, "gy", gy_down)])
    chunk = shape(TILES + 6, 8, LANES)
    s0, s1, s2, s3, plane, sums = call(
        pack_kernel,
        (chunk, chunk, chunk, chunk, shape(per_layout * 4, 8, LANES), shape(8, LANES)),
        [SMEM, HBM, HBM, VMEM],
        [
            pltpu.VMEM((4, XI, NZ, LANES), F32),
            pltpu.VMEM((per_layout, 4, NZ, LANES), F32),
            pltpu.SemaphoreType.DMA((4,)),
            pltpu.SemaphoreType.DMA,
        ],
        name="pack",
    )(scal, state[0], planes, ids)
    received = [swapped(value, "gx", GX, s) for s, value in ((1, s1), (2, s2), (3, s3))]
    received[0], plane, sums = lax.optimization_barrier((received[0], plane, sums))
    plane_received = [swapped(plane, "layout", layouts, s) for s in range(1, layouts)]

    half = groups // 2

    def last_round(value):
        return sum([swapped(value, "gy", groups, d) for d in range(1, half)], value)

    partial = last_round(sums + swapped(sums, "gx", GX, 1))
    partial = partial + swapped(partial, "gy", groups, half)
    s0, partial = lax.optimization_barrier((s0, partial))
    arriving = swapped(partial, "gx", GX, 2)
    partial = partial + cells * profile[3:4]

    first_payload = shape(TILES + MORE + 4, 8, LANES)
    fields, inflow, su, sd, bands, ids = call(
        functools.partial(unpack_kernel, layouts=layouts, per_layout=per_layout),
        (
            shape(4, XI, OWN, LANES),
            shape(4, OWN, LANES),
            first_payload,
            first_payload,
            shape(2, OWN, LANES),
            shape(3, GX, XI, LANES),
        ),
        [SMEM, VMEM] + [VMEM] * (4 + layouts),
        [
            pltpu.VMEM((GX, TILES, 8, LANES), F32),
            pltpu.VMEM((layouts, per_layout * 4, 8, LANES), F32),
        ],
        name="unpack",
    )(scal, profile, s0, *received, plane, *plane_received)

    maps = call(maps_kernel, shape(4, 2 * OWN, LANES), [SMEM, VMEM], name="maps")(scal, ids)

    mean = pending = None
    for step in range(STEPS):
        if step > 0:
            partial = sums + swapped(sums, "gx", GX, 1)
            su, sd, partial = lax.optimization_barrier((su, sd, partial))
        lo = lax.ppermute(su, ("gx", "gy"), up)
        hi = lax.ppermute(sd, ("gx", "gy"), down)
        if step > 0:
            mean = last_round(pending) if step > 1 else pending
            partial = partial + swapped(partial, "gy", groups, half)
            fields, partial = lax.optimization_barrier((fields, partial))
            arriving = swapped(partial, "gx", GX, 2)
        outs = [shape(4, XI, OWN, LANES)]
        if step < STEPS - 1:
            payload = shape(TILES + MORE, 8, LANES)
            outs += [payload, payload, shape(2, OWN, LANES), shape(8, LANES)]
        if step == 0:
            outs += [shape(4, EXT, LANES)]
        operands = [fields, lo, hi, maps, bands, inflow] + ([mean] if step > 0 else [])
        results = call(
            functools.partial(step_kernel, step=step, cells=cells),
            tuple(outs),
            [VMEM] * len(operands),
            step_scratch(),
            flops=6_000_000_000,
            name="step%d" % step,
        )(*operands)
        results = list(results)
        fields = results.pop(0)
        if step < STEPS - 1:
            su, sd, bands, sums = results[:4]
            del results[:4]
        if step == 0:
            inflow = results.pop(0)
        su, sd, fields, arriving = lax.optimization_barrier((su, sd, fields, arriving))
        pending = partial + arriving
    mean = last_round(pending)

    chunk = shape(TILES, 8, LANES)
    s0, s1, s2, s3 = call(
        send_kernel,
        (chunk, chunk, chunk, chunk),
        [SMEM, VMEM],
        [pltpu.VMEM((XI, GX, 4, 8, LANES), F32)],
        name="send",
    )(scal, fields)
    received = [swapped(value, "gx", GX, s) for s, value in ((1, s1), (2, s2), (3, s3))]
    fields = call(
        functools.partial(final_kernel, cells=cells),
        shape(4, XI, NZ, LANES),
        [SMEM, VMEM] + [VMEM] * 4,
        [pltpu.VMEM((LANES, LANES), F32)],
        name="final",
    )(scal, mean, s0, *received)
    return fields[None]


def solution(mesh):
    body = functools.partial(local, layouts=mesh.shape["layout"], groups=mesh.shape["gy"])
    return jax.shard_map(
        body,
        mesh=mesh,
        in_specs=(
            P("layout", None, "gx", None, "gy"),
            P("layout", None, None, "gy"),
            P("layout", "gx", None, "gy"),
            P("layout", None),
            P("layout", None),
            P(),
        ),
        out_specs=P("layout", None, "gx", None, "gy"),
        check_vma=False,
    )
```

```python
import functools
import math

import jax
import jax.numpy as jnp
from jax import lax
from jax.experimental import pallas as pl
from jax.experimental.pallas import tpu as pltpu
from jax.sharding import PartitionSpec as P

STEPS = 4
SWEEPS = 4
RADIUS = 5
NZ = 32
XI = 16
GX = 4
OWN = 32
HALO = 8
EXT = OWN + 2 * HALO
PAD = EXT + 16
LANES = 128
WIDTH = 2 * RADIUS + 1
LOWEST = NZ // 2 - RADIUS
TILES = 4 * XI
MORE = 4
UNROLL = {"fill": 4, "tend": 4, "div": 16, "relax": 16, "correct": 16}

TIME_STEP = 0.25
VISCOSITY = 0.02
SMAGORINSKY = 0.0289
DIFFUSIVITY_RATIO = 1.0 / 0.7
BUOYANCY = 0.5
THRUST_COEFF = 1.33
YAW_INCREMENT = 0.1
SIXTH = 1.0 / 6.0
F32 = jnp.float32
INTS = 7
VLIMIT = 40 * 1024 * 1024

VMEM = pl.BlockSpec(memory_space=pltpu.VMEM)
SMEM = pl.BlockSpec(memory_space=pltpu.SMEM)


def shape(*dims):
    return jax.ShapeDtypeStruct(dims, F32)


def lanes(rows=8):
    return lax.broadcasted_iota(jnp.int32, (rows, LANES), 1)


def level_masks(rows=8):
    level = lanes(rows) & (NZ - 1)
    return level == 0, level == NZ - 1


def below(f, first):
    return jnp.where(first, f, pltpu.roll(f, 1, axis=1))


def above(f, last):
    return jnp.where(last, f, pltpu.roll(f, LANES - 1, axis=1))


def call(kernel, out_shape, in_specs, scratch=(), flops=2_000_000_000, **kwargs):
    return pl.pallas_call(
        kernel,
        out_shape=out_shape,
        in_specs=in_specs,
        out_specs=jax.tree.map(lambda _: VMEM, out_shape),
        scratch_shapes=list(scratch),
        compiler_params=pltpu.CompilerParams(vmem_limit_bytes=VLIMIT),
        cost_estimate=pl.CostEstimate(flops=flops, bytes_accessed=4_000_000, transcendentals=0),
        **kwargs,
    )


def rows(name, body, carry=0):
    count = UNROLL[name]

    def some(index, carry):
        for offset in range(count):
            carry = body(index * count + offset, carry)
        return carry

    return lax.fori_loop(0, XI // count, some, carry)


def group_matrix(banded):
    row = lax.broadcasted_iota(jnp.int32, (LANES, LANES), 0)
    column = lax.broadcasted_iota(jnp.int32, (LANES, LANES), 1)
    level = (row if banded == "row" else column) & (NZ - 1)
    inside = (level >= LOWEST) & (level < LOWEST + WIDTH)
    return jnp.where(((row >> 5) == (column >> 5)) & inside, 1.0, 0.0).astype(F32)


def exact_dot(a, b):
    return jnp.dot(a, b, precision=lax.Precision.HIGHEST, preferred_element_type=F32)


def band_sums(fields, su, sd, sums):
    matrix = group_matrix("row")
    level = lanes(OWN) & (NZ - 1)
    for c in range(2):
        total = exact_dot(fields[c].reshape(XI * OWN, LANES), matrix)
        packed = jnp.zeros((OWN, LANES), F32)
        for xi in range(XI):
            packed = jnp.where(level == xi, total[xi * OWN : (xi + 1) * OWN], packed)
        sums[c] = packed
        for t in range(2):
            sd[TILES + 2 * c + t] = packed[t * 8 : t * 8 + 8]
            su[TILES + 2 * c + t] = packed[16 + t * 8 : 24 + t * 8]


def block_transposed(sources, group, masks):
    out = None
    for c, value in enumerate(sources):
        moved = pltpu.roll(value, ((c - group) & 3) * 32, axis=1)
        out = moved if out is None else jnp.where(masks[c], moved, out)
    return out


def pack_kernel(scal, state, planes, ids, s0, s1, s2, s3, pl_out):
    slab = scal[1]
    group = lanes() >> 5
    masks = [group == c for c in range(4)]
    outs = (s0, s1, s2, s3)

    def per_row(x, total):
        for kt in range(4):
            sources = [state[c, x, kt * 8 : kt * 8 + 8, :] for c in range(4)]
            for s, out in enumerate(outs):
                out[x * 4 + kt] = block_transposed(sources, slab ^ s, masks)
        return total + state[3, x]

    total = rows("fill", per_row, jnp.zeros((NZ, LANES), F32))
    levels = jnp.concatenate([total] * GX, axis=0).T
    levels = jnp.broadcast_to(jnp.sum(levels, axis=0, keepdims=True), (8, LANES))
    for out in outs:
        for half in range(6):
            out[TILES + half] = ids[half // 2, (half % 2) * 8 : (half % 2) * 8 + 8]
        out[TILES + 6] = levels
    for plane in range(planes.shape[0]):
        for kt in range(4):
            sources = [planes[plane, c, kt * 8 : kt * 8 + 8, :] for c in range(4)]
            pl_out[plane * 4 + kt] = block_transposed(sources, slab, masks)


def maps_kernel(ints, ids, maps):
    slab = ints[1]
    lane = lanes(NZ)
    pieces = []
    for g in range(GX):
        moved_mid = pltpu.roll(ids[0, g], (16 - 32 * slab) & (LANES - 1), axis=1)
        moved_left = pltpu.roll(ids[1, g], 16, axis=1)
        moved_right = pltpu.roll(ids[2, g], OWN + 16, axis=1)
        here = jnp.where((lane[:XI] < 16) & (slab == 0), moved_left, moved_mid)
        here = jnp.where((lane[:XI] >= OWN + 16) & (slab == 3), moved_right, here)
        pieces += [here, jnp.full((XI, LANES), -1.0, F32)]
    here = jnp.concatenate(pieces, axis=0)
    turbines = (ints.shape[0] - INTS) // 2

    def per_turbine(t, carry):
        sector, running = carry
        match = here == t.astype(F32)
        return (
            jnp.where(match, ints[INTS + turbines + t].astype(F32), sector),
            jnp.where(match, ints[INTS + t].astype(F32), running),
        )

    sector, running = lax.fori_loop(
        0, turbines, per_turbine, (jnp.full((LANES, LANES), -1.0, F32), jnp.zeros((LANES, LANES), F32))
    )
    cosine = jnp.zeros((LANES, LANES), F32)
    sine = jnp.zeros((LANES, LANES), F32)
    for value in range(8):
        angle = (value - 3.5) * YAW_INCREMENT
        cosine = jnp.where(sector == value, F32(math.cos(angle)), cosine)
        sine = jnp.where(sector == value, F32(math.sin(angle)), sine)
    thrust = running * F32(-0.5 * THRUST_COEFF * TIME_STEP / float(WIDTH**2) ** 2)
    low = lanes(LANES) < 64
    first = jnp.where(low, here, pltpu.roll(thrust, 64, axis=1)).T
    second = jnp.where(low, cosine, pltpu.roll(sine, 64, axis=1)).T
    maps[0], maps[3] = first[:64], first[64:]
    maps[1], maps[2] = second[:64], second[64:]


def over_groups(row):
    row = row + pltpu.roll(row, 64, axis=1)
    return row + pltpu.roll(row, 32, axis=1)


def unpack_kernel(
    scal, profile, s0, r1, r2, r3, p0, *rest, layouts, per_layout
):
    plane_refs = (p0,) + rest[: layouts - 1]
    fields, inflow, su, sd, bands, sums, ids, held, planes = rest[layouts - 1 :]
    own, here = scal[0], scal[2]
    for s, source in enumerate((s0, r1, r2, r3)):
        held[own ^ s] = source[:TILES]
        for half in range(6):
            ids[half // 2, own ^ s, (half % 2) * 8 : (half % 2) * 8 + 8, :] = source[TILES + half]
    sums[...] = s0[TILES + 6] + r1[TILES + 6] + r2[TILES + 6] + r3[TILES + 6]
    for s, source in enumerate(plane_refs):
        planes[here ^ s] = source[...]

    def per_row(xi, carry):
        parts = [held[g, pl.ds(xi * 4, 4)].reshape(NZ, LANES) for g in range(GX)]
        turned = jnp.concatenate(parts, axis=0).T
        for c in range(4):
            value = turned[c * 32 : c * 32 + 32] + profile[c : c + 1, :]
            fields[c, xi] = value
            sd[c * XI + xi] = value[:HALO]
            su[c * XI + xi] = value[OWN - HALO :]
        return carry

    rows("fill", per_row)
    parts = []
    for step in range(STEPS):
        plane = scal[3 + step]
        parts.append(
            planes[plane // per_layout, pl.ds((plane % per_layout) * 4, 4)].reshape(NZ, LANES)
        )
    turned = jnp.concatenate(parts, axis=0).T
    for c in range(4):
        value = turned[c * 32 : c * 32 + 32] + profile[c : c + 1, :]
        inflow[c] = value
        sd[TILES + MORE + c] = value[:HALO]
        su[TILES + MORE + c] = value[OWN - HALO :]
    band_sums(fields, su, sd, bands)


def mean_response(mean):
    lane = lanes(XI)
    row = lax.broadcasted_iota(jnp.int32, (XI, LANES), 0)
    level = lane & (NZ - 1)
    first, last = level == 0, level == NZ - 1

    def x_pair(p):
        lower = pltpu.roll(p, 1, axis=0)
        edge = jnp.where(lane < 32, 0.0, pltpu.roll(lower, 32, axis=1))
        lower = jnp.where(row == 0, edge, lower)
        upper = pltpu.roll(p, XI - 1, axis=0)
        edge = jnp.where(lane >= 96, 0.0, pltpu.roll(upper, 96, axis=1))
        upper = jnp.where(row == XI - 1, edge, upper)
        return lower, upper

    vertical = jnp.broadcast_to(mean, (XI, LANES)) * F32(-TIME_STEP * BUOYANCY)
    up = jnp.where(last, 0.0, pltpu.roll(vertical, LANES - 1, axis=1))
    down = jnp.where(first, 0.0, pltpu.roll(vertical, 1, axis=1))
    source = (up - down) * 0.5
    p = source * F32(-SIXTH)
    for sweep in range(SWEEPS):
        lower, upper = x_pair(p)
        p = (lower + upper + 2.0 * p + above(p, last) + below(p, first) - source) * F32(SIXTH)
    lower, upper = x_pair(p)
    return (upper - lower) * -0.5, vertical - (above(p, last) - below(p, first)) * 0.5


def step_kernel(*refs, step, cells):
    refs = list(refs)
    fields_in, lo, hi, maps, bands_in, inflow_in = refs[:6]
    del refs[:6]
    mean = None
    if step > 0:
        mean = refs.pop(0)
    out = refs.pop(0)
    su = sd = bands = sums = inflow_out = None
    if step < STEPS - 1:
        su, sd, bands, sums = refs[:4]
        del refs[:4]
    if step == 0:
        inflow_out = refs.pop(0)
    f, v, r, pa, pb, ns, change, inflow = refs
    first, last = level_masks()
    lane_ext = lanes(EXT)
    body = slice(8, 8 + EXT)

    if step > 0:
        du, dw = mean_response(mean[0:1, :] * F32(1.0 / cells))
        change[0] = du
        change[1] = dw
        inflow[...] = inflow_in[...]
    else:
        for c in range(4):
            inflow[c, 0:8] = lo[TILES + MORE + c]
            inflow[c, 8 : 8 + OWN] = inflow_in[c]
            inflow[c, 8 + OWN : EXT] = hi[TILES + MORE + c]
        inflow_out[...] = inflow[...]

    def fill(xi, carry):
        for c in range(4):
            low, mid, high = lo[c * XI + xi], fields_in[c, xi], hi[c * XI + xi]
            if step > 0 and c in (0, 2):
                d = change[c // 2, pl.ds(xi, 1), :]
                low, mid, high = low + d, mid + d, high + d
            f[c, xi + 1, 8:16] = low
            f[c, xi + 1, 16 : 16 + OWN] = mid
            f[c, xi + 1, 16 + OWN : 8 + EXT] = high
        return carry

    rows("fill", fill)
    shift = (LANES - 32 * step) % LANES

    def entry(c):
        value = inflow[c]
        return pltpu.roll(value, shift, axis=1) if shift else value

    for c in range(4):
        f[c, 0, body] = jnp.where(
            lane_ext < 32, entry(c), pltpu.roll(f[c, XI, body], 32, axis=1)
        )
        f[c, XI + 1, body] = jnp.where(
            lane_ext >= 96, f[c, XI, body], pltpu.roll(f[c, 1, body], 96, axis=1)
        )

    packed = []
    for c in range(2):
        parts = [lo[TILES + 2 * c + t] for t in range(2)] + [bands_in[c]]
        parts += [hi[TILES + 2 * c + t] for t in range(2)]
        packed.append(jnp.concatenate(parts, axis=0))
    if step > 0:
        level = lanes(XI) & (NZ - 1)
        row = lax.broadcasted_iota(jnp.int32, (XI, LANES), 0)
        shift_u = jnp.where(level == row, exact_dot(change[0], group_matrix("row")), 0.0)
        packed[0] = packed[0] + jnp.sum(shift_u, axis=0, keepdims=True)
    ident, cosine, sine = maps[0], maps[1], maps[2]
    speed = cosine * packed[0] + sine * packed[1]
    forward = backward = speed
    size = ident.shape[0]
    row = lax.broadcasted_iota(jnp.int32, ident.shape, 0)
    for d in (1, 2, 4, 8):
        same = (ident == pltpu.roll(ident, d, axis=0)) & (row >= d)
        forward = forward + jnp.where(same, pltpu.roll(forward, d, axis=0), 0.0)
        same = (ident == pltpu.roll(ident, size - d, axis=0)) & (row < size - d)
        backward = backward + jnp.where(same, pltpu.roll(backward, size - d, axis=0), 0.0)
    total = forward + backward - speed
    thrust = maps[3] * total * jnp.abs(total)
    level = lanes(EXT) & (NZ - 1)
    matrix = group_matrix("column")
    for c, direction in enumerate((cosine, sine)):
        pushed = (thrust * direction)[8 : 8 + EXT]
        for part in range(0, XI, 4):
            spread = [jnp.where(level == xi, pushed, 0.0) for xi in range(part, part + 4)]
            result = exact_dot(jnp.concatenate(spread, axis=0), matrix)
            ns[c, part : part + 4] = result.reshape(4, EXT, LANES)

    def tendencies(xi, total):
        for tile in range(EXT // 8):
            base = 8 + tile * 8
            centre, gx, gy, gz, lap = [], [], [], [], []
            for c in range(4):
                mid = f[c, xi + 1, base : base + 8, :]
                xm = f[c, xi, base : base + 8, :]
                xp = f[c, xi + 2, base : base + 8, :]
                ym = f[c, xi + 1, base - 1 : base + 7, :]
                yp = f[c, xi + 1, base + 1 : base + 9, :]
                if c == 2:
                    zm = jnp.where(first, 0.0, pltpu.roll(mid, 1, axis=1))
                    zp = jnp.where(last, 0.0, pltpu.roll(mid, LANES - 1, axis=1))
                else:
                    zm, zp = below(mid, first), above(mid, last)
                centre.append(mid)
                gx.append(xp - xm)
                gy.append(yp - ym)
                gz.append(zp - zm)
                lap.append((xp + xm) + (yp + ym) + (zp + zm) - 6.0 * mid)
            s_xy = gy[0] + gx[1]
            s_xz = gz[0] + gx[2]
            s_yz = gz[1] + gy[2]
            strain = jnp.sqrt(
                2.0 * (gx[0] * gx[0] + gy[1] * gy[1] + gz[2] * gz[2])
                + (s_xy * s_xy + s_xz * s_xz + s_yz * s_yz)
            )
            nu = F32(TIME_STEP * VISCOSITY) + F32(0.5 * TIME_STEP * SMAGORINSKY) * strain
            half = F32(0.5 * TIME_STEP)
            au, av, aw = half * centre[0], half * centre[1], half * centre[2]
            for c in range(4):
                scale = nu * F32(DIFFUSIVITY_RATIO) if c == 3 else nu
                new = centre[c] + (scale * lap[c] - (au * gx[c] + av * gy[c] + aw * gz[c]))
                if c < 2:
                    new = new + ns[c, xi, tile * 8 : tile * 8 + 8, :]
                elif c == 2:
                    new = new + F32(TIME_STEP * BUOYANCY) * centre[3]
                if c < 3:
                    v[c, xi + 1, base : base + 8, :] = new
                elif 1 <= tile <= 4:
                    out[3, xi, tile * 8 - 8 : tile * 8, :] = new
                    if sums is not None:
                        total = total + new
                        if tile == 1:
                            sd[3 * XI + xi] = new
                        if tile == 4:
                            su[3 * XI + xi] = new
        return total

    total = rows("tend", tendencies, jnp.zeros((8, LANES), F32))
    if sums is not None:
        total = over_groups(jnp.sum(total, axis=0, keepdims=True))
        sums[...] = jnp.broadcast_to(total, (8, LANES))

    v[0, 0, body] = jnp.where(lane_ext < 32, entry(0), pltpu.roll(v[0, XI, body], 32, axis=1))
    v[0, XI + 1, body] = jnp.where(
        lane_ext >= 96, v[0, XI, body], pltpu.roll(v[0, 1, body], 96, axis=1)
    )

    def divergence(xi, carry):
        for tile in range(EXT // 8):
            base = 8 + tile * 8
            here = slice(base, base + 8)
            w = v[2, xi + 1, here, :]
            up = jnp.where(last, 0.0, pltpu.roll(w, LANES - 1, axis=1))
            down = jnp.where(first, 0.0, pltpu.roll(w, 1, axis=1))
            total = (v[0, xi + 2, here, :] - v[0, xi, here, :]) + (up - down)
            total = total + (
                v[1, xi + 1, base + 1 : base + 9, :] - v[1, xi + 1, base - 1 : base + 7, :]
            )
            source = total * F32(0.5 * SIXTH)
            r[xi, tile * 8 : tile * 8 + 8, :] = source
            pa[xi + 1, here, :] = -source
        return carry

    rows("div", divergence)

    def ends(p):
        p[0, body] = jnp.where(lane_ext < 32, 0.0, pltpu.roll(p[XI, body], 32, axis=1))
        p[XI + 1, body] = jnp.where(lane_ext >= 96, 0.0, pltpu.roll(p[1, body], 96, axis=1))

    for sweep in range(SWEEPS):
        p, q = (pa, pb) if sweep % 2 == 0 else (pb, pa)
        ends(p)

        def relax(xi, carry, p=p, q=q):
            for tile in range(EXT // 8):
                base = 8 + tile * 8
                here = slice(base, base + 8)
                mid = p[xi + 1, here, :]
                beside = (p[xi, here, :] + p[xi + 2, here, :]) + (
                    p[xi + 1, base - 1 : base + 7, :] + p[xi + 1, base + 1 : base + 9, :]
                )
                beside = beside + (below(mid, first) + above(mid, last))
                q[xi + 1, here, :] = beside * F32(SIXTH) - r[xi, tile * 8 : tile * 8 + 8, :]
            return carry

        rows("relax", relax)
    p = pa if SWEEPS % 2 == 0 else pb
    ends(p)

    def correct(xi, carry):
        for tile in range(1, 5):
            base = 8 + tile * 8
            here = slice(base, base + 8)
            mid = p[xi + 1, here, :]
            slopes = (
                p[xi + 2, here, :] - p[xi, here, :],
                p[xi + 1, base + 1 : base + 9, :] - p[xi + 1, base - 1 : base + 7, :],
                above(mid, last) - below(mid, first),
            )
            for c in range(3):
                new = v[c, xi + 1, here, :] - 0.5 * slopes[c]
                out[c, xi, tile * 8 - 8 : tile * 8, :] = new
                if sums is not None:
                    if tile == 1:
                        sd[c * XI + xi] = new
                    if tile == 4:
                        su[c * XI + xi] = new
        return carry

    rows("correct", correct)
    if sums is not None:
        band_sums(out, su, sd, bands)


def step_scratch():
    return [
        pltpu.VMEM((4, XI + 2, PAD, LANES), F32),
        pltpu.VMEM((3, XI + 2, PAD, LANES), F32),
        pltpu.VMEM((XI, EXT, LANES), F32),
        pltpu.VMEM((XI + 2, PAD, LANES), F32),
        pltpu.VMEM((XI + 2, PAD, LANES), F32),
        pltpu.VMEM((2, XI, EXT, LANES), F32),
        pltpu.VMEM((2, XI, LANES), F32),
        pltpu.VMEM((4, EXT, LANES), F32),
    ]


def send_kernel(scal, fields, s0, s1, s2, s3, turned):
    own = scal[0]

    def per_row(xi, carry):
        stacked = jnp.concatenate([fields[c, xi] for c in range(4)], axis=0)
        turned[xi] = stacked.T.reshape(GX, 4, 8, LANES)
        for s, out in enumerate((s0, s1, s2, s3)):
            out[pl.ds(xi * 4, 4)] = turned[xi, own ^ s]
        return carry

    rows("fill", per_row)


def final_kernel(scal, mean, s0, r1, r2, r3, out, columns, *, cells):
    own, slab = scal[0], scal[1]
    du, dw = mean_response(mean[0:1, :] * F32(1.0 / cells))
    pad = jnp.zeros((LANES - 2 * XI, LANES), F32)
    columns[...] = jnp.concatenate([du, dw, pad], axis=0).T
    own_columns = columns[pl.ds(pl.multiple_of(own * NZ, NZ), NZ), :]
    group = lanes() >> 5
    masks = [group == (slab ^ s) for s in range(4)]
    for x in range(XI):
        for kt in range(4):
            sources = [ref[x * 4 + kt] for ref in (s0, r1, r2, r3)]
            for c in range(4):
                value = None
                for s, source in enumerate(sources):
                    moved = pltpu.roll(source, (((slab ^ s) - c) & 3) * 32, axis=1)
                    value = moved if value is None else jnp.where(masks[s], moved, value)
                if c in (0, 2):
                    column = (0 if c == 0 else XI) + x
                    value = value + own_columns[kt * 8 : kt * 8 + 8, column : column + 1]
                out[c, x, kt * 8 : kt * 8 + 8, :] = value


def ring(groups):
    place = []
    for j in range(groups):
        for b in range(GX):
            i = b ^ (3 * (j & 1))
            place.append(i * groups + j)
    size = len(place)
    up = [(place[s], place[(s + 1) % size]) for s in range(size)]
    return up, [(b, a) for a, b in up]


def swapped(value, axis, size, distance):
    return lax.ppermute(value, axis, [(i, i ^ distance) for i in range(size)])


def local(state, planes, turbine_cell, active, yaw_sector, slot, *, layouts, groups):
    gx_index, gy_index = lax.axis_index("gx"), lax.axis_index("gy")
    slab = gx_index ^ (3 * (gy_index & 1))
    scal = jnp.stack([gx_index, slab, lax.axis_index("layout")]).astype(jnp.int32)
    scal = jnp.concatenate([scal, slot, active[0], yaw_sector[0]])
    cells = float(GX * XI * GX * OWN * groups)
    per_layout = planes.shape[0]
    height = (jnp.arange(NZ).astype(F32) + 0.5) / NZ
    zeros = jnp.zeros((NZ,), F32)
    profile = jnp.tile(jnp.stack([height ** (1.0 / 7.0), zeros, zeros, 0.5 * height]), (1, GX))
    profile = jnp.pad(profile, ((0, 4), (0, 0)))
    up, down = ring(groups)
    gy_up = [(j, (j + 1) % groups) for j in range(groups)]
    gy_down = [(b, a) for a, b in gy_up]

    ids = turbine_cell[0, :, NZ // 2, :].astype(F32)
    ids = jnp.stack([ids, lax.ppermute(ids, "gy", gy_up), lax.ppermute(ids, "gy", gy_down)])
    chunk = shape(TILES + 7, 8, LANES)
    s0, s1, s2, s3, plane = call(
        pack_kernel,
        (chunk, chunk, chunk, chunk, shape(per_layout * 4, 8, LANES)),
        [SMEM, VMEM, VMEM, VMEM],
        name="pack",
    )(scal, state[0], planes, ids)
    received = [swapped(value, "gx", GX, s) for s, value in ((1, s1), (2, s2), (3, s3))]
    received[0], plane = lax.optimization_barrier((received[0], plane))
    plane_received = [swapped(plane, "layout", layouts, s) for s in range(1, layouts)]

    first_payload = shape(TILES + MORE + 4, 8, LANES)
    fields, inflow, su, sd, bands, sums, ids = call(
        functools.partial(unpack_kernel, layouts=layouts, per_layout=per_layout),
        (
            shape(4, XI, OWN, LANES),
            shape(4, OWN, LANES),
            first_payload,
            first_payload,
            shape(2, OWN, LANES),
            shape(8, LANES),
            shape(3, GX, XI, LANES),
        ),
        [SMEM, VMEM] + [VMEM] * (4 + layouts),
        [
            pltpu.VMEM((GX, TILES, 8, LANES), F32),
            pltpu.VMEM((layouts, per_layout * 4, 8, LANES), F32),
        ],
        name="unpack",
    )(scal, profile, s0, *received, plane, *plane_received)

    maps = call(maps_kernel, shape(4, 2 * OWN, LANES), [SMEM, VMEM], name="maps")(scal, ids)

    half = groups // 2

    def among_x(value):
        return sum([swapped(value, "gy", groups, d) for d in range(1, half)], value)

    def last_swap(value):
        return value + swapped(value, "gy", groups, half)

    mean = pending = None
    for step in range(STEPS):
        partial = sums
        if step > 0:
            partial = partial + swapped(partial, "gx", GX, 1)
            su, sd, partial = lax.optimization_barrier((su, sd, partial))
            mean = last_swap(pending) if step > 1 else pending
        lo = lax.ppermute(su, ("gx", "gy"), up)
        hi = lax.ppermute(sd, ("gx", "gy"), down)
        fields, partial = lax.optimization_barrier((fields, among_x(partial)))
        arriving = swapped(partial, "gx", GX, 2) if step > 0 else swapped(partial, "gy", groups, half)
        if step == 0:
            partial = partial + cells * profile[3:4]
        outs = [shape(4, XI, OWN, LANES)]
        if step < STEPS - 1:
            payload = shape(TILES + MORE, 8, LANES)
            outs += [payload, payload, shape(2, OWN, LANES), shape(8, LANES)]
        if step == 0:
            outs += [shape(4, EXT, LANES)]
        operands = [fields, lo, hi, maps, bands, inflow] + ([mean] if step > 0 else [])
        results = call(
            functools.partial(step_kernel, step=step, cells=cells),
            tuple(outs),
            [VMEM] * len(operands),
            step_scratch(),
            flops=6_000_000_000,
            name="step%d" % step,
        )(*operands)
        results = list(results)
        fields = results.pop(0)
        if step < STEPS - 1:
            su, sd, bands, sums = results[:4]
            del results[:4]
        if step == 0:
            inflow = results.pop(0)
        su, sd, fields, arriving = lax.optimization_barrier((su, sd, fields, arriving))
        pending = partial + arriving
    mean = last_swap(pending)

    chunk = shape(TILES, 8, LANES)
    s0, s1, s2, s3 = call(
        send_kernel,
        (chunk, chunk, chunk, chunk),
        [SMEM, VMEM],
        [pltpu.VMEM((XI, GX, 4, 8, LANES), F32)],
        name="send",
    )(scal, fields)
    received = [swapped(value, "gx", GX, s) for s, value in ((1, s1), (2, s2), (3, s3))]
    fields = call(
        functools.partial(final_kernel, cells=cells),
        shape(4, XI, NZ, LANES),
        [SMEM, VMEM] + [VMEM] * 4,
        [pltpu.VMEM((LANES, LANES), F32)],
        name="final",
    )(scal, mean, s0, *received)
    return fields[None]


def solution(mesh):
    body = functools.partial(local, layouts=mesh.shape["layout"], groups=mesh.shape["gy"])
    return jax.shard_map(
        body,
        mesh=mesh,
        in_specs=(
            P("layout", None, "gx", None, "gy"),
            P("layout", None, None, "gy"),
            P("layout", "gx", None, "gy"),
            P("layout", None),
            P("layout", None),
            P(),
        ),
        out_specs=P("layout", None, "gx", None, "gy"),
        check_vma=False,
    )
```

```python
import functools
import math

import jax
import jax.numpy as jnp
from jax import lax
from jax.experimental import pallas as pl
from jax.experimental.pallas import tpu as pltpu
from jax.sharding import PartitionSpec as P

STEPS = 4
SWEEPS = 4
RADIUS = 5
NZ = 32
XI = 16
GX = 4
OWN = 32
HALO = 8
EXT = OWN + 2 * HALO
PAD = EXT + 16
LANES = 128
WIDTH = 2 * RADIUS + 1
LOWEST = NZ // 2 - RADIUS
TILES = 4 * XI
MORE = 4
UNROLL = {"fill": 4, "tend": 4, "div": 16, "relax": 16, "correct": 16}

TIME_STEP = 0.25
VISCOSITY = 0.02
SMAGORINSKY = 0.0289
DIFFUSIVITY_RATIO = 1.0 / 0.7
BUOYANCY = 0.5
THRUST_COEFF = 1.33
YAW_INCREMENT = 0.1
SIXTH = 1.0 / 6.0
F32 = jnp.float32
INTS = 7
VLIMIT = 40 * 1024 * 1024

VMEM = pl.BlockSpec(memory_space=pltpu.VMEM)
SMEM = pl.BlockSpec(memory_space=pltpu.SMEM)


def shape(*dims):
    return jax.ShapeDtypeStruct(dims, F32)


def lanes(rows=8):
    return lax.broadcasted_iota(jnp.int32, (rows, LANES), 1)


def level_masks(rows=8):
    level = lanes(rows) & (NZ - 1)
    return level == 0, level == NZ - 1


def below(f, first):
    return jnp.where(first, f, pltpu.roll(f, 1, axis=1))


def above(f, last):
    return jnp.where(last, f, pltpu.roll(f, LANES - 1, axis=1))


def call(kernel, out_shape, in_specs, scratch=(), flops=2_000_000_000, **kwargs):
    return pl.pallas_call(
        kernel,
        out_shape=out_shape,
        in_specs=in_specs,
        out_specs=jax.tree.map(lambda _: VMEM, out_shape),
        scratch_shapes=list(scratch),
        compiler_params=pltpu.CompilerParams(vmem_limit_bytes=VLIMIT),
        cost_estimate=pl.CostEstimate(flops=flops, bytes_accessed=4_000_000, transcendentals=0),
        **kwargs,
    )


def rows(name, body, carry=0):
    count = UNROLL[name]

    def some(index, carry):
        for offset in range(count):
            carry = body(index * count + offset, carry)
        return carry

    return lax.fori_loop(0, XI // count, some, carry)


def group_matrix(banded):
    row = lax.broadcasted_iota(jnp.int32, (LANES, LANES), 0)
    column = lax.broadcasted_iota(jnp.int32, (LANES, LANES), 1)
    level = (row if banded == "row" else column) & (NZ - 1)
    inside = (level >= LOWEST) & (level < LOWEST + WIDTH)
    return jnp.where(((row >> 5) == (column >> 5)) & inside, 1.0, 0.0).astype(F32)


def exact_dot(a, b):
    return jnp.dot(a, b, precision=lax.Precision.HIGHEST, preferred_element_type=F32)


def band_sums(fields, su, sd, sums):
    matrix = group_matrix("row")
    level = lanes(OWN) & (NZ - 1)
    for c in range(2):
        total = exact_dot(fields[c].reshape(XI * OWN, LANES), matrix)
        packed = jnp.zeros((OWN, LANES), F32)
        for xi in range(XI):
            packed = jnp.where(level == xi, total[xi * OWN : (xi + 1) * OWN], packed)
        sums[c] = packed
        for t in range(2):
            sd[TILES + 2 * c + t] = packed[t * 8 : t * 8 + 8]
            su[TILES + 2 * c + t] = packed[16 + t * 8 : 24 + t * 8]


def block_transposed(sources, group, masks):
    out = None
    for c, value in enumerate(sources):
        moved = pltpu.roll(value, ((c - group) & 3) * 32, axis=1)
        out = moved if out is None else jnp.where(masks[c], moved, out)
    return out


def transposed4(a, odd, high):
    b0 = jnp.where(odd, pltpu.roll(a[1], 32, axis=1), a[0])
    b1 = jnp.where(odd, a[1], pltpu.roll(a[0], 96, axis=1))
    b2 = jnp.where(odd, pltpu.roll(a[3], 32, axis=1), a[2])
    b3 = jnp.where(odd, a[3], pltpu.roll(a[2], 96, axis=1))
    return (
        jnp.where(high, pltpu.roll(b2, 64, axis=1), b0),
        jnp.where(high, pltpu.roll(b3, 64, axis=1), b1),
        jnp.where(high, b2, pltpu.roll(b0, 64, axis=1)),
        jnp.where(high, b3, pltpu.roll(b1, 64, axis=1)),
    )


def pack_kernel(scal, state, planes, ids, s0, s1, s2, s3, pl_out, stage):
    slab = scal[1]
    group = lanes() >> 5
    masks = [group == c for c in range(4)]
    outs = (s0, s1, s2, s3)
    odd, high = (group & 1) == 1, group >= 2

    def per_row(x, total):
        for kt in range(4):
            sources = [state[c, x, kt * 8 : kt * 8 + 8, :] for c in range(4)]
            for b, value in enumerate(transposed4(sources, odd, high)):
                stage[b, x * 4 + kt] = value
        return total + state[3, x]

    total = rows("fill", per_row, jnp.zeros((NZ, LANES), F32))
    for s, out in enumerate(outs):
        out[:TILES] = stage[slab ^ s]
    levels = jnp.concatenate([total] * GX, axis=0).T
    levels = jnp.broadcast_to(jnp.sum(levels, axis=0, keepdims=True), (8, LANES))
    for out in outs:
        for half in range(6):
            out[TILES + half] = ids[half // 2, (half % 2) * 8 : (half % 2) * 8 + 8]
        out[TILES + 6] = levels
    for plane in range(planes.shape[0]):
        for kt in range(4):
            sources = [planes[plane, c, kt * 8 : kt * 8 + 8, :] for c in range(4)]
            pl_out[plane * 4 + kt] = block_transposed(sources, slab, masks)


def maps_kernel(ints, ids, maps):
    slab = ints[1]
    lane = lanes(NZ)
    pieces = []
    for g in range(GX):
        moved_mid = pltpu.roll(ids[0, g], (16 - 32 * slab) & (LANES - 1), axis=1)
        moved_left = pltpu.roll(ids[1, g], 16, axis=1)
        moved_right = pltpu.roll(ids[2, g], OWN + 16, axis=1)
        here = jnp.where((lane[:XI] < 16) & (slab == 0), moved_left, moved_mid)
        here = jnp.where((lane[:XI] >= OWN + 16) & (slab == 3), moved_right, here)
        pieces += [here, jnp.full((XI, LANES), -1.0, F32)]
    here = jnp.concatenate(pieces, axis=0)
    turbines = (ints.shape[0] - INTS) // 2

    def per_turbine(t, carry):
        sector, running = carry
        match = here == t.astype(F32)
        return (
            jnp.where(match, ints[INTS + turbines + t].astype(F32), sector),
            jnp.where(match, ints[INTS + t].astype(F32), running),
        )

    sector, running = lax.fori_loop(
        0, turbines, per_turbine, (jnp.full((LANES, LANES), -1.0, F32), jnp.zeros((LANES, LANES), F32))
    )
    cosine = jnp.zeros((LANES, LANES), F32)
    sine = jnp.zeros((LANES, LANES), F32)
    for value in range(8):
        angle = (value - 3.5) * YAW_INCREMENT
        cosine = jnp.where(sector == value, F32(math.cos(angle)), cosine)
        sine = jnp.where(sector == value, F32(math.sin(angle)), sine)
    thrust = running * F32(-0.5 * THRUST_COEFF * TIME_STEP / float(WIDTH**2) ** 2)
    low = lanes(LANES) < 64
    first = jnp.where(low, here, pltpu.roll(thrust, 64, axis=1)).T
    second = jnp.where(low, cosine, pltpu.roll(sine, 64, axis=1)).T
    maps[0], maps[3] = first[:64], first[64:]
    maps[1], maps[2] = second[:64], second[64:]


def over_groups(row):
    row = row + pltpu.roll(row, 64, axis=1)
    return row + pltpu.roll(row, 32, axis=1)


def unpack_kernel(
    scal, profile, s0, r1, r2, r3, p0, *rest, layouts, per_layout
):
    plane_refs = (p0,) + rest[: layouts - 1]
    fields, inflow, su, sd, bands, sums, ids, held, planes = rest[layouts - 1 :]
    own, here = scal[0], scal[2]
    for s, source in enumerate((s0, r1, r2, r3)):
        held[own ^ s] = source[:TILES]
        for half in range(6):
            ids[half // 2, own ^ s, (half % 2) * 8 : (half % 2) * 8 + 8, :] = source[TILES + half]
    sums[...] = s0[TILES + 6] + r1[TILES + 6] + r2[TILES + 6] + r3[TILES + 6]
    for s, source in enumerate(plane_refs):
        planes[here ^ s] = source[...]

    def per_row(xi, carry):
        parts = [held[g, pl.ds(xi * 4, 4)].reshape(NZ, LANES) for g in range(GX)]
        turned = jnp.concatenate(parts, axis=0).T
        for c in range(4):
            value = turned[c * 32 : c * 32 + 32] + profile[c : c + 1, :]
            fields[c, xi] = value
            sd[c * XI + xi] = value[:HALO]
            su[c * XI + xi] = value[OWN - HALO :]
        return carry

    rows("fill", per_row)
    parts = []
    for step in range(STEPS):
        plane = scal[3 + step]
        parts.append(
            planes[plane // per_layout, pl.ds((plane % per_layout) * 4, 4)].reshape(NZ, LANES)
        )
    turned = jnp.concatenate(parts, axis=0).T
    for c in range(4):
        value = turned[c * 32 : c * 32 + 32] + profile[c : c + 1, :]
        inflow[c] = value
        sd[TILES + MORE + c] = value[:HALO]
        su[TILES + MORE + c] = value[OWN - HALO :]
    band_sums(fields, su, sd, bands)


def mean_response(mean):
    lane = lanes(XI)
    row = lax.broadcasted_iota(jnp.int32, (XI, LANES), 0)
    level = lane & (NZ - 1)
    first, last = level == 0, level == NZ - 1

    def x_pair(p):
        lower = pltpu.roll(p, 1, axis=0)
        edge = jnp.where(lane < 32, 0.0, pltpu.roll(lower, 32, axis=1))
        lower = jnp.where(row == 0, edge, lower)
        upper = pltpu.roll(p, XI - 1, axis=0)
        edge = jnp.where(lane >= 96, 0.0, pltpu.roll(upper, 96, axis=1))
        upper = jnp.where(row == XI - 1, edge, upper)
        return lower, upper

    vertical = jnp.broadcast_to(mean, (XI, LANES)) * F32(-TIME_STEP * BUOYANCY)
    up = jnp.where(last, 0.0, pltpu.roll(vertical, LANES - 1, axis=1))
    down = jnp.where(first, 0.0, pltpu.roll(vertical, 1, axis=1))
    source = (up - down) * 0.5
    p = source * F32(-SIXTH)
    for sweep in range(SWEEPS):
        lower, upper = x_pair(p)
        p = (lower + upper + 2.0 * p + above(p, last) + below(p, first) - source) * F32(SIXTH)
    lower, upper = x_pair(p)
    return (upper - lower) * -0.5, vertical - (above(p, last) - below(p, first)) * 0.5


def step_kernel(*refs, step, cells):
    refs = list(refs)
    fields_in, lo, hi, maps, bands_in, inflow_in = refs[:6]
    del refs[:6]
    mean = None
    if step > 0:
        mean = refs.pop(0)
    out = refs.pop(0)
    su = sd = bands = sums = inflow_out = None
    if step < STEPS - 1:
        su, sd, bands, sums = refs[:4]
        del refs[:4]
    if step == 0:
        inflow_out = refs.pop(0)
    f, v, r, pa, pb, ns, change, inflow = refs
    first, last = level_masks()
    lane_ext = lanes(EXT)
    body = slice(8, 8 + EXT)

    if step > 0:
        du, dw = mean_response(mean[0:1, :] * F32(1.0 / cells))
        change[0] = du
        change[1] = dw
        inflow[...] = inflow_in[...]
    else:
        for c in range(4):
            inflow[c, 0:8] = lo[TILES + MORE + c]
            inflow[c, 8 : 8 + OWN] = inflow_in[c]
            inflow[c, 8 + OWN : EXT] = hi[TILES + MORE + c]
        inflow_out[...] = inflow[...]

    def fill(xi, carry):
        for c in range(4):
            low, mid, high = lo[c * XI + xi], fields_in[c, xi], hi[c * XI + xi]
            if step > 0 and c in (0, 2):
                d = change[c // 2, pl.ds(xi, 1), :]
                low, mid, high = low + d, mid + d, high + d
            f[c, xi + 1, 8:16] = low
            f[c, xi + 1, 16 : 16 + OWN] = mid
            f[c, xi + 1, 16 + OWN : 8 + EXT] = high
        return carry

    rows("fill", fill)
    shift = (LANES - 32 * step) % LANES

    def entry(c):
        value = inflow[c]
        return pltpu.roll(value, shift, axis=1) if shift else value

    for c in range(4):
        f[c, 0, body] = jnp.where(
            lane_ext < 32, entry(c), pltpu.roll(f[c, XI, body], 32, axis=1)
        )
        f[c, XI + 1, body] = jnp.where(
            lane_ext >= 96, f[c, XI, body], pltpu.roll(f[c, 1, body], 96, axis=1)
        )

    packed = []
    for c in range(2):
        parts = [lo[TILES + 2 * c + t] for t in range(2)] + [bands_in[c]]
        parts += [hi[TILES + 2 * c + t] for t in range(2)]
        packed.append(jnp.concatenate(parts, axis=0))
    if step > 0:
        level = lanes(XI) & (NZ - 1)
        row = lax.broadcasted_iota(jnp.int32, (XI, LANES), 0)
        shift_u = jnp.where(level == row, exact_dot(change[0], group_matrix("row")), 0.0)
        packed[0] = packed[0] + jnp.sum(shift_u, axis=0, keepdims=True)
    ident, cosine, sine = maps[0], maps[1], maps[2]
    speed = cosine * packed[0] + sine * packed[1]
    forward = backward = speed
    size = ident.shape[0]
    row = lax.broadcasted_iota(jnp.int32, ident.shape, 0)
    for d in (1, 2, 4, 8):
        same = (ident == pltpu.roll(ident, d, axis=0)) & (row >= d)
        forward = forward + jnp.where(same, pltpu.roll(forward, d, axis=0), 0.0)
        same = (ident == pltpu.roll(ident, size - d, axis=0)) & (row < size - d)
        backward = backward + jnp.where(same, pltpu.roll(backward, size - d, axis=0), 0.0)
    total = forward + backward - speed
    thrust = maps[3] * total * jnp.abs(total)
    level = lanes(EXT) & (NZ - 1)
    matrix = group_matrix("column")
    for c, direction in enumerate((cosine, sine)):
        pushed = (thrust * direction)[8 : 8 + EXT]
        for part in range(0, XI, 4):
            spread = [jnp.where(level == xi, pushed, 0.0) for xi in range(part, part + 4)]
            result = exact_dot(jnp.concatenate(spread, axis=0), matrix)
            ns[c, part : part + 4] = result.reshape(4, EXT, LANES)

    def tendencies(xi, total):
        for tile in range(EXT // 8):
            base = 8 + tile * 8
            centre, gx, gy, gz, lap = [], [], [], [], []
            for c in range(4):
                mid = f[c, xi + 1, base : base + 8, :]
                xm = f[c, xi, base : base + 8, :]
                xp = f[c, xi + 2, base : base + 8, :]
                ym = f[c, xi + 1, base - 1 : base + 7, :]
                yp = f[c, xi + 1, base + 1 : base + 9, :]
                if c == 2:
                    zm = jnp.where(first, 0.0, pltpu.roll(mid, 1, axis=1))
                    zp = jnp.where(last, 0.0, pltpu.roll(mid, LANES - 1, axis=1))
                else:
                    zm, zp = below(mid, first), above(mid, last)
                centre.append(mid)
                gx.append(xp - xm)
                gy.append(yp - ym)
                gz.append(zp - zm)
                lap.append((xp + xm) + (yp + ym) + (zp + zm) - 6.0 * mid)
            s_xy = gy[0] + gx[1]
            s_xz = gz[0] + gx[2]
            s_yz = gz[1] + gy[2]
            strain = jnp.sqrt(
                2.0 * (gx[0] * gx[0] + gy[1] * gy[1] + gz[2] * gz[2])
                + (s_xy * s_xy + s_xz * s_xz + s_yz * s_yz)
            )
            nu = F32(TIME_STEP * VISCOSITY) + F32(0.5 * TIME_STEP * SMAGORINSKY) * strain
            half = F32(0.5 * TIME_STEP)
            au, av, aw = half * centre[0], half * centre[1], half * centre[2]
            for c in range(4):
                scale = nu * F32(DIFFUSIVITY_RATIO) if c == 3 else nu
                new = centre[c] + (scale * lap[c] - (au * gx[c] + av * gy[c] + aw * gz[c]))
                if c < 2:
                    new = new + ns[c, xi, tile * 8 : tile * 8 + 8, :]
                elif c == 2:
                    new = new + F32(TIME_STEP * BUOYANCY) * centre[3]
                if c < 3:
                    v[c, xi + 1, base : base + 8, :] = new
                elif 1 <= tile <= 4:
                    out[3, xi, tile * 8 - 8 : tile * 8, :] = new
                    if sums is not None:
                        total = total + new
                        if tile == 1:
                            sd[3 * XI + xi] = new
                        if tile == 4:
                            su[3 * XI + xi] = new
        return total

    total = rows("tend", tendencies, jnp.zeros((8, LANES), F32))
    if sums is not None:
        total = over_groups(jnp.sum(total, axis=0, keepdims=True))
        sums[...] = jnp.broadcast_to(total, (8, LANES))

    v[0, 0, body] = jnp.where(lane_ext < 32, entry(0), pltpu.roll(v[0, XI, body], 32, axis=1))
    v[0, XI + 1, body] = jnp.where(
        lane_ext >= 96, v[0, XI, body], pltpu.roll(v[0, 1, body], 96, axis=1)
    )

    def divergence(xi, carry):
        for tile in range(EXT // 8):
            base = 8 + tile * 8
            here = slice(base, base + 8)
            w = v[2, xi + 1, here, :]
            up = jnp.where(last, 0.0, pltpu.roll(w, LANES - 1, axis=1))
            down = jnp.where(first, 0.0, pltpu.roll(w, 1, axis=1))
            total = (v[0, xi + 2, here, :] - v[0, xi, here, :]) + (up - down)
            total = total + (
                v[1, xi + 1, base + 1 : base + 9, :] - v[1, xi + 1, base - 1 : base + 7, :]
            )
            source = total * F32(0.5 * SIXTH)
            r[xi, tile * 8 : tile * 8 + 8, :] = source
            pa[xi + 1, here, :] = -source
        return carry

    rows("div", divergence)

    def ends(p):
        p[0, body] = jnp.where(lane_ext < 32, 0.0, pltpu.roll(p[XI, body], 32, axis=1))
        p[XI + 1, body] = jnp.where(lane_ext >= 96, 0.0, pltpu.roll(p[1, body], 96, axis=1))

    for sweep in range(SWEEPS):
        p, q = (pa, pb) if sweep % 2 == 0 else (pb, pa)
        ends(p)

        def relax(xi, carry, p=p, q=q):
            for tile in range(EXT // 8):
                base = 8 + tile * 8
                here = slice(base, base + 8)
                mid = p[xi + 1, here, :]
                beside = (p[xi, here, :] + p[xi + 2, here, :]) + (
                    p[xi + 1, base - 1 : base + 7, :] + p[xi + 1, base + 1 : base + 9, :]
                )
                beside = beside + (below(mid, first) + above(mid, last))
                q[xi + 1, here, :] = beside * F32(SIXTH) - r[xi, tile * 8 : tile * 8 + 8, :]
            return carry

        rows("relax", relax)
    p = pa if SWEEPS % 2 == 0 else pb
    ends(p)

    def correct(xi, carry):
        for tile in range(1, 5):
            base = 8 + tile * 8
            here = slice(base, base + 8)
            mid = p[xi + 1, here, :]
            slopes = (
                p[xi + 2, here, :] - p[xi, here, :],
                p[xi + 1, base + 1 : base + 9, :] - p[xi + 1, base - 1 : base + 7, :],
                above(mid, last) - below(mid, first),
            )
            for c in range(3):
                new = v[c, xi + 1, here, :] - 0.5 * slopes[c]
                out[c, xi, tile * 8 - 8 : tile * 8, :] = new
                if sums is not None:
                    if tile == 1:
                        sd[c * XI + xi] = new
                    if tile == 4:
                        su[c * XI + xi] = new
        return carry

    rows("correct", correct)
    if sums is not None:
        band_sums(out, su, sd, bands)


def step_scratch():
    return [
        pltpu.VMEM((4, XI + 2, PAD, LANES), F32),
        pltpu.VMEM((3, XI + 2, PAD, LANES), F32),
        pltpu.VMEM((XI, EXT, LANES), F32),
        pltpu.VMEM((XI + 2, PAD, LANES), F32),
        pltpu.VMEM((XI + 2, PAD, LANES), F32),
        pltpu.VMEM((2, XI, EXT, LANES), F32),
        pltpu.VMEM((2, XI, LANES), F32),
        pltpu.VMEM((4, EXT, LANES), F32),
    ]


def send_kernel(scal, fields, s0, s1, s2, s3, turned):
    own = scal[0]

    def per_row(xi, carry):
        stacked = jnp.concatenate([fields[c, xi] for c in range(4)], axis=0)
        turned[xi] = stacked.T.reshape(GX, 4, 8, LANES)
        for s, out in enumerate((s0, s1, s2, s3)):
            out[pl.ds(xi * 4, 4)] = turned[xi, own ^ s]
        return carry

    rows("fill", per_row)


def final_kernel(scal, mean, s0, r1, r2, r3, out, columns, stage, *, cells):
    own, slab = scal[0], scal[1]
    for s, source in enumerate((s0, r1, r2, r3)):
        stage[slab ^ s] = source[...]
    du, dw = mean_response(mean[0:1, :] * F32(1.0 / cells))
    pad = jnp.zeros((LANES - 2 * XI, LANES), F32)
    columns[...] = jnp.concatenate([du, dw, pad], axis=0).T
    own_columns = columns[pl.ds(pl.multiple_of(own * NZ, NZ), NZ), :]
    group = lanes() >> 5
    odd, high = (group & 1) == 1, group >= 2
    for x in range(XI):
        for kt in range(4):
            sources = [stage[b, x * 4 + kt] for b in range(4)]
            for c, value in enumerate(transposed4(sources, odd, high)):
                if c in (0, 2):
                    column = (0 if c == 0 else XI) + x
                    value = value + own_columns[kt * 8 : kt * 8 + 8, column : column + 1]
                out[c, x, kt * 8 : kt * 8 + 8, :] = value


def ring(groups):
    place = []
    for j in range(groups):
        for b in range(GX):
            i = b ^ (3 * (j & 1))
            place.append(i * groups + j)
    size = len(place)
    up = [(place[s], place[(s + 1) % size]) for s in range(size)]
    return up, [(b, a) for a, b in up]


def swapped(value, axis, size, distance):
    return lax.ppermute(value, axis, [(i, i ^ distance) for i in range(size)])


def local(state, planes, turbine_cell, active, yaw_sector, slot, *, layouts, groups):
    gx_index, gy_index = lax.axis_index("gx"), lax.axis_index("gy")
    slab = gx_index ^ (3 * (gy_index & 1))
    scal = jnp.stack([gx_index, slab, lax.axis_index("layout")]).astype(jnp.int32)
    scal = jnp.concatenate([scal, slot, active[0], yaw_sector[0]])
    cells = float(GX * XI * GX * OWN * groups)
    per_layout = planes.shape[0]
    height = (jnp.arange(NZ).astype(F32) + 0.5) / NZ
    zeros = jnp.zeros((NZ,), F32)
    profile = jnp.tile(jnp.stack([height ** (1.0 / 7.0), zeros, zeros, 0.5 * height]), (1, GX))
    profile = jnp.pad(profile, ((0, 4), (0, 0)))
    up, down = ring(groups)
    gy_up = [(j, (j + 1) % groups) for j in range(groups)]
    gy_down = [(b, a) for a, b in gy_up]

    ids = turbine_cell[0, :, NZ // 2, :].astype(F32)
    ids = jnp.stack([ids, lax.ppermute(ids, "gy", gy_up), lax.ppermute(ids, "gy", gy_down)])
    chunk = shape(TILES + 7, 8, LANES)
    s0, s1, s2, s3, plane = call(
        pack_kernel,
        (chunk, chunk, chunk, chunk, shape(per_layout * 4, 8, LANES)),
        [SMEM, VMEM, VMEM, VMEM],
        [pltpu.VMEM((GX, TILES, 8, LANES), F32)],
        name="pack",
    )(scal, state[0], planes, ids)
    received = [swapped(value, "gx", GX, s) for s, value in ((1, s1), (2, s2), (3, s3))]
    received[0], plane = lax.optimization_barrier((received[0], plane))
    plane_received = [swapped(plane, "layout", layouts, s) for s in range(1, layouts)]

    first_payload = shape(TILES + MORE + 4, 8, LANES)
    fields, inflow, su, sd, bands, sums, ids = call(
        functools.partial(unpack_kernel, layouts=layouts, per_layout=per_layout),
        (
            shape(4, XI, OWN, LANES),
            shape(4, OWN, LANES),
            first_payload,
            first_payload,
            shape(2, OWN, LANES),
            shape(8, LANES),
            shape(3, GX, XI, LANES),
        ),
        [SMEM, VMEM] + [VMEM] * (4 + layouts),
        [
            pltpu.VMEM((GX, TILES, 8, LANES), F32),
            pltpu.VMEM((layouts, per_layout * 4, 8, LANES), F32),
        ],
        name="unpack",
    )(scal, profile, s0, *received, plane, *plane_received)

    maps = call(maps_kernel, shape(4, 2 * OWN, LANES), [SMEM, VMEM], name="maps")(scal, ids)

    half = groups // 2

    def among_x(value):
        return sum([swapped(value, "gy", groups, d) for d in range(1, half)], value)

    mean = pending = None
    for step in range(STEPS):
        partial = sums
        if step > 0:
            partial = partial + swapped(partial, "gx", GX, 1)
            su, sd, partial = lax.optimization_barrier((su, sd, partial))
            mean = among_x(pending)
        lo = lax.ppermute(su, ("gx", "gy"), up)
        hi = lax.ppermute(sd, ("gx", "gy"), down)
        if step == 1:
            mean = mean + cells * profile[3:4]
        if step > 0:
            partial = partial + swapped(partial, "gy", groups, half)
            fields, partial = lax.optimization_barrier((fields, partial))
        arriving = swapped(partial, "gx", GX, 2) if step > 0 else swapped(partial, "gy", groups, half)
        outs = [shape(4, XI, OWN, LANES)]
        if step < STEPS - 1:
            payload = shape(TILES + MORE, 8, LANES)
            outs += [payload, payload, shape(2, OWN, LANES), shape(8, LANES)]
        if step == 0:
            outs += [shape(4, EXT, LANES)]
        operands = [fields, lo, hi, maps, bands, inflow] + ([mean] if step > 0 else [])
        results = call(
            functools.partial(step_kernel, step=step, cells=cells),
            tuple(outs),
            [VMEM] * len(operands),
            step_scratch(),
            flops=6_000_000_000,
            name="step%d" % step,
        )(*operands)
        results = list(results)
        fields = results.pop(0)
        if step < STEPS - 1:
            su, sd, bands, sums = results[:4]
            del results[:4]
        if step == 0:
            inflow = results.pop(0)
        su, sd, fields, arriving = lax.optimization_barrier((su, sd, fields, arriving))
        pending = partial + arriving
    mean = among_x(pending)

    chunk = shape(TILES, 8, LANES)
    s0, s1, s2, s3 = call(
        send_kernel,
        (chunk, chunk, chunk, chunk),
        [SMEM, VMEM],
        [pltpu.VMEM((XI, GX, 4, 8, LANES), F32)],
        name="send",
    )(scal, fields)
    received = [swapped(value, "gx", GX, s) for s, value in ((1, s1), (2, s2), (3, s3))]
    fields = call(
        functools.partial(final_kernel, cells=cells),
        shape(4, XI, NZ, LANES),
        [SMEM, VMEM] + [VMEM] * 4,
        [pltpu.VMEM((LANES, LANES), F32), pltpu.VMEM((GX, TILES, 8, LANES), F32)],
        name="final",
    )(scal, mean, s0, *received)
    return fields[None]


def solution(mesh):
    body = functools.partial(local, layouts=mesh.shape["layout"], groups=mesh.shape["gy"])
    return jax.shard_map(
        body,
        mesh=mesh,
        in_specs=(
            P("layout", None, "gx", None, "gy"),
            P("layout", None, None, "gy"),
            P("layout", "gx", None, "gy"),
            P("layout", None),
            P("layout", None),
            P(),
        ),
        out_specs=P("layout", None, "gx", None, "gy"),
        check_vma=False,
    )
```

```python
import functools
import math

import jax
import jax.numpy as jnp
from jax import lax
from jax.experimental import pallas as pl
from jax.experimental.pallas import tpu as pltpu
from jax.sharding import PartitionSpec as P

STEPS = 4
SWEEPS = 4
RADIUS = 5
NZ = 32
XI = 16
GX = 4
OWN = 32
HALO = 8
EXT = OWN + 2 * HALO
PAD = EXT + 16
LANES = 128
WIDTH = 2 * RADIUS + 1
LOWEST = NZ // 2 - RADIUS
TILES = 4 * XI
MORE = 4
UNROLL = {"fill": 4, "tend": 4, "div": 16, "relax": 16, "correct": 16}

TIME_STEP = 0.25
VISCOSITY = 0.02
SMAGORINSKY = 0.0289
DIFFUSIVITY_RATIO = 1.0 / 0.7
BUOYANCY = 0.5
THRUST_COEFF = 1.33
YAW_INCREMENT = 0.1
SIXTH = 1.0 / 6.0
F32 = jnp.float32
INTS = 7
VLIMIT = 40 * 1024 * 1024

VMEM = pl.BlockSpec(memory_space=pltpu.VMEM)
SMEM = pl.BlockSpec(memory_space=pltpu.SMEM)


def shape(*dims):
    return jax.ShapeDtypeStruct(dims, F32)


def lanes(rows=8):
    return lax.broadcasted_iota(jnp.int32, (rows, LANES), 1)


def level_masks(rows=8):
    level = lanes(rows) & (NZ - 1)
    return level == 0, level == NZ - 1


def below(f, first):
    return jnp.where(first, f, pltpu.roll(f, 1, axis=1))


def above(f, last):
    return jnp.where(last, f, pltpu.roll(f, LANES - 1, axis=1))


def call(kernel, out_shape, in_specs, scratch=(), flops=2_000_000_000, **kwargs):
    return pl.pallas_call(
        kernel,
        out_shape=out_shape,
        in_specs=in_specs,
        out_specs=jax.tree.map(lambda _: VMEM, out_shape),
        scratch_shapes=list(scratch),
        compiler_params=pltpu.CompilerParams(vmem_limit_bytes=VLIMIT),
        cost_estimate=pl.CostEstimate(flops=flops, bytes_accessed=4_000_000, transcendentals=0),
        **kwargs,
    )


def rows(name, body, carry=0):
    count = UNROLL[name]

    def some(index, carry):
        for offset in range(count):
            carry = body(index * count + offset, carry)
        return carry

    return lax.fori_loop(0, XI // count, some, carry)


def group_matrix(banded):
    row = lax.broadcasted_iota(jnp.int32, (LANES, LANES), 0)
    column = lax.broadcasted_iota(jnp.int32, (LANES, LANES), 1)
    level = (row if banded == "row" else column) & (NZ - 1)
    inside = (level >= LOWEST) & (level < LOWEST + WIDTH)
    return jnp.where(((row >> 5) == (column >> 5)) & inside, 1.0, 0.0).astype(F32)


def exact_dot(a, b):
    return jnp.dot(a, b, precision=lax.Precision.HIGHEST, preferred_element_type=F32)


def band_sums(fields, su, sd, sums):
    matrix = group_matrix("row")
    level = lanes(OWN) & (NZ - 1)
    for c in range(2):
        total = exact_dot(fields[c].reshape(XI * OWN, LANES), matrix)
        packed = jnp.zeros((OWN, LANES), F32)
        for xi in range(XI):
            packed = jnp.where(level == xi, total[xi * OWN : (xi + 1) * OWN], packed)
        sums[c] = packed
        for t in range(2):
            sd[TILES + 2 * c + t] = packed[t * 8 : t * 8 + 8]
            su[TILES + 2 * c + t] = packed[16 + t * 8 : 24 + t * 8]


def block_transposed(sources, group, masks):
    out = None
    for c, value in enumerate(sources):
        moved = pltpu.roll(value, ((c - group) & 3) * 32, axis=1)
        out = moved if out is None else jnp.where(masks[c], moved, out)
    return out


def transposed4(a, odd, high):
    b0 = jnp.where(odd, pltpu.roll(a[1], 32, axis=1), a[0])
    b1 = jnp.where(odd, a[1], pltpu.roll(a[0], 96, axis=1))
    b2 = jnp.where(odd, pltpu.roll(a[3], 32, axis=1), a[2])
    b3 = jnp.where(odd, a[3], pltpu.roll(a[2], 96, axis=1))
    return (
        jnp.where(high, pltpu.roll(b2, 64, axis=1), b0),
        jnp.where(high, pltpu.roll(b3, 64, axis=1), b1),
        jnp.where(high, b2, pltpu.roll(b0, 64, axis=1)),
        jnp.where(high, b3, pltpu.roll(b1, 64, axis=1)),
    )


def pack_kernel(scal, state, planes, ids, s0, s1, s2, s3, pl_out, stage):
    slab = scal[1]
    group = lanes() >> 5
    masks = [group == c for c in range(4)]
    outs = (s0, s1, s2, s3)
    odd, high = (group & 1) == 1, group >= 2

    def per_row(x, total):
        for kt in range(4):
            sources = [state[c, x, kt * 8 : kt * 8 + 8, :] for c in range(4)]
            for b, value in enumerate(transposed4(sources, odd, high)):
                stage[b, x * 4 + kt] = value
        return total + state[3, x]

    total = rows("fill", per_row, jnp.zeros((NZ, LANES), F32))
    for s, out in enumerate(outs):
        out[:TILES] = stage[slab ^ s]
    levels = jnp.concatenate([total] * GX, axis=0).T
    levels = jnp.broadcast_to(jnp.sum(levels, axis=0, keepdims=True), (8, LANES))
    for out in outs:
        for half in range(6):
            out[TILES + half] = ids[half // 2, (half % 2) * 8 : (half % 2) * 8 + 8]
        out[TILES + 6] = levels
    for plane in range(planes.shape[0]):
        for kt in range(4):
            sources = [planes[plane, c, kt * 8 : kt * 8 + 8, :] for c in range(4)]
            pl_out[plane * 4 + kt] = block_transposed(sources, slab, masks)


def maps_kernel(ints, ids, maps):
    slab = ints[1]
    lane = lanes(NZ)
    pieces = []
    for g in range(GX):
        moved_mid = pltpu.roll(ids[0, g], (16 - 32 * slab) & (LANES - 1), axis=1)
        moved_left = pltpu.roll(ids[1, g], 16, axis=1)
        moved_right = pltpu.roll(ids[2, g], OWN + 16, axis=1)
        here = jnp.where((lane[:XI] < 16) & (slab == 0), moved_left, moved_mid)
        here = jnp.where((lane[:XI] >= OWN + 16) & (slab == 3), moved_right, here)
        pieces += [here, jnp.full((XI, LANES), -1.0, F32)]
    here = jnp.concatenate(pieces, axis=0)
    turbines = (ints.shape[0] - INTS) // 2

    def per_turbine(t, carry):
        sector, running = carry
        match = here == t.astype(F32)
        return (
            jnp.where(match, ints[INTS + turbines + t].astype(F32), sector),
            jnp.where(match, ints[INTS + t].astype(F32), running),
        )

    sector, running = lax.fori_loop(
        0, turbines, per_turbine, (jnp.full((LANES, LANES), -1.0, F32), jnp.zeros((LANES, LANES), F32))
    )
    cosine = jnp.zeros((LANES, LANES), F32)
    sine = jnp.zeros((LANES, LANES), F32)
    for value in range(8):
        angle = (value - 3.5) * YAW_INCREMENT
        cosine = jnp.where(sector == value, F32(math.cos(angle)), cosine)
        sine = jnp.where(sector == value, F32(math.sin(angle)), sine)
    thrust = running * F32(-0.5 * THRUST_COEFF * TIME_STEP / float(WIDTH**2) ** 2)
    low = lanes(LANES) < 64
    first = jnp.where(low, here, pltpu.roll(thrust, 64, axis=1)).T
    second = jnp.where(low, cosine, pltpu.roll(sine, 64, axis=1)).T
    maps[0], maps[3] = first[:64], first[64:]
    maps[1], maps[2] = second[:64], second[64:]


def over_groups(row):
    row = row + pltpu.roll(row, 64, axis=1)
    return row + pltpu.roll(row, 32, axis=1)


def unpack_kernel(
    scal, profile, s0, r1, r2, r3, p0, *rest, layouts, per_layout
):
    plane_refs = (p0,) + rest[: layouts - 1]
    fields, inflow, su, sd, bands, sums, ids, held, planes = rest[layouts - 1 :]
    own, here = scal[0], scal[2]
    for s, source in enumerate((s0, r1, r2, r3)):
        held[own ^ s] = source[:TILES]
        for half in range(6):
            ids[half // 2, own ^ s, (half % 2) * 8 : (half % 2) * 8 + 8, :] = source[TILES + half]
    sums[...] = s0[TILES + 6] + r1[TILES + 6] + r2[TILES + 6] + r3[TILES + 6]
    for s, source in enumerate(plane_refs):
        planes[here ^ s] = source[...]

    def per_row(xi, carry):
        parts = [held[g, pl.ds(xi * 4, 4)].reshape(NZ, LANES) for g in range(GX)]
        turned = jnp.concatenate(parts, axis=0).T
        for c in range(4):
            value = turned[c * 32 : c * 32 + 32] + profile[c : c + 1, :]
            fields[c, xi] = value
            sd[c * XI + xi] = value[:HALO]
            su[c * XI + xi] = value[OWN - HALO :]
        return carry

    rows("fill", per_row)
    parts = []
    for step in range(STEPS):
        plane = scal[3 + step]
        parts.append(
            planes[plane // per_layout, pl.ds((plane % per_layout) * 4, 4)].reshape(NZ, LANES)
        )
    turned = jnp.concatenate(parts, axis=0).T
    for c in range(4):
        value = turned[c * 32 : c * 32 + 32] + profile[c : c + 1, :]
        inflow[c] = value
        sd[TILES + MORE + c] = value[:HALO]
        su[TILES + MORE + c] = value[OWN - HALO :]
    band_sums(fields, su, sd, bands)


def mean_response(mean):
    lane = lanes(XI)
    row = lax.broadcasted_iota(jnp.int32, (XI, LANES), 0)
    level = lane & (NZ - 1)
    first, last = level == 0, level == NZ - 1

    def x_pair(p):
        lower = pltpu.roll(p, 1, axis=0)
        edge = jnp.where(lane < 32, 0.0, pltpu.roll(lower, 32, axis=1))
        lower = jnp.where(row == 0, edge, lower)
        upper = pltpu.roll(p, XI - 1, axis=0)
        edge = jnp.where(lane >= 96, 0.0, pltpu.roll(upper, 96, axis=1))
        upper = jnp.where(row == XI - 1, edge, upper)
        return lower, upper

    vertical = jnp.broadcast_to(mean, (XI, LANES)) * F32(-TIME_STEP * BUOYANCY)
    up = jnp.where(last, 0.0, pltpu.roll(vertical, LANES - 1, axis=1))
    down = jnp.where(first, 0.0, pltpu.roll(vertical, 1, axis=1))
    source = (up - down) * 0.5
    p = source * F32(-SIXTH)
    for sweep in range(SWEEPS):
        lower, upper = x_pair(p)
        p = (lower + upper + 2.0 * p + above(p, last) + below(p, first) - source) * F32(SIXTH)
    lower, upper = x_pair(p)
    return (upper - lower) * -0.5, vertical - (above(p, last) - below(p, first)) * 0.5


def step_kernel(*refs, step, cells):
    refs = list(refs)
    fields_in, lo, hi, maps, bands_in, inflow_in = refs[:6]
    del refs[:6]
    mean = None
    if step > 0:
        mean = refs.pop(0)
    out = refs.pop(0)
    su = sd = bands = sums = inflow_out = None
    if step < STEPS - 1:
        su, sd, bands, sums = refs[:4]
        del refs[:4]
    if step == 0:
        inflow_out = refs.pop(0)
    f, v, r, pa, pb, ns, change, inflow = refs
    first, last = level_masks()
    lane_ext = lanes(EXT)
    body = slice(8, 8 + EXT)

    if step > 0:
        du, dw = mean_response(mean[0:1, :] * F32(1.0 / cells))
        change[0] = du
        change[1] = dw
        inflow[...] = inflow_in[...]
    else:
        for c in range(4):
            inflow[c, 0:8] = lo[TILES + MORE + c]
            inflow[c, 8 : 8 + OWN] = inflow_in[c]
            inflow[c, 8 + OWN : EXT] = hi[TILES + MORE + c]
        inflow_out[...] = inflow[...]

    def fill(xi, carry):
        for c in range(4):
            low, mid, high = lo[c * XI + xi], fields_in[c, xi], hi[c * XI + xi]
            if step > 0 and c in (0, 2):
                d = change[c // 2, pl.ds(xi, 1), :]
                low, mid, high = low + d, mid + d, high + d
            f[c, xi + 1, 8:16] = low
            f[c, xi + 1, 16 : 16 + OWN] = mid
            f[c, xi + 1, 16 + OWN : 8 + EXT] = high
        return carry

    rows("fill", fill)
    shift = (LANES - 32 * step) % LANES

    def entry(c):
        value = inflow[c]
        return pltpu.roll(value, shift, axis=1) if shift else value

    for c in range(4):
        f[c, 0, body] = jnp.where(
            lane_ext < 32, entry(c), pltpu.roll(f[c, XI, body], 32, axis=1)
        )
        f[c, XI + 1, body] = jnp.where(
            lane_ext >= 96, f[c, XI, body], pltpu.roll(f[c, 1, body], 96, axis=1)
        )

    packed = []
    for c in range(2):
        parts = [lo[TILES + 2 * c + t] for t in range(2)] + [bands_in[c]]
        parts += [hi[TILES + 2 * c + t] for t in range(2)]
        packed.append(jnp.concatenate(parts, axis=0))
    if step > 0:
        level = lanes(XI) & (NZ - 1)
        row = lax.broadcasted_iota(jnp.int32, (XI, LANES), 0)
        shift_u = jnp.where(level == row, exact_dot(change[0], group_matrix("row")), 0.0)
        packed[0] = packed[0] + jnp.sum(shift_u, axis=0, keepdims=True)
    ident, cosine, sine = maps[0], maps[1], maps[2]
    speed = cosine * packed[0] + sine * packed[1]
    forward = backward = speed
    size = ident.shape[0]
    row = lax.broadcasted_iota(jnp.int32, ident.shape, 0)
    for d in (1, 2, 4, 8):
        same = (ident == pltpu.roll(ident, d, axis=0)) & (row >= d)
        forward = forward + jnp.where(same, pltpu.roll(forward, d, axis=0), 0.0)
        same = (ident == pltpu.roll(ident, size - d, axis=0)) & (row < size - d)
        backward = backward + jnp.where(same, pltpu.roll(backward, size - d, axis=0), 0.0)
    total = forward + backward - speed
    thrust = maps[3] * total * jnp.abs(total)
    level = lanes(EXT) & (NZ - 1)
    matrix = group_matrix("column")
    for c, direction in enumerate((cosine, sine)):
        pushed = (thrust * direction)[8 : 8 + EXT]
        for part in range(0, XI, 4):
            spread = [jnp.where(level == xi, pushed, 0.0) for xi in range(part, part + 4)]
            result = exact_dot(jnp.concatenate(spread, axis=0), matrix)
            ns[c, part : part + 4] = result.reshape(4, EXT, LANES)

    def tendencies(xi, total):
        for tile in range(EXT // 8):
            base = 8 + tile * 8
            centre, gx, gy, gz, lap = [], [], [], [], []
            for c in range(4):
                mid = f[c, xi + 1, base : base + 8, :]
                xm = f[c, xi, base : base + 8, :]
                xp = f[c, xi + 2, base : base + 8, :]
                ym = f[c, xi + 1, base - 1 : base + 7, :]
                yp = f[c, xi + 1, base + 1 : base + 9, :]
                if c == 2:
                    zm = jnp.where(first, 0.0, pltpu.roll(mid, 1, axis=1))
                    zp = jnp.where(last, 0.0, pltpu.roll(mid, LANES - 1, axis=1))
                else:
                    zm, zp = below(mid, first), above(mid, last)
                centre.append(mid)
                gx.append(xp - xm)
                gy.append(yp - ym)
                gz.append(zp - zm)
                lap.append((xp + xm) + (yp + ym) + (zp + zm) - 6.0 * mid)
            s_xy = gy[0] + gx[1]
            s_xz = gz[0] + gx[2]
            s_yz = gz[1] + gy[2]
            strain = jnp.sqrt(
                2.0 * (gx[0] * gx[0] + gy[1] * gy[1] + gz[2] * gz[2])
                + (s_xy * s_xy + s_xz * s_xz + s_yz * s_yz)
            )
            nu = F32(TIME_STEP * VISCOSITY) + F32(0.5 * TIME_STEP * SMAGORINSKY) * strain
            half = F32(0.5 * TIME_STEP)
            au, av, aw = half * centre[0], half * centre[1], half * centre[2]
            for c in range(4):
                scale = nu * F32(DIFFUSIVITY_RATIO) if c == 3 else nu
                new = centre[c] + (scale * lap[c] - (au * gx[c] + av * gy[c] + aw * gz[c]))
                if c < 2:
                    new = new + ns[c, xi, tile * 8 : tile * 8 + 8, :]
                elif c == 2:
                    new = new + F32(TIME_STEP * BUOYANCY) * centre[3]
                if c < 3:
                    v[c, xi + 1, base : base + 8, :] = new
                elif 1 <= tile <= 4:
                    out[3, xi, tile * 8 - 8 : tile * 8, :] = new
                    if sums is not None:
                        total = total + new
                        if tile == 1:
                            sd[3 * XI + xi] = new
                        if tile == 4:
                            su[3 * XI + xi] = new
        return total

    total = rows("tend", tendencies, jnp.zeros((8, LANES), F32))
    if sums is not None:
        total = over_groups(jnp.sum(total, axis=0, keepdims=True))
        sums[...] = jnp.broadcast_to(total, (8, LANES))

    v[0, 0, body] = jnp.where(lane_ext < 32, entry(0), pltpu.roll(v[0, XI, body], 32, axis=1))
    v[0, XI + 1, body] = jnp.where(
        lane_ext >= 96, v[0, XI, body], pltpu.roll(v[0, 1, body], 96, axis=1)
    )

    def divergence(xi, carry):
        for tile in range(EXT // 8):
            base = 8 + tile * 8
            here = slice(base, base + 8)
            w = v[2, xi + 1, here, :]
            up = jnp.where(last, 0.0, pltpu.roll(w, LANES - 1, axis=1))
            down = jnp.where(first, 0.0, pltpu.roll(w, 1, axis=1))
            total = (v[0, xi + 2, here, :] - v[0, xi, here, :]) + (up - down)
            total = total + (
                v[1, xi + 1, base + 1 : base + 9, :] - v[1, xi + 1, base - 1 : base + 7, :]
            )
            source = total * F32(0.5 * SIXTH)
            r[xi, tile * 8 : tile * 8 + 8, :] = source
            pa[xi + 1, here, :] = -source
        return carry

    rows("div", divergence)

    def ends(p):
        p[0, body] = jnp.where(lane_ext < 32, 0.0, pltpu.roll(p[XI, body], 32, axis=1))
        p[XI + 1, body] = jnp.where(lane_ext >= 96, 0.0, pltpu.roll(p[1, body], 96, axis=1))

    for sweep in range(SWEEPS):
        p, q = (pa, pb) if sweep % 2 == 0 else (pb, pa)
        ends(p)

        def relax(xi, carry, p=p, q=q):
            for tile in range(EXT // 8):
                base = 8 + tile * 8
                here = slice(base, base + 8)
                mid = p[xi + 1, here, :]
                beside = (p[xi, here, :] + p[xi + 2, here, :]) + (
                    p[xi + 1, base - 1 : base + 7, :] + p[xi + 1, base + 1 : base + 9, :]
                )
                beside = beside + (below(mid, first) + above(mid, last))
                q[xi + 1, here, :] = beside * F32(SIXTH) - r[xi, tile * 8 : tile * 8 + 8, :]
            return carry

        rows("relax", relax)
    p = pa if SWEEPS % 2 == 0 else pb
    ends(p)

    def correct(xi, carry):
        for tile in range(1, 5):
            base = 8 + tile * 8
            here = slice(base, base + 8)
            mid = p[xi + 1, here, :]
            slopes = (
                p[xi + 2, here, :] - p[xi, here, :],
                p[xi + 1, base + 1 : base + 9, :] - p[xi + 1, base - 1 : base + 7, :],
                above(mid, last) - below(mid, first),
            )
            for c in range(3):
                new = v[c, xi + 1, here, :] - 0.5 * slopes[c]
                out[c, xi, tile * 8 - 8 : tile * 8, :] = new
                if sums is not None:
                    if tile == 1:
                        sd[c * XI + xi] = new
                    if tile == 4:
                        su[c * XI + xi] = new
        return carry

    rows("correct", correct)
    if sums is not None:
        band_sums(out, su, sd, bands)


def step_scratch():
    return [
        pltpu.VMEM((4, XI + 2, PAD, LANES), F32),
        pltpu.VMEM((3, XI + 2, PAD, LANES), F32),
        pltpu.VMEM((XI, EXT, LANES), F32),
        pltpu.VMEM((XI + 2, PAD, LANES), F32),
        pltpu.VMEM((XI + 2, PAD, LANES), F32),
        pltpu.VMEM((2, XI, EXT, LANES), F32),
        pltpu.VMEM((2, XI, LANES), F32),
        pltpu.VMEM((4, EXT, LANES), F32),
    ]


def send_kernel(scal, fields, s0, s1, s2, s3, turned):
    own = scal[0]

    def per_row(xi, carry):
        stacked = jnp.concatenate([fields[c, xi] for c in range(4)], axis=0)
        turned[xi] = stacked.T.reshape(GX, 4, 8, LANES)
        for s, out in enumerate((s0, s1, s2, s3)):
            out[pl.ds(xi * 4, 4)] = turned[xi, own ^ s]
        return carry

    rows("fill", per_row)


def final_kernel(scal, mean, s0, r1, r2, r3, out, columns, *, cells):
    own, slab = scal[0], scal[1]
    du, dw = mean_response(mean[0:1, :] * F32(1.0 / cells))
    pad = jnp.zeros((LANES - 2 * XI, LANES), F32)
    columns[...] = jnp.concatenate([du, dw, pad], axis=0).T
    own_columns = columns[pl.ds(pl.multiple_of(own * NZ, NZ), NZ), :]
    group = lanes() >> 5
    masks = [group == (slab ^ s) for s in range(4)]
    for x in range(XI):
        for kt in range(4):
            sources = [ref[x * 4 + kt] for ref in (s0, r1, r2, r3)]
            for c in range(4):
                value = None
                for s, source in enumerate(sources):
                    moved = pltpu.roll(source, (((slab ^ s) - c) & 3) * 32, axis=1)
                    value = moved if value is None else jnp.where(masks[s], moved, value)
                if c in (0, 2):
                    column = (0 if c == 0 else XI) + x
                    value = value + own_columns[kt * 8 : kt * 8 + 8, column : column + 1]
                out[c, x, kt * 8 : kt * 8 + 8, :] = value


def ring(groups):
    place = []
    for j in range(groups):
        for b in range(GX):
            i = b ^ (3 * (j & 1))
            place.append(i * groups + j)
    size = len(place)
    up = [(place[s], place[(s + 1) % size]) for s in range(size)]
    return up, [(b, a) for a, b in up]


def swapped(value, axis, size, distance):
    return lax.ppermute(value, axis, [(i, i ^ distance) for i in range(size)])


def local(state, planes, turbine_cell, active, yaw_sector, slot, *, layouts, groups):
    gx_index, gy_index = lax.axis_index("gx"), lax.axis_index("gy")
    slab = gx_index ^ (3 * (gy_index & 1))
    scal = jnp.stack([gx_index, slab, lax.axis_index("layout")]).astype(jnp.int32)
    scal = jnp.concatenate([scal, slot, active[0], yaw_sector[0]])
    cells = float(GX * XI * GX * OWN * groups)
    per_layout = planes.shape[0]
    height = (jnp.arange(NZ).astype(F32) + 0.5) / NZ
    zeros = jnp.zeros((NZ,), F32)
    profile = jnp.tile(jnp.stack([height ** (1.0 / 7.0), zeros, zeros, 0.5 * height]), (1, GX))
    profile = jnp.pad(profile, ((0, 4), (0, 0)))
    up, down = ring(groups)
    gy_up = [(j, (j + 1) % groups) for j in range(groups)]
    gy_down = [(b, a) for a, b in gy_up]

    ids = turbine_cell[0, :, NZ // 2, :].astype(F32)
    ids = jnp.stack([ids, lax.ppermute(ids, "gy", gy_up), lax.ppermute(ids, "gy", gy_down)])
    chunk = shape(TILES + 7, 8, LANES)
    s0, s1, s2, s3, plane = call(
        pack_kernel,
        (chunk, chunk, chunk, chunk, shape(per_layout * 4, 8, LANES)),
        [SMEM, VMEM, VMEM, VMEM],
        [pltpu.VMEM((GX, TILES, 8, LANES), F32)],
        name="pack",
    )(scal, state[0], planes, ids)
    received = [swapped(value, "gx", GX, s) for s, value in ((1, s1), (2, s2), (3, s3))]
    received[0], plane = lax.optimization_barrier((received[0], plane))
    plane_received = [swapped(plane, "layout", layouts, s) for s in range(1, layouts)]

    first_payload = shape(TILES + MORE + 4, 8, LANES)
    fields, inflow, su, sd, bands, sums, ids = call(
        functools.partial(unpack_kernel, layouts=layouts, per_layout=per_layout),
        (
            shape(4, XI, OWN, LANES),
            shape(4, OWN, LANES),
            first_payload,
            first_payload,
            shape(2, OWN, LANES),
            shape(8, LANES),
            shape(3, GX, XI, LANES),
        ),
        [SMEM, VMEM] + [VMEM] * (4 + layouts),
        [
            pltpu.VMEM((GX, TILES, 8, LANES), F32),
            pltpu.VMEM((layouts, per_layout * 4, 8, LANES), F32),
        ],
        name="unpack",
    )(scal, profile, s0, *received, plane, *plane_received)

    maps = call(maps_kernel, shape(4, 2 * OWN, LANES), [SMEM, VMEM], name="maps")(scal, ids)

    half = groups // 2

    def among_x(value):
        return sum([swapped(value, "gy", groups, d) for d in range(1, half)], value)

    mean = pending = None
    for step in range(STEPS):
        partial = sums
        if step > 0:
            partial = partial + swapped(partial, "gx", GX, 1)
            su, sd, partial, pending = lax.optimization_barrier((su, sd, partial, pending))
            mean = among_x(pending)
        lo = lax.ppermute(su, ("gx", "gy"), up)
        hi = lax.ppermute(sd, ("gx", "gy"), down)
        if step == 1:
            mean = mean + cells * profile[3:4]
        if step > 0:
            partial = partial + swapped(partial, "gy", groups, half)
            fields, partial = lax.optimization_barrier((fields, partial))
        arriving = swapped(partial, "gx", GX, 2) if step > 0 else swapped(partial, "gy", groups, half)
        outs = [shape(4, XI, OWN, LANES)]
        if step < STEPS - 1:
            payload = shape(TILES + MORE, 8, LANES)
            outs += [payload, payload, shape(2, OWN, LANES), shape(8, LANES)]
        if step == 0:
            outs += [shape(4, EXT, LANES)]
        operands = [fields, lo, hi, maps, bands, inflow] + ([mean] if step > 0 else [])
        results = call(
            functools.partial(step_kernel, step=step, cells=cells),
            tuple(outs),
            [VMEM] * len(operands),
            step_scratch(),
            flops=6_000_000_000,
            name="step%d" % step,
        )(*operands)
        results = list(results)
        fields = results.pop(0)
        if step < STEPS - 1:
            su, sd, bands, sums = results[:4]
            del results[:4]
        if step == 0:
            inflow = results.pop(0)
        su, sd, fields, arriving = lax.optimization_barrier((su, sd, fields, arriving))
        pending = partial + arriving
    mean = among_x(pending)

    chunk = shape(TILES, 8, LANES)
    s0, s1, s2, s3 = call(
        send_kernel,
        (chunk, chunk, chunk, chunk),
        [SMEM, VMEM],
        [pltpu.VMEM((XI, GX, 4, 8, LANES), F32)],
        name="send",
    )(scal, fields)
    received = [swapped(value, "gx", GX, s) for s, value in ((1, s1), (2, s2), (3, s3))]
    fields = call(
        functools.partial(final_kernel, cells=cells),
        shape(4, XI, NZ, LANES),
        [SMEM, VMEM] + [VMEM] * 4,
        [pltpu.VMEM((LANES, LANES), F32)],
        name="final",
    )(scal, mean, s0, *received)
    return fields[None]


def solution(mesh):
    body = functools.partial(local, layouts=mesh.shape["layout"], groups=mesh.shape["gy"])
    return jax.shard_map(
        body,
        mesh=mesh,
        in_specs=(
            P("layout", None, "gx", None, "gy"),
            P("layout", None, None, "gy"),
            P("layout", "gx", None, "gy"),
            P("layout", None),
            P("layout", None),
            P(),
        ),
        out_specs=P("layout", None, "gx", None, "gy"),
        check_vma=False,
    )
```

```python
import functools
import math

import jax
import jax.numpy as jnp
from jax import lax
from jax.experimental import pallas as pl
from jax.experimental.pallas import tpu as pltpu
from jax.sharding import PartitionSpec as P

STEPS = 4
SWEEPS = 4
RADIUS = 5
NZ = 32
XI = 16
GX = 4
OWN = 32
HALO = 8
EXT = OWN + 2 * HALO
PAD = EXT + 16
LANES = 128
WIDTH = 2 * RADIUS + 1
LOWEST = NZ // 2 - RADIUS
TILES = 4 * XI
MORE = 4
UNROLL = {"fill": 4, "tend": 8, "div": 16, "relax": 16, "correct": 16}

TIME_STEP = 0.25
VISCOSITY = 0.02
SMAGORINSKY = 0.0289
DIFFUSIVITY_RATIO = 1.0 / 0.7
BUOYANCY = 0.5
THRUST_COEFF = 1.33
YAW_INCREMENT = 0.1
SIXTH = 1.0 / 6.0
F32 = jnp.float32
INTS = 7
VLIMIT = 40 * 1024 * 1024

VMEM = pl.BlockSpec(memory_space=pltpu.VMEM)
SMEM = pl.BlockSpec(memory_space=pltpu.SMEM)


def shape(*dims):
    return jax.ShapeDtypeStruct(dims, F32)


def lanes(rows=8):
    return lax.broadcasted_iota(jnp.int32, (rows, LANES), 1)


def level_masks(rows=8):
    level = lanes(rows) & (NZ - 1)
    return level == 0, level == NZ - 1


def below(f, first):
    return jnp.where(first, f, pltpu.roll(f, 1, axis=1))


def above(f, last):
    return jnp.where(last, f, pltpu.roll(f, LANES - 1, axis=1))


def call(kernel, out_shape, in_specs, scratch=(), flops=2_000_000_000, **kwargs):
    return pl.pallas_call(
        kernel,
        out_shape=out_shape,
        in_specs=in_specs,
        out_specs=jax.tree.map(lambda _: VMEM, out_shape),
        scratch_shapes=list(scratch),
        compiler_params=pltpu.CompilerParams(vmem_limit_bytes=VLIMIT),
        cost_estimate=pl.CostEstimate(flops=flops, bytes_accessed=4_000_000, transcendentals=0),
        **kwargs,
    )


def rows(name, body, carry=0):
    count = UNROLL[name]

    def some(index, carry):
        for offset in range(count):
            carry = body(index * count + offset, carry)
        return carry

    return lax.fori_loop(0, XI // count, some, carry)


def group_matrix(banded):
    row = lax.broadcasted_iota(jnp.int32, (LANES, LANES), 0)
    column = lax.broadcasted_iota(jnp.int32, (LANES, LANES), 1)
    level = (row if banded == "row" else column) & (NZ - 1)
    inside = (level >= LOWEST) & (level < LOWEST + WIDTH)
    return jnp.where(((row >> 5) == (column >> 5)) & inside, 1.0, 0.0).astype(F32)


def exact_dot(a, b):
    return jnp.dot(a, b, precision=lax.Precision.HIGHEST, preferred_element_type=F32)


def band_sums(fields, su, sd, sums):
    matrix = group_matrix("row")
    level = lanes(OWN) & (NZ - 1)
    for c in range(2):
        total = exact_dot(fields[c].reshape(XI * OWN, LANES), matrix)
        packed = jnp.zeros((OWN, LANES), F32)
        for xi in range(XI):
            packed = jnp.where(level == xi, total[xi * OWN : (xi + 1) * OWN], packed)
        sums[c] = packed
        for t in range(2):
            sd[TILES + 2 * c + t] = packed[t * 8 : t * 8 + 8]
            su[TILES + 2 * c + t] = packed[16 + t * 8 : 24 + t * 8]


def block_transposed(sources, group, masks):
    out = None
    for c, value in enumerate(sources):
        moved = pltpu.roll(value, ((c - group) & 3) * 32, axis=1)
        out = moved if out is None else jnp.where(masks[c], moved, out)
    return out


def transposed4(a, odd, high):
    b0 = jnp.where(odd, pltpu.roll(a[1], 32, axis=1), a[0])
    b1 = jnp.where(odd, a[1], pltpu.roll(a[0], 96, axis=1))
    b2 = jnp.where(odd, pltpu.roll(a[3], 32, axis=1), a[2])
    b3 = jnp.where(odd, a[3], pltpu.roll(a[2], 96, axis=1))
    return (
        jnp.where(high, pltpu.roll(b2, 64, axis=1), b0),
        jnp.where(high, pltpu.roll(b3, 64, axis=1), b1),
        jnp.where(high, b2, pltpu.roll(b0, 64, axis=1)),
        jnp.where(high, b3, pltpu.roll(b1, 64, axis=1)),
    )


def pack_kernel(scal, state, planes, ids, s0, s1, s2, s3, pl_out, stage):
    slab = scal[1]
    group = lanes() >> 5
    masks = [group == c for c in range(4)]
    odd, high = (group & 1) == 1, group >= 2

    def per_row(x, carry):
        for kt in range(4):
            sources = [state[c, x, kt * 8 : kt * 8 + 8, :] for c in range(4)]
            for b, value in enumerate(transposed4(sources, odd, high)):
                stage[b, x * 4 + kt] = value
        return carry

    rows("fill", per_row)
    for s, out in enumerate((s0, s1, s2, s3)):
        out[:TILES] = stage[slab ^ s]
    for half in range(6):
        for out in (s0, s1, s2, s3):
            out[TILES + half] = ids[half // 2, (half % 2) * 8 : (half % 2) * 8 + 8]
    for plane in range(planes.shape[0]):
        for kt in range(4):
            sources = [planes[plane, c, kt * 8 : kt * 8 + 8, :] for c in range(4)]
            pl_out[plane * 4 + kt] = block_transposed(sources, slab, masks)


def maps_kernel(ints, ids, maps):
    slab = ints[1]
    lane = lanes(NZ)
    pieces = []
    for g in range(GX):
        moved_mid = pltpu.roll(ids[0, g], (16 - 32 * slab) & (LANES - 1), axis=1)
        moved_left = pltpu.roll(ids[1, g], 16, axis=1)
        moved_right = pltpu.roll(ids[2, g], OWN + 16, axis=1)
        here = jnp.where((lane[:XI] < 16) & (slab == 0), moved_left, moved_mid)
        here = jnp.where((lane[:XI] >= OWN + 16) & (slab == 3), moved_right, here)
        pieces += [here, jnp.full((XI, LANES), -1.0, F32)]
    here = jnp.concatenate(pieces, axis=0)
    turbines = (ints.shape[0] - INTS) // 2

    def per_turbine(t, carry):
        sector, running = carry
        match = here == t.astype(F32)
        return (
            jnp.where(match, ints[INTS + turbines + t].astype(F32), sector),
            jnp.where(match, ints[INTS + t].astype(F32), running),
        )

    sector, running = lax.fori_loop(
        0, turbines, per_turbine, (jnp.full((LANES, LANES), -1.0, F32), jnp.zeros((LANES, LANES), F32))
    )
    cosine = jnp.zeros((LANES, LANES), F32)
    sine = jnp.zeros((LANES, LANES), F32)
    for value in range(8):
        angle = (value - 3.5) * YAW_INCREMENT
        cosine = jnp.where(sector == value, F32(math.cos(angle)), cosine)
        sine = jnp.where(sector == value, F32(math.sin(angle)), sine)
    thrust = running * F32(-0.5 * THRUST_COEFF * TIME_STEP / float(WIDTH**2) ** 2)
    low = lanes(LANES) < 64
    first = jnp.where(low, here, pltpu.roll(thrust, 64, axis=1)).T
    second = jnp.where(low, cosine, pltpu.roll(sine, 64, axis=1)).T
    maps[0], maps[3] = first[:64], first[64:]
    maps[1], maps[2] = second[:64], second[64:]


def over_groups(row):
    row = row + pltpu.roll(row, 64, axis=1)
    return row + pltpu.roll(row, 32, axis=1)


def unpack_kernel(
    scal, profile, s0, r1, r2, r3, p0, *rest, layouts, per_layout
):
    plane_refs = (p0,) + rest[: layouts - 1]
    fields, inflow, su, sd, bands, sums, ids, held, planes = rest[layouts - 1 :]
    own, here = scal[0], scal[2]
    for s, source in enumerate((s0, r1, r2, r3)):
        held[own ^ s] = source[:TILES]
        for half in range(6):
            ids[half // 2, own ^ s, (half % 2) * 8 : (half % 2) * 8 + 8, :] = source[TILES + half]
    for s, source in enumerate(plane_refs):
        planes[here ^ s] = source[...]

    def per_row(xi, total):
        parts = [held[g, pl.ds(xi * 4, 4)].reshape(NZ, LANES) for g in range(GX)]
        turned = jnp.concatenate(parts, axis=0).T
        for c in range(4):
            value = turned[c * 32 : c * 32 + 32] + profile[c : c + 1, :]
            fields[c, xi] = value
            sd[c * XI + xi] = value[:HALO]
            su[c * XI + xi] = value[OWN - HALO :]
            if c == 3:
                total = total + jnp.sum(value, axis=0, keepdims=True)
        return total

    total = rows("fill", per_row, jnp.zeros((1, LANES), F32))
    sums[...] = jnp.broadcast_to(over_groups(total), (8, LANES))
    parts = []
    for step in range(STEPS):
        plane = scal[3 + step]
        parts.append(
            planes[plane // per_layout, pl.ds((plane % per_layout) * 4, 4)].reshape(NZ, LANES)
        )
    turned = jnp.concatenate(parts, axis=0).T
    for c in range(4):
        value = turned[c * 32 : c * 32 + 32] + profile[c : c + 1, :]
        inflow[c] = value
        sd[TILES + MORE + c] = value[:HALO]
        su[TILES + MORE + c] = value[OWN - HALO :]
    band_sums(fields, su, sd, bands)


def mean_response(mean):
    lane = lanes(XI)
    row = lax.broadcasted_iota(jnp.int32, (XI, LANES), 0)
    level = lane & (NZ - 1)
    first, last = level == 0, level == NZ - 1

    def x_pair(p):
        lower = pltpu.roll(p, 1, axis=0)
        edge = jnp.where(lane < 32, 0.0, pltpu.roll(lower, 32, axis=1))
        lower = jnp.where(row == 0, edge, lower)
        upper = pltpu.roll(p, XI - 1, axis=0)
        edge = jnp.where(lane >= 96, 0.0, pltpu.roll(upper, 96, axis=1))
        upper = jnp.where(row == XI - 1, edge, upper)
        return lower, upper

    vertical = jnp.broadcast_to(mean, (XI, LANES)) * F32(-TIME_STEP * BUOYANCY)
    up = jnp.where(last, 0.0, pltpu.roll(vertical, LANES - 1, axis=1))
    down = jnp.where(first, 0.0, pltpu.roll(vertical, 1, axis=1))
    source = (up - down) * 0.5
    p = source * F32(-SIXTH)
    for sweep in range(SWEEPS):
        lower, upper = x_pair(p)
        p = (lower + upper + 2.0 * p + above(p, last) + below(p, first) - source) * F32(SIXTH)
    lower, upper = x_pair(p)
    return (upper - lower) * -0.5, vertical - (above(p, last) - below(p, first)) * 0.5


def step_kernel(*refs, step, cells):
    refs = list(refs)
    fields_in, lo, hi, maps, bands_in, inflow_in = refs[:6]
    del refs[:6]
    mean = None
    if step > 0:
        mean = refs.pop(0)
    out = refs.pop(0)
    su = sd = bands = sums = inflow_out = None
    if step < STEPS - 1:
        su, sd, bands, sums = refs[:4]
        del refs[:4]
    if step == 0:
        inflow_out = refs.pop(0)
    f, v, r, pa, pb, ns, change, inflow = refs
    first, last = level_masks()
    lane_ext = lanes(EXT)
    body = slice(8, 8 + EXT)

    if step > 0:
        du, dw = mean_response(mean[0:1, :] * F32(1.0 / cells))
        change[0] = du
        change[1] = dw
        inflow[...] = inflow_in[...]
    else:
        for c in range(4):
            inflow[c, 0:8] = lo[TILES + MORE + c]
            inflow[c, 8 : 8 + OWN] = inflow_in[c]
            inflow[c, 8 + OWN : EXT] = hi[TILES + MORE + c]
        inflow_out[...] = inflow[...]

    def fill(xi, carry):
        for c in range(4):
            low, mid, high = lo[c * XI + xi], fields_in[c, xi], hi[c * XI + xi]
            if step > 0 and c in (0, 2):
                d = change[c // 2, pl.ds(xi, 1), :]
                low, mid, high = low + d, mid + d, high + d
            f[c, xi + 1, 8:16] = low
            f[c, xi + 1, 16 : 16 + OWN] = mid
            f[c, xi + 1, 16 + OWN : 8 + EXT] = high
        return carry

    rows("fill", fill)
    shift = (LANES - 32 * step) % LANES

    def entry(c):
        value = inflow[c]
        return pltpu.roll(value, shift, axis=1) if shift else value

    for c in range(4):
        f[c, 0, body] = jnp.where(
            lane_ext < 32, entry(c), pltpu.roll(f[c, XI, body], 32, axis=1)
        )
        f[c, XI + 1, body] = jnp.where(
            lane_ext >= 96, f[c, XI, body], pltpu.roll(f[c, 1, body], 96, axis=1)
        )

    packed = []
    for c in range(2):
        parts = [lo[TILES + 2 * c + t] for t in range(2)] + [bands_in[c]]
        parts += [hi[TILES + 2 * c + t] for t in range(2)]
        packed.append(jnp.concatenate(parts, axis=0))
    if step > 0:
        level = lanes(XI) & (NZ - 1)
        row = lax.broadcasted_iota(jnp.int32, (XI, LANES), 0)
        shift_u = jnp.where(level == row, exact_dot(change[0], group_matrix("row")), 0.0)
        packed[0] = packed[0] + jnp.sum(shift_u, axis=0, keepdims=True)
    ident, cosine, sine = maps[0], maps[1], maps[2]
    speed = cosine * packed[0] + sine * packed[1]
    forward = backward = speed
    size = ident.shape[0]
    row = lax.broadcasted_iota(jnp.int32, ident.shape, 0)
    for d in (1, 2, 4, 8):
        same = (ident == pltpu.roll(ident, d, axis=0)) & (row >= d)
        forward = forward + jnp.where(same, pltpu.roll(forward, d, axis=0), 0.0)
        same = (ident == pltpu.roll(ident, size - d, axis=0)) & (row < size - d)
        backward = backward + jnp.where(same, pltpu.roll(backward, size - d, axis=0), 0.0)
    total = forward + backward - speed
    thrust = maps[3] * total * jnp.abs(total)
    level = lanes(EXT) & (NZ - 1)
    matrix = group_matrix("column")
    for c, direction in enumerate((cosine, sine)):
        pushed = (thrust * direction)[8 : 8 + EXT]
        for part in range(0, XI, 4):
            spread = [jnp.where(level == xi, pushed, 0.0) for xi in range(part, part + 4)]
            result = exact_dot(jnp.concatenate(spread, axis=0), matrix)
            ns[c, part : part + 4] = result.reshape(4, EXT, LANES)

    def tendencies(xi, total):
        for tile in range(EXT // 8):
            base = 8 + tile * 8
            centre, gx, gy, gz, lap = [], [], [], [], []
            for c in range(4):
                mid = f[c, xi + 1, base : base + 8, :]
                xm = f[c, xi, base : base + 8, :]
                xp = f[c, xi + 2, base : base + 8, :]
                ym = f[c, xi + 1, base - 1 : base + 7, :]
                yp = f[c, xi + 1, base + 1 : base + 9, :]
                if c == 2:
                    zm = jnp.where(first, 0.0, pltpu.roll(mid, 1, axis=1))
                    zp = jnp.where(last, 0.0, pltpu.roll(mid, LANES - 1, axis=1))
                else:
                    zm, zp = below(mid, first), above(mid, last)
                centre.append(mid)
                gx.append(xp - xm)
                gy.append(yp - ym)
                gz.append(zp - zm)
                lap.append((xp + xm) + (yp + ym) + (zp + zm) - 6.0 * mid)
            s_xy = gy[0] + gx[1]
            s_xz = gz[0] + gx[2]
            s_yz = gz[1] + gy[2]
            strain = jnp.sqrt(
                2.0 * (gx[0] * gx[0] + gy[1] * gy[1] + gz[2] * gz[2])
                + (s_xy * s_xy + s_xz * s_xz + s_yz * s_yz)
            )
            nu = F32(TIME_STEP * VISCOSITY) + F32(0.5 * TIME_STEP * SMAGORINSKY) * strain
            half = F32(0.5 * TIME_STEP)
            au, av, aw = half * centre[0], half * centre[1], half * centre[2]
            for c in range(4):
                scale = nu * F32(DIFFUSIVITY_RATIO) if c == 3 else nu
                new = centre[c] + (scale * lap[c] - (au * gx[c] + av * gy[c] + aw * gz[c]))
                if c < 2:
                    new = new + ns[c, xi, tile * 8 : tile * 8 + 8, :]
                elif c == 2:
                    new = new + F32(TIME_STEP * BUOYANCY) * centre[3]
                if c < 3:
                    v[c, xi + 1, base : base + 8, :] = new
                elif 1 <= tile <= 4:
                    out[3, xi, tile * 8 - 8 : tile * 8, :] = new
                    if sums is not None:
                        total = total + new
                        if tile == 1:
                            sd[3 * XI + xi] = new
                        if tile == 4:
                            su[3 * XI + xi] = new
        return total

    total = rows("tend", tendencies, jnp.zeros((8, LANES), F32))
    if sums is not None:
        total = over_groups(jnp.sum(total, axis=0, keepdims=True))
        sums[...] = jnp.broadcast_to(total, (8, LANES))

    v[0, 0, body] = jnp.where(lane_ext < 32, entry(0), pltpu.roll(v[0, XI, body], 32, axis=1))
    v[0, XI + 1, body] = jnp.where(
        lane_ext >= 96, v[0, XI, body], pltpu.roll(v[0, 1, body], 96, axis=1)
    )

    def divergence(xi, carry):
        for tile in range(EXT // 8):
            base = 8 + tile * 8
            here = slice(base, base + 8)
            w = v[2, xi + 1, here, :]
            up = jnp.where(last, 0.0, pltpu.roll(w, LANES - 1, axis=1))
            down = jnp.where(first, 0.0, pltpu.roll(w, 1, axis=1))
            total = (v[0, xi + 2, here, :] - v[0, xi, here, :]) + (up - down)
            total = total + (
                v[1, xi + 1, base + 1 : base + 9, :] - v[1, xi + 1, base - 1 : base + 7, :]
            )
            source = total * F32(0.5 * SIXTH)
            r[xi, tile * 8 : tile * 8 + 8, :] = source
            pa[xi + 1, here, :] = -source
        return carry

    rows("div", divergence)

    def ends(p):
        p[0, body] = jnp.where(lane_ext < 32, 0.0, pltpu.roll(p[XI, body], 32, axis=1))
        p[XI + 1, body] = jnp.where(lane_ext >= 96, 0.0, pltpu.roll(p[1, body], 96, axis=1))

    for sweep in range(SWEEPS):
        p, q = (pa, pb) if sweep % 2 == 0 else (pb, pa)
        ends(p)

        def relax(xi, carry, p=p, q=q):
            for tile in range(EXT // 8):
                base = 8 + tile * 8
                here = slice(base, base + 8)
                mid = p[xi + 1, here, :]
                beside = (p[xi, here, :] + p[xi + 2, here, :]) + (
                    p[xi + 1, base - 1 : base + 7, :] + p[xi + 1, base + 1 : base + 9, :]
                )
                beside = beside + (below(mid, first) + above(mid, last))
                q[xi + 1, here, :] = beside * F32(SIXTH) - r[xi, tile * 8 : tile * 8 + 8, :]
            return carry

        rows("relax", relax)
    p = pa if SWEEPS % 2 == 0 else pb
    ends(p)

    def correct(xi, carry):
        for tile in range(1, 5):
            base = 8 + tile * 8
            here = slice(base, base + 8)
            mid = p[xi + 1, here, :]
            slopes = (
                p[xi + 2, here, :] - p[xi, here, :],
                p[xi + 1, base + 1 : base + 9, :] - p[xi + 1, base - 1 : base + 7, :],
                above(mid, last) - below(mid, first),
            )
            for c in range(3):
                new = v[c, xi + 1, here, :] - 0.5 * slopes[c]
                out[c, xi, tile * 8 - 8 : tile * 8, :] = new
                if sums is not None:
                    if tile == 1:
                        sd[c * XI + xi] = new
                    if tile == 4:
                        su[c * XI + xi] = new
        return carry

    rows("correct", correct)
    if sums is not None:
        band_sums(out, su, sd, bands)


def step_scratch():
    return [
        pltpu.VMEM((4, XI + 2, PAD, LANES), F32),
        pltpu.VMEM((3, XI + 2, PAD, LANES), F32),
        pltpu.VMEM((XI, EXT, LANES), F32),
        pltpu.VMEM((XI + 2, PAD, LANES), F32),
        pltpu.VMEM((XI + 2, PAD, LANES), F32),
        pltpu.VMEM((2, XI, EXT, LANES), F32),
        pltpu.VMEM((2, XI, LANES), F32),
        pltpu.VMEM((4, EXT, LANES), F32),
    ]


def send_kernel(scal, fields, s0, s1, s2, s3, turned):
    own = scal[0]

    def per_row(xi, carry):
        stacked = jnp.concatenate([fields[c, xi] for c in range(4)], axis=0)
        turned[xi] = stacked.T.reshape(GX, 4, 8, LANES)
        for s, out in enumerate((s0, s1, s2, s3)):
            out[pl.ds(xi * 4, 4)] = turned[xi, own ^ s]
        return carry

    rows("fill", per_row)


def final_kernel(scal, mean, s0, r1, r2, r3, out, columns, *, cells):
    own, slab = scal[0], scal[1]
    du, dw = mean_response(mean[0:1, :] * F32(1.0 / cells))
    pad = jnp.zeros((LANES - 2 * XI, LANES), F32)
    columns[...] = jnp.concatenate([du, dw, pad], axis=0).T
    own_columns = columns[pl.ds(pl.multiple_of(own * NZ, NZ), NZ), :]
    group = lanes() >> 5
    masks = [group == (slab ^ s) for s in range(4)]
    for x in range(XI):
        for kt in range(4):
            sources = [ref[x * 4 + kt] for ref in (s0, r1, r2, r3)]
            for c in range(4):
                value = None
                for s, source in enumerate(sources):
                    moved = pltpu.roll(source, (((slab ^ s) - c) & 3) * 32, axis=1)
                    value = moved if value is None else jnp.where(masks[s], moved, value)
                if c in (0, 2):
                    column = (0 if c == 0 else XI) + x
                    value = value + own_columns[kt * 8 : kt * 8 + 8, column : column + 1]
                out[c, x, kt * 8 : kt * 8 + 8, :] = value


def ring(groups):
    place = []
    for j in range(groups):
        for b in range(GX):
            i = b ^ (3 * (j & 1))
            place.append(i * groups + j)
    size = len(place)
    up = [(place[s], place[(s + 1) % size]) for s in range(size)]
    return up, [(b, a) for a, b in up]


def swapped(value, axis, size, distance):
    return lax.ppermute(value, axis, [(i, i ^ distance) for i in range(size)])


def local(state, planes, turbine_cell, active, yaw_sector, slot, *, layouts, groups):
    gx_index, gy_index = lax.axis_index("gx"), lax.axis_index("gy")
    slab = gx_index ^ (3 * (gy_index & 1))
    scal = jnp.stack([gx_index, slab, lax.axis_index("layout")]).astype(jnp.int32)
    scal = jnp.concatenate([scal, slot, active[0], yaw_sector[0]])
    cells = float(GX * XI * GX * OWN * groups)
    per_layout = planes.shape[0]
    height = (jnp.arange(NZ).astype(F32) + 0.5) / NZ
    zeros = jnp.zeros((NZ,), F32)
    profile = jnp.tile(jnp.stack([height ** (1.0 / 7.0), zeros, zeros, 0.5 * height]), (1, GX))
    profile = jnp.pad(profile, ((0, 4), (0, 0)))
    up, down = ring(groups)
    gy_up = [(j, (j + 1) % groups) for j in range(groups)]
    gy_down = [(b, a) for a, b in gy_up]

    ids = turbine_cell[0, :, NZ // 2, :].astype(F32)
    ids = jnp.stack([ids, lax.ppermute(ids, "gy", gy_up), lax.ppermute(ids, "gy", gy_down)])
    chunk = shape(TILES + 6, 8, LANES)
    s0, s1, s2, s3, plane = call(
        pack_kernel,
        (chunk, chunk, chunk, chunk, shape(per_layout * 4, 8, LANES)),
        [SMEM, VMEM, VMEM, VMEM],
        [pltpu.VMEM((GX, TILES, 8, LANES), F32)],
        name="pack",
    )(scal, state[0], planes, ids)
    received = [swapped(value, "gx", GX, s) for s, value in ((1, s1), (2, s2), (3, s3))]
    received[0], plane = lax.optimization_barrier((received[0], plane))
    plane_received = [swapped(plane, "layout", layouts, s) for s in range(1, layouts)]

    first_payload = shape(TILES + MORE + 4, 8, LANES)
    fields, inflow, su, sd, bands, sums, ids = call(
        functools.partial(unpack_kernel, layouts=layouts, per_layout=per_layout),
        (
            shape(4, XI, OWN, LANES),
            shape(4, OWN, LANES),
            first_payload,
            first_payload,
            shape(2, OWN, LANES),
            shape(8, LANES),
            shape(3, GX, XI, LANES),
        ),
        [SMEM, VMEM] + [VMEM] * (4 + layouts),
        [
            pltpu.VMEM((GX, TILES, 8, LANES), F32),
            pltpu.VMEM((layouts, per_layout * 4, 8, LANES), F32),
        ],
        name="unpack",
    )(scal, profile, s0, *received, plane, *plane_received)

    maps = call(maps_kernel, shape(4, 2 * OWN, LANES), [SMEM, VMEM], name="maps")(scal, ids)

    half = groups // 2

    def last_round(value):
        return sum([swapped(value, "gy", groups, d) for d in range(1, half)], value)

    mean = pending = None
    for step in range(STEPS):
        partial = sums + swapped(sums, "gx", GX, 1)
        su, sd, partial = lax.optimization_barrier((su, sd, partial))
        lo = lax.ppermute(su, ("gx", "gy"), up)
        hi = lax.ppermute(sd, ("gx", "gy"), down)
        if pending is not None:
            mean = last_round(pending)
        partial = partial + swapped(partial, "gy", groups, half)
        fields, partial = lax.optimization_barrier((fields, partial))
        arriving = swapped(partial, "gx", GX, 2)
        outs = [shape(4, XI, OWN, LANES)]
        if step < STEPS - 1:
            payload = shape(TILES + MORE, 8, LANES)
            outs += [payload, payload, shape(2, OWN, LANES), shape(8, LANES)]
        if step == 0:
            outs += [shape(4, EXT, LANES)]
        operands = [fields, lo, hi, maps, bands, inflow] + ([mean] if step > 0 else [])
        results = call(
            functools.partial(step_kernel, step=step, cells=cells),
            tuple(outs),
            [VMEM] * len(operands),
            step_scratch(),
            flops=6_000_000_000,
            name="step%d" % step,
        )(*operands)
        results = list(results)
        fields = results.pop(0)
        if step < STEPS - 1:
            su, sd, bands, sums = results[:4]
            del results[:4]
        if step == 0:
            inflow = results.pop(0)
        su, sd, fields, arriving = lax.optimization_barrier((su, sd, fields, arriving))
        pending = partial + arriving
    mean = last_round(pending)

    chunk = shape(TILES, 8, LANES)
    s0, s1, s2, s3 = call(
        send_kernel,
        (chunk, chunk, chunk, chunk),
        [SMEM, VMEM],
        [pltpu.VMEM((XI, GX, 4, 8, LANES), F32)],
        name="send",
    )(scal, fields)
    received = [swapped(value, "gx", GX, s) for s, value in ((1, s1), (2, s2), (3, s3))]
    fields = call(
        functools.partial(final_kernel, cells=cells),
        shape(4, XI, NZ, LANES),
        [SMEM, VMEM] + [VMEM] * 4,
        [pltpu.VMEM((LANES, LANES), F32)],
        name="final",
    )(scal, mean, s0, *received)
    return fields[None]


def solution(mesh):
    body = functools.partial(local, layouts=mesh.shape["layout"], groups=mesh.shape["gy"])
    return jax.shard_map(
        body,
        mesh=mesh,
        in_specs=(
            P("layout", None, "gx", None, "gy"),
            P("layout", None, None, "gy"),
            P("layout", "gx", None, "gy"),
            P("layout", None),
            P("layout", None),
            P(),
        ),
        out_specs=P("layout", None, "gx", None, "gy"),
        check_vma=False,
    )
```
